128 devices in a mesh: row: 8 (over y_lo, x), head: 16 (over y_hi, z, core).
Axes of the slice: x: 4, y: 4 (y_hi: 2, y_lo: 2; y = y_hi * 2 + y_lo), z: 4, core: 2. Of those that a mesh axis runs over, the one named last changes fastest.
Arguments:
- link_tensor_source: bfloat16 [128, 256, 256], P('head', 'row'), may hold values from -6 to 6
- neighbour_allowance: int32 [256, 256], P('row'), may hold values 0 or 1
- asking_projector: bfloat16 [128, 128], P(None, 'head'), may hold values from -0.5 to 0.5
- lookup_projector: bfloat16 [128, 128], P(None, 'head'), may hold values from -0.5 to 0.5
- first_content_projector: bfloat16 [128, 128], P(None, 'head'), may hold values from -0.5 to 0.5
- second_content_projector: bfloat16 [128, 128], P(None, 'head'), may hold values from -0.5 to 0.5
- final_projector: bfloat16 [128, 128], P('head'), may hold values from -0.5 to 0.5
- per_slot_scaling: float32 [16], P('head'), may hold values from 0.15 to 2, as said below
- upstream_sensitivity: bfloat16 [128, 256, 256], P('head', 'row'), may hold values from -48 to 48
Outputs:
- grad_pairs: bfloat16 [128, 256, 256], P('head', 'row')
- grad_query: float32 [128, 128], P(None, 'head')
- grad_key: float32 [128, 128], P(None, 'head')
- grad_left: float32 [128, 128], P(None, 'head')
- grad_right: float32 [128, 128], P(None, 'head')
- grad_out: float32 [128, 128], P('head')
The draws below stay inside these ranges and needn't reach their ends.
Inputs may be any that keep to these rules, and one draw needn't show every extreme that they name: `per_slot_scaling`: 16 positive factors, one a head.
All inputs are finite; a program needn't handle non-finite values. No bound on the sum of `neighbour_allowance` on one device may be relied on, other than what follows from the above.
Results may differ from the reference program's by a relative error of at most 0.0025.
The reference program's roundings to bfloat16 on the way count: a program that leaves them out, or rounds other values in their place, can miss the bound.
Values may be sent and summed in bfloat16 or wider, within the bound.
A program may use at most 64 MiB of HBM per device.

```python
import math
import jax
import jax.numpy as jnp
from jax import lax

D = 128
H = 16
N = 256


def draw_per_slot_scaling(key, part):
    key = jax.random.fold_in(key, 11)
    logs = jax.random.uniform(key, (H,), jnp.float32, math.log(0.15), math.log(0.6))
    return jnp.exp(logs)


def with_ends(array, own_key, smallest, largest):
    extent = array.shape
    spot = [jax.random.randint(jax.random.fold_in(own_key, axis), (), 0, extent[axis]) for axis in range(len(extent))]
    array = array.at[tuple(spot)].set(smallest)
    longest = extent.index(max(extent))
    spot[longest] = (spot[longest] + 1) % extent[longest]
    return array.at[tuple(spot)].set(largest)


def level_of(rng, shape, split, smallest, high):
    factor_of = 1.0
    for position, shards_of in split:
        draws = jax.random.uniform(jax.random.fold_in(jax.random.fold_in(rng, 6), position), (shards_of,), jnp.float32, smallest / len(split), high / len(split))
        factor_of = factor_of * jnp.repeat(jnp.exp(draws), shape[position] // shards_of).reshape((-1,) + (1,) * (len(shape) - 1 - position))
    return factor_of


def scatter_about(own_key, extent, width, limit, pieces=(), kind=jnp.bfloat16):
    drawn = jax.random.normal(own_key, extent, jnp.float32) * width
    if len(pieces) > 0:
        drawn = level_of(own_key, extent, pieces, -0.22, 0.18) * drawn
    return jnp.clip(drawn, min=-limit, max=limit).astype(kind)


def setup_inputs(seed: int = 0) -> dict:
    key_of = jax.random.split(jax.random.key(seed), 10)
    link_tensor_source = scatter_about(key_of[0], (D, N, N), 1.0, 6.0, ((0, 16), (1, 8)))
    neighbour_allowance = with_ends((jax.random.randint(key_of[1], (N, N), 0, 2) < 1).astype(jnp.int32), jax.random.fold_in(key_of[1], 1), 0, 1)
    asking_projector = scatter_about(key_of[2], (D, D), D ** -0.5, 0.5, ((1, 16),))
    lookup_projector = scatter_about(key_of[3], (D, D), D ** -0.5, 0.5, ((1, 16),))
    first_content_projector = scatter_about(key_of[4], (D, D), D ** -0.5, 0.5, ((1, 16),))
    second_content_projector = scatter_about(key_of[5], (D, D), D ** -0.5, 0.5, ((1, 16),))
    final_projector = scatter_about(key_of[6], (D, D), D ** -0.5, 0.5, ((0, 16),))
    per_slot_scaling = draw_per_slot_scaling(jax.random.fold_in(key_of[9], 71), 0)
    upstream_sensitivity = scatter_about(key_of[8], (D, N, N), 8.0, 48.0, ((0, 16), (1, 8)))
    return {"link_tensor_source": link_tensor_source, "neighbour_allowance": neighbour_allowance, "asking_projector": asking_projector, "lookup_projector": lookup_projector, "first_content_projector": first_content_projector, "second_content_projector": second_content_projector, "final_projector": final_projector, "per_slot_scaling": per_slot_scaling, "upstream_sensitivity": upstream_sensitivity}


HIGH = lax.Precision.HIGHEST
NEG = -1e30


def head_backward(query, key_part, left, right_part, stacked_derivative, factor, valid):
    qf = query.astype(jnp.float32)
    kf = key_part.astype(jnp.float32)
    lf = left.astype(jnp.float32)
    rf = right_part.astype(jnp.float32)
    gf = stacked_derivative.astype(jnp.float32)
    raw = jnp.einsum('cil,clj->ilj', qf, kf, precision=HIGH)
    logits = jnp.where(valid[:, :, None], factor * raw, NEG)
    top = logits.max(axis=1, keepdims=True)
    weights = jnp.exp(logits - top)
    prob = jnp.where(valid[:, :, None], weights / weights.sum(axis=1, keepdims=True), 0.0)
    mixed = lax.map(lambda pair: jnp.einsum('ilj,il,lj->ij', prob, pair[0], pair[1], precision=HIGH), (lf, rf))

    def add_channel(total, trio):
        return total + trio[0][:, None, :] * trio[1][:, :, None] * trio[2][None, :, :], None

    grad_prob, _ = lax.scan(add_channel, jnp.zeros_like(prob), (gf, lf, rf))
    delta = (gf * mixed).sum(axis=0)
    grad_score = prob * (grad_prob - delta[:, None, :])
    back_query = factor * jnp.einsum('ilj,clj->cil', grad_score, kf, precision=HIGH)
    back_key = factor * jnp.einsum('ilj,cil->clj', grad_score, qf, precision=HIGH)
    back_left = lax.map(lambda pair: jnp.einsum('ilj,ij,lj->il', prob, pair[0], pair[1], precision=HIGH), (gf, rf))
    back_right = lax.map(lambda pair: jnp.einsum('ilj,ij,il->lj', prob, pair[0], pair[1], precision=HIGH), (gf, lf))
    return (mixed.astype(jnp.bfloat16), back_query.astype(jnp.bfloat16), back_key.astype(jnp.bfloat16),
            back_left.astype(jnp.bfloat16), back_right.astype(jnp.bfloat16))


def reference(link_tensor_source, neighbour_allowance, asking_projector, lookup_projector, first_content_projector, second_content_projector, final_projector, per_slot_scaling, upstream_sensitivity):
    flat_pairs = link_tensor_source.reshape(D, N * N)
    flat_cot = upstream_sensitivity.reshape(D, N * N)
    w_cat = jnp.concatenate([asking_projector, lookup_projector, first_content_projector, second_content_projector], axis=1)
    mapped_activations = lax.dot_general(w_cat, flat_pairs, (((0,), (0,)), ((), ())), preferred_element_type=jnp.float32)
    mapped_activations = mapped_activations.astype(jnp.bfloat16).reshape(4, H, D // H, N, N)
    stacked_derivative = jnp.dot(final_projector, flat_cot, preferred_element_type=jnp.float32).astype(jnp.bfloat16)
    stacked_derivative = stacked_derivative.reshape(H, D // H, N, N)
    nodes = jnp.arange(N, dtype=jnp.int32)
    valid = (neighbour_allowance == 1) | (nodes[:, None] == nodes[None, :])
    mixed, back_query, back_key, back_left, back_right = lax.map(
        lambda group: head_backward(*group, valid),
        (mapped_activations[0], mapped_activations[1], mapped_activations[2], mapped_activations[3], stacked_derivative, per_slot_scaling))
    backs = jnp.concatenate([part.reshape(D, N * N) for part in (back_query, back_key, back_left, back_right)], axis=0)
    grad_pairs = jnp.dot(w_cat, backs, preferred_element_type=jnp.float32).astype(jnp.bfloat16).reshape(D, N, N)
    grad_weights = lax.dot_general(flat_pairs, backs, (((1,), (1,)), ((), ())), preferred_element_type=jnp.float32) / N
    grad_out = lax.dot_general(mixed.reshape(D, N * N), flat_cot, (((1,), (1,)), ((), ())), preferred_element_type=jnp.float32) / N
    return (grad_pairs, grad_weights[:, 0:D], grad_weights[:, D:2 * D], grad_weights[:, 2 * D:3 * D],
            grad_weights[:, 3 * D:4 * D], grad_out)
```

```python
import functools

import jax
import jax.numpy as jnp
from jax import lax
from jax.experimental import pallas as pl
from jax.experimental.pallas import tpu as pltpu
from jax.sharding import PartitionSpec as P

F32, BF16 = jnp.float32, jnp.bfloat16
MESH = pl.DeviceIdType.MESH
NT = (((1,), (1,)), ((), ()))
NN = (((1,), (0,)), ((), ()))
TN = (((0,), (0,)), ((), ()))
CH, I, L, J = 8, 64, 256, 128
NX = 8
HEADS, ROWS = 16, 8


def dot(a, b, dims=NN):
    return lax.dot_general(a, b, dims, preferred_element_type=F32)


def core_scratch():
    return dict(
        pt=pltpu.VMEM((1024, 1024), BF16),
        q2=pltpu.VMEM((I, 2048), BF16), b2=pltpu.VMEM((I, 2048), BF16),
        qt=pltpu.VMEM((2048, 128), BF16), kf=pltpu.VMEM((2048, J), F32), rf=pltpu.VMEM((2048, J), F32),
        k2=pltpu.VMEM((2048, J), BF16), mt=pltpu.VMEM((16, 256), BF16), wc=pltpu.VMEM((128, 1024), BF16), lb16=pltpu.VMEM((I, 2048), BF16), rg=pltpu.VMEM((2048, J), BF16),
        s=pltpu.VMEM((L, I, J), F32), m=pltpu.VMEM((I, J), F32), gs=pltpu.VMEM((CH, I, J), F32), ds=pltpu.VMEM((I, J), F32),
        mix=pltpu.VMEM((CH, I, J), F32), tot=pltpu.VMEM((I, J), F32),
        e=pltpu.VMEM((16, I, J), F32), br8=pltpu.VMEM((2, 64, J), F32), br2=pltpu.VMEM((2048, J), F32), bk2=pltpu.VMEM((2048, J), F32),
    )


def permutation(pt):
    @pl.loop(0, 8)
    def _(n):
        a = lax.broadcasted_iota(jnp.int32, (128, 1024), 0) + n * 128
        b = lax.broadcasted_iota(jnp.int32, (128, 1024), 1)
        hit = ((a >> 3) == (b & 127)) & ((a & 7) == (b >> 7))
        pt[pl.ds(pl.multiple_of(n * 128, 128), 128), :] = jnp.where(hit, 1.0, 0.0).astype(BF16)

def core(ql, kr, gg, fac, bq2, bl2, mixed, w, after=None):
    permutation(w["pt"])
    pt = w["pt"]
    row = lax.broadcasted_iota(jnp.int32, (16, 256), 0)
    lane = lax.broadcasted_iota(jnp.int32, (16, 256), 1)
    w["mt"][...] = jnp.where(((lane & 127) >> 3) == row, 1.0, 0.0).astype(BF16)
    ra = lax.broadcasted_iota(jnp.int32, (128, 1024), 0)
    rb_ = lax.broadcasted_iota(jnp.int32, (128, 1024), 1)
    w["wc"][...] = jnp.where((ra & 7) == (rb_ >> 7), 1.0, 0.0).astype(BF16)
    for half in range(2):
        cut = slice(half * 128, half * 128 + 128)
        out = slice(half * 1024, half * 1024 + 1024)
        both = lambda c: jnp.concatenate([ql[0, c, :, cut], ql[1, c, :, cut]], axis=0)
        qcat = jnp.concatenate([both(c) for c in range(CH)], axis=1)
        lcat = jnp.concatenate([both(CH + c) for c in range(CH)], axis=1)
        bcat = jnp.concatenate([both(2 * CH), jnp.zeros((I, 896), BF16)], axis=1)
        got = dot(jnp.concatenate([qcat, lcat, bcat], axis=0), pt[...], NT)
        w["q2"][:, out] = got[:I].astype(BF16)
        w["lb16"][:, out] = got[I:2 * I].astype(BF16)
        w["b2"][:, out] = got[2 * I:].astype(BF16)
        w["qt"][out, :] = dot(pt[...], jnp.concatenate([qcat, qcat], axis=0), NT).astype(BF16)
    for c in range(CH):
        for z in range(8):
            w["kf"][pl.ds(z * 256 + c, 32, stride=8), :] = kr[z, c].astype(F32)
            w["rf"][pl.ds(z * 256 + c, 32, stride=8), :] = kr[z, CH + c].astype(F32)
    w["k2"][...] = w["kf"][...].astype(BF16)
    w["rg"][...] = w["rf"][...].astype(BF16)
    w["m"][...] = jnp.full((I, J), -3e38, F32)

    @pl.loop(0, 16)
    def _(n):
        at = pl.ds(pl.multiple_of(n * 128, 128), 128)
        qb = jnp.concatenate([w["q2"][:, at], w["b2"][:, at]], axis=1)
        kk = jnp.concatenate([w["k2"][at, :], jnp.ones((128, J), BF16)], axis=0)
        lhs = jnp.concatenate([qb * w["mt"][t:t + 1, :] for t in range(16)], axis=0)
        raw = dot(lhs, kk).reshape(16, I, J)
        top = w["m"][...]
        for t in range(16):
            top = jnp.maximum(top, raw[t])
        w["m"][...] = top
        w["s"][pl.ds(n * 16, 16)] = raw

    f = fac[0]

    @pl.loop(0, 4)
    def _(ip):
        rows = pl.ds(pl.multiple_of(ip * 16, 16), 16)
        top = w["m"][rows, :]

        def step(n, carry):
            total, acc = carry
            acc = list(acc)
            tile = w["lb16"][rows, pl.ds(pl.multiple_of(n * 128, 128), 128)]
            lhs = jnp.concatenate([tile * w["mt"][t:t + 1, :128] for t in range(16)], axis=0)
            spread = dot(lhs, w["wc"][...])
            for t in range(16):
                lv = n * 16 + t
                wt = jnp.exp(f * (w["s"][lv, rows, :] - top))
                w["s"][lv, rows, :] = wt
                total = total + wt
                rr = w["rf"][pl.ds(pl.multiple_of(lv * 8, 8), 8), :]
                for c in range(CH):
                    lb = spread[t * 16:t * 16 + 16, c * 128:c * 128 + 128]
                    acc[c] = acc[c] + (wt * rr[c:c + 1, :]) * lb
            return total, tuple(acc)

        zero = jnp.zeros((16, J), F32)
        total, acc = lax.fori_loop(0, 16, step, (zero, (zero,) * CH))
        inv = 1.0 / total
        delta = zero
        for c in range(CH):
            gc = gg[ip >> 1, c, pl.ds(pl.multiple_of((ip & 1) * 16, 16), 16), :].astype(F32)
            mc = acc[c] * inv
            mixed[c, rows, :] = mc.astype(BF16)
            delta = delta + gc * mc
            w["gs"][c, rows, :] = gc * inv
        w["ds"][rows, :] = delta * inv

    lanes = lax.broadcasted_iota(jnp.int32, (8, 128), 1)

    @pl.loop(0, 16)
    def _(n):
        at = pl.ds(pl.multiple_of(n * 128, 128), 128)
        bl2[:, at] = jnp.zeros((I, 128), F32)

        rg = w["rg"][at, :]
        rdup = jnp.concatenate([rg, rg], axis=1)

        @pl.loop(0, 16, unroll=4)
        def _(t):
            lv = n * 16 + t
            lanes64 = lax.broadcasted_iota(jnp.int32, (I, 128), 1)
            pick = jnp.where((lanes64 >> 3) == t, 1.0, 0.0).astype(BF16)
            spread = dot(w["lb16"][:, at] * pick, w["wc"][...])
            rr = w["rf"][pl.ds(pl.multiple_of(lv * 8, 8), 8), :]
            rb = [jnp.broadcast_to(rr[c:c + 1, :], (8, J)) for c in range(CH)]
            br = [jnp.zeros((8, J), F32) for c in range(CH)]
            base = t * 8
            halves = [[] for c in range(CH)]
            for it in range(8):
                rows = slice(it * 8, it * 8 + 8)
                wt = w["s"][lv, rows, :]
                pgp = None
                for c in range(CH):
                    x = wt * w["gs"][c, rows, :]
                    xl = x * spread[rows, c * 128:c * 128 + 128]
                    br[c] = br[c] + xl
                    term = xl * rb[c]
                    pgp = term if pgp is None else pgp + term
                    halves[c].append(x)
                w["e"][t, rows, :] = pgp - wt * w["ds"][rows, :]
            blt = bl2[:, at]
            for c in range(CH):
                if c < NX:
                    red = jnp.sum(jnp.concatenate(halves[c], axis=0) * rr[c:c + 1, :], axis=1, keepdims=True)
                else:
                    xc = jnp.concatenate(halves[c], axis=0)
                    xh = xc.astype(BF16)
                    xo = (xc - xh.astype(F32)).astype(BF16)
                    red = dot(jnp.concatenate([xh, xo], axis=1), rdup, NT)
                blt = jnp.where(lanes64 == base + c, red, blt)
            bl2[:, at] = blt
            slot = lax.rem(t, 2)
            for c in range(CH):
                w["br8"][slot, c * 8:c * 8 + 8, :] = br[c]
            tot = w["br8"][slot, pl.ds(0, 8, stride=8), :]
            for z in range(1, 8):
                tot = tot + w["br8"][slot, pl.ds(z, 8, stride=8), :]
            w["br2"][pl.ds(pl.multiple_of(lv * 8, 8), 8), :] = tot

        ev = w["e"][...].reshape(16 * I, J)
        hi = ev.astype(BF16)
        lo = (ev - hi.astype(F32)).astype(BF16)
        kt = w["k2"][at, :]
        bqw = dot(jnp.concatenate([hi, lo], axis=1), jnp.concatenate([kt, kt], axis=1), NT)
        tot = jnp.zeros((I, 128), F32)
        lane2 = lax.broadcasted_iota(jnp.int32, (I, 128), 1)
        for t in range(16):
            tot = jnp.where((lane2 >> 3) == t, bqw[t * I:(t + 1) * I, :], tot)
        bq2[:, at] = f * tot
        sub_r = lax.broadcasted_iota(jnp.int32, (32, 256), 0)
        sub_c = lax.broadcasted_iota(jnp.int32, (32, 256), 1)
        keep = jnp.where((sub_r >> 3) == (sub_c >> 6), 1.0, 0.0).astype(BF16)
        for u in range(4):
            qrow = w["qt"][pl.ds(pl.multiple_of(n * 128 + u * 32, 32), 32), :]
            lhs = jnp.concatenate([qrow, qrow], axis=1) * keep
            part = dot(jnp.concatenate([lhs, lhs], axis=1), jnp.concatenate([hi[u * 256:u * 256 + 256], lo[u * 256:u * 256 + 256]], axis=0))
            w["bk2"][pl.ds(pl.multiple_of(n * 128 + u * 32, 32), 32), :] = f * part
        if after is not None:
            after(n)


def greet(groups):
    barrier = pltpu.get_barrier_semaphore()
    count = 0
    for axis, n in groups:
        me = lax.axis_index(axis)

        @pl.loop(1, n)
        def _(s):
            pl.semaphore_signal(barrier, inc=1, device_id={axis: lax.rem(me + s, n)}, device_id_type=MESH)

        count += n - 1
    pl.semaphore_wait(barrier, count)


class Trade:
    def __init__(self, axis, n, src, dst, send_sem, recv_sem):
        self.axis, self.n, self.src, self.dst, self.send_sem, self.recv_sem = axis, n, src, dst, send_sem, recv_sem
        self.me = lax.axis_index(axis)

    def copy(self, s):
        peer = lax.rem(self.me + s, self.n)
        return pltpu.make_async_remote_copy(
            src_ref=self.src(peer), dst_ref=self.dst(self.me), send_sem=self.send_sem.at[s], recv_sem=self.recv_sem.at[s],
            device_id={self.axis: peer}, device_id_type=MESH)

    def start(self):
        @pl.loop(1, self.n)
        def _(s):
            self.copy(s).start()

    def finish(self):
        @pl.loop(1, self.n)
        def _(s):
            self.copy(s).wait_recv()

    def drain(self):
        @pl.loop(1, self.n)
        def _(s):
            self.copy(s).wait_send()


def to_pairs(wide, stage, count):
    for i in range(32):
        for z in range(2):
            at = (i % 2) * 256 + z * 128
            stage[i // 2, :, at:at + 128] = wide[z, pl.ds(i, count, stride=32), :].astype(BF16)


def from_pairs(recv, wide, count):
    for i in range(32):
        for z in range(2):
            at = (i % 2) * 256 + z * 128
            wide[z, pl.ds(i, count, stride=32), :] = recv[i // 2, :, at:at + 128][:count].astype(F32)


def project_kernel(x, u, wself, nat, gathered, wall, xs, stage1, stage2, recv2, natf, sems):
    me = lax.axis_index("head")
    for z in range(2):
        xs[z, 0:256, :] = x[:, :, z * 128:z * 128 + 128].reshape(256, 128).astype(F32)
        xs[z, 256:512, :] = u[:, :, z * 128:z * 128 + 128].reshape(256, 128).astype(F32)
    to_pairs(xs, stage1, 16)
    greet([("head", HEADS)])
    first = Trade("head", HEADS, lambda p: stage1.at[p], lambda p: gathered.at[p], sems.at[0], sems.at[1])
    weights = Trade("head", HEADS, lambda p: wself, lambda p: wall.at[p], sems.at[2], sems.at[3])
    first.start()
    weights.start()
    gathered[me] = stage1[me]
    wall[me] = wself[...]
    first.finish()
    weights.finish()
    mapped = dot(wall[...].reshape(768, 256), gathered[...].reshape(256, 512))
    stage2[...] = mapped.astype(BF16).reshape(16, 48, 512)
    second = Trade("head", HEADS, lambda p: stage2.at[p], lambda p: recv2.at[p], sems.at[4], sems.at[5])
    second.start()
    recv2[me] = stage2[me]
    second.finish()
    from_pairs(recv2, natf, 40)
    for z in range(2):
        nat[:, :, z * 128:z * 128 + 128] = natf[z].astype(BF16).reshape(40, 32, 128)
    first.drain()
    weights.drain()
    second.drain()


def attention_kernel(names, nat, bias, fac, backs, ql, kr, gg, ql2, qlin, kro, krin, mx, mixin, sems, psems, *scratch):
    w = dict(zip(names, scratch))
    me = lax.axis_index("row")
    jb = lax.rem(me, 2)
    partner = me + 1 - 2 * jb
    pj = 1 - jb

    def half(j):
        return pl.ds(pl.multiple_of(j * 128, 128), 128)

    def to_partner(n, src, dst):
        return pltpu.make_async_remote_copy(src_ref=src, dst_ref=dst, send_sem=psems.at[0, n], recv_sem=psems.at[1, n],
                                            device_id={"row": partner}, device_id_type=MESH)

    greet([("row", ROWS)])
    pairs_in = Trade("row", ROWS, lambda p: kr_src.at[:, :, half(lax.rem(p, 2))], lambda p: kr.at[p], sems.at[0], sems.at[1])
    kr_src = nat.at[pl.ds(0, 16)]
    ahead = [
        to_partner(0, nat.at[pl.ds(16, 16)], ql.at[jb, pl.ds(0, 16)]),
        to_partner(1, bias, ql.at[jb, 16]),
        to_partner(2, nat.at[pl.ds(32, 8), :, half(pj)], gg.at[jb]),
    ]
    for copy in ahead:
        copy.start()
    pairs_in.start()
    ql[jb, 0:16] = nat[16:32]
    ql[jb, 16] = bias[...]
    gg[jb] = nat[32:40, :, half(jb)]
    kr[me] = nat[0:16, :, half(jb)]
    for copy in ahead:
        copy.wait()
    pairs_in.finish()
    core(ql, kr, gg, fac, ql2.at[0], ql2.at[1], mx, w)
    for z in range(8):
        for c in range(CH):
            kro[z, c] = w["bk2"][pl.ds(z * 256 + c, 32, stride=8), :]
            kro[z, CH + c] = w["br2"][pl.ds(z * 256 + c, 32, stride=8), :]
    pairs_out = Trade("row", ROWS, lambda p: kro.at[p], lambda p: krin.at[p], sems.at[2], sems.at[3])
    other = pl.ds(pl.multiple_of(pj * 32, 32), 32)
    own = pl.ds(pl.multiple_of(jb * 32, 32), 32)
    back = [to_partner(3, ql2.at[:, other], qlin), to_partner(4, mx.at[:, other], mixin)]
    for copy in back:
        copy.start()
    pairs_out.start()
    krin[me] = kro[me]
    for copy in back:
        copy.wait()
    both = (ql2[:, own, :] + qlin[...]).astype(BF16).reshape(64, 2048)
    for h in range(2):
        plain = dot(both[:, h * 1024:h * 1024 + 1024], w["pt"][...]).astype(BF16)
        for c in range(CH):
            backs[16 + c, :, h * 128:h * 128 + 128] = plain[0:32, c * 128:c * 128 + 128]
            backs[24 + c, :, h * 128:h * 128 + 128] = plain[32:64, c * 128:c * 128 + 128]
    backs[32:40, :, half(jb)] = mx[:, own, :]
    backs[32:40, :, half(pj)] = mixin[...]
    pairs_out.finish()
    for j in range(2):
        total = krin[j] + krin[2 + j] + krin[4 + j] + krin[6 + j]
        total = total.astype(BF16)
        backs[0:16, :, j * 128:j * 128 + 128] = total
    pairs_in.drain()
    pairs_out.drain()


def gradient_kernel(backs, gathered, wall, grads, weights, bf, stage3, recv3, stage4, recv4, gw, gwin, part, gwrow, gf, sems):
    me, row = lax.axis_index("head"), lax.axis_index("row")
    for z in range(2):
        bf[z, 0:1280, :] = backs[:, :, z * 128:z * 128 + 128].reshape(1280, 128).astype(F32)
        bf[z, 1280:1536, :] = jnp.zeros((256, 128), F32)
    to_pairs(bf, stage3, 48)
    greet([("head", HEADS), ("row", ROWS)])
    first = Trade("head", HEADS, lambda p: stage3.at[p], lambda p: recv3.at[p], sems.at[0], sems.at[1])
    first.start()
    recv3[me] = stage3[me]
    first.finish()
    every = recv3[...].reshape(768, 512)
    gw[...] = dot(every, gathered[...].reshape(256, 512), NT).reshape(16, 48, 256)
    sums = Trade("head", HEADS, lambda p: gw.at[p, pl.ds(0, 40)], lambda p: gwin.at[p], sems.at[2], sems.at[3])
    sums.start()
    gwin[me] = gw[me, 0:40, :]
    stage4[...] = dot(wall[...].reshape(768, 256), every, TN).astype(BF16).reshape(16, 16, 512)
    second = Trade("head", HEADS, lambda p: stage4.at[p], lambda p: recv4.at[p], sems.at[4], sems.at[5])
    second.start()
    recv4[me] = stage4[me]
    sums.finish()
    total = gwin[0]
    for p in range(1, 16):
        total = total + gwin[p]
    part[...] = total
    last = Trade("row", ROWS, lambda p: part, lambda p: gwrow.at[p], sems.at[6], sems.at[7])
    last.start()
    gwrow[row] = total
    second.finish()
    from_pairs(recv4, gf, 8)
    for z in range(2):
        grads[:, :, z * 128:z * 128 + 128] = gf[z].astype(BF16).reshape(8, 32, 128)
    last.finish()
    total = gwrow[0]
    for p in range(1, 8):
        total = total + gwrow[p]
    weights[...] = total * (1.0 / 256.0)
    for trade in (first, sums, second, last):
        trade.drain()


VM = pl.BlockSpec(memory_space=pltpu.VMEM)


def params(number):
    return pltpu.CompilerParams(collective_id=number, has_side_effects=True, vmem_limit_bytes=56 * 2 ** 20)


def local(x, allowance, asking, lookup, first_content, second_content, final, scaling, upstream):
    order = [lookup, second_content, asking, first_content]
    rows = jnp.concatenate(order, axis=1).T.reshape(32, 16, 1, 8)
    from_x = jnp.concatenate([rows, jnp.zeros_like(rows)], axis=2).reshape(32, 256)
    rows = final.reshape(8, 16, 1, 8)
    from_u = jnp.concatenate([jnp.zeros_like(rows), rows], axis=2).reshape(8, 256)
    wself = jnp.concatenate([from_x, from_u, jnp.zeros((8, 256), BF16)], axis=0)
    node = lax.axis_index("row") * 32 + lax.broadcasted_iota(jnp.int32, (32, 256), 0)
    valid = (allowance == 1) | (node == lax.broadcasted_iota(jnp.int32, (32, 256), 1))
    bias = jnp.where(valid, 0.0, -1e30).astype(BF16)

    dma = pltpu.SemaphoreType.DMA
    nat, gathered, wall = pl.pallas_call(
        project_kernel,
        out_shape=[jax.ShapeDtypeStruct((40, 32, 256), BF16), jax.ShapeDtypeStruct((16, 16, 512), BF16),
                   jax.ShapeDtypeStruct((16, 48, 256), BF16)],
        in_specs=[VM] * 3, out_specs=[VM] * 3,
        scratch_shapes=[pltpu.VMEM((2, 512, 128), F32), pltpu.VMEM((16, 16, 512), BF16), pltpu.VMEM((16, 48, 512), BF16),
                        pltpu.VMEM((16, 48, 512), BF16), pltpu.VMEM((2, 1280, 128), F32), dma((6, 16))],
        compiler_params=params(0), name="project",
    )(x, upstream, wself)

    names = core_scratch()
    backs = pl.pallas_call(
        functools.partial(attention_kernel, list(names)),
        out_shape=jax.ShapeDtypeStruct((40, 32, 256), BF16),
        in_specs=[VM, VM, pl.BlockSpec(memory_space=pltpu.SMEM)], out_specs=VM,
        scratch_shapes=[
            pltpu.VMEM((2, 17, 32, 256), BF16), pltpu.VMEM((8, 16, 32, 128), BF16), pltpu.VMEM((2, 8, 32, 128), BF16),
            pltpu.VMEM((2, 64, 2048), F32), pltpu.VMEM((2, 32, 2048), F32),
            pltpu.VMEM((8, 16, 32, 128), F32), pltpu.VMEM((8, 16, 32, 128), F32),
            pltpu.VMEM((8, 64, 128), BF16), pltpu.VMEM((8, 32, 128), BF16), dma((4, 8)), dma((2, 5)),
        ] + list(names.values()),
        compiler_params=params(1), name="attention",
    )(nat, bias, scaling)

    grads, weights = pl.pallas_call(
        gradient_kernel,
        out_shape=[jax.ShapeDtypeStruct((8, 32, 256), BF16), jax.ShapeDtypeStruct((40, 256), F32)],
        in_specs=[VM] * 3, out_specs=[VM] * 2,
        scratch_shapes=[
            pltpu.VMEM((2, 1536, 128), F32), pltpu.VMEM((16, 48, 512), BF16), pltpu.VMEM((16, 48, 512), BF16),
            pltpu.VMEM((16, 16, 512), BF16), pltpu.VMEM((16, 16, 512), BF16),
            pltpu.VMEM((16, 48, 256), F32), pltpu.VMEM((16, 40, 256), F32), pltpu.VMEM((40, 256), F32),
            pltpu.VMEM((8, 40, 256), F32), pltpu.VMEM((2, 256, 128), F32), dma((8, 16)),
        ],
        compiler_params=params(2), name="gradient",
    )(backs, gathered, wall)
    split = weights.reshape(5, 8, 16, 2, 8)
    of_x = split[:4, :, :, 0, :].reshape(4, 8, 128)
    of_u = split[4, :, :, 1, :].reshape(8, 128)
    return grads, of_x[2].T, of_x[0].T, of_x[3].T, of_x[1].T, of_u


def solution(mesh):
    pairs, columns = P("head", "row", None), P(None, "head")
    placed = (pairs, P("row", None), columns, columns, columns, columns, P("head", None), P("head"), pairs)
    return jax.shard_map(
        local, mesh=mesh, in_specs=placed,
        out_specs=(pairs, columns, columns, columns, columns, P("head", None)), check_vma=False,
    )
```

```python
import functools

import jax
import jax.numpy as jnp
from jax import lax
from jax.experimental import pallas as pl
from jax.experimental.pallas import tpu as pltpu
from jax.sharding import PartitionSpec as P

F32, BF16 = jnp.float32, jnp.bfloat16
MESH = pl.DeviceIdType.MESH
NT = (((1,), (1,)), ((), ()))
NN = (((1,), (0,)), ((), ()))
TN = (((0,), (0,)), ((), ()))
CH, I, L, J = 8, 64, 256, 128
NX = 8
HEADS, ROWS = 16, 8


def dot(a, b, dims=NN):
    return lax.dot_general(a, b, dims, preferred_element_type=F32)


def core_scratch():
    return dict(
        pt=pltpu.VMEM((1024, 1024), BF16),
        q2=pltpu.VMEM((I, 2048), BF16), b2=pltpu.VMEM((I, 2048), BF16),
        qt=pltpu.VMEM((2048, 128), BF16), kf=pltpu.VMEM((2048, J), F32), rf=pltpu.VMEM((2048, J), F32),
        k2=pltpu.VMEM((2048, J), BF16), mt=pltpu.VMEM((16, 256), BF16), wc=pltpu.VMEM((128, 1024), BF16), lb16=pltpu.VMEM((I, 2048), BF16), rg=pltpu.VMEM((2048, J), BF16),
        s=pltpu.VMEM((L, I, J), F32), m=pltpu.VMEM((I, J), F32), gs=pltpu.VMEM((CH, I, J), F32), ds=pltpu.VMEM((I, J), F32),

        e=pltpu.VMEM((16, I, J), F32), br8=pltpu.VMEM((2, 64, J), F32), br2=pltpu.VMEM((256, J), F32), bk2=pltpu.VMEM((256, J), F32),
    )


def permutation(pt):
    @pl.loop(0, 8)
    def _(n):
        a = lax.broadcasted_iota(jnp.int32, (128, 1024), 0) + n * 128
        b = lax.broadcasted_iota(jnp.int32, (128, 1024), 1)
        hit = ((a >> 3) == (b & 127)) & ((a & 7) == (b >> 7))
        pt[pl.ds(pl.multiple_of(n * 128, 128), 128), :] = jnp.where(hit, 1.0, 0.0).astype(BF16)


def constants(w):
    permutation(w["pt"])
    row = lax.broadcasted_iota(jnp.int32, (16, 256), 0)
    lane = lax.broadcasted_iota(jnp.int32, (16, 256), 1)
    w["mt"][...] = jnp.where(((lane & 127) >> 3) == row, 1.0, 0.0).astype(BF16)
    ra = lax.broadcasted_iota(jnp.int32, (128, 1024), 0)
    rb_ = lax.broadcasted_iota(jnp.int32, (128, 1024), 1)
    w["wc"][...] = jnp.where((ra & 7) == (rb_ >> 7), 1.0, 0.0).astype(BF16)


def scores(ql, kr, w):
    pt = w["pt"]
    for half in range(2):
        cut = slice(half * 128, half * 128 + 128)
        out = slice(half * 1024, half * 1024 + 1024)
        both = lambda c: jnp.concatenate([ql[0, c, :, cut], ql[1, c, :, cut]], axis=0)
        qcat = jnp.concatenate([both(c) for c in range(CH)], axis=1)
        lcat = jnp.concatenate([both(CH + c) for c in range(CH)], axis=1)
        bcat = jnp.concatenate([both(2 * CH), jnp.zeros((I, 896), BF16)], axis=1)
        got = dot(jnp.concatenate([qcat, lcat, bcat], axis=0), pt[...], NT)
        w["q2"][:, out] = got[:I].astype(BF16)
        w["lb16"][:, out] = got[I:2 * I].astype(BF16)
        w["b2"][:, out] = got[2 * I:].astype(BF16)
        w["qt"][out, :] = dot(pt[...], jnp.concatenate([qcat, qcat], axis=0), NT).astype(BF16)
    for c in range(CH):
        for z in range(8):
            w["kf"][pl.ds(z * 256 + c, 32, stride=8), :] = kr[z, c].astype(F32)
            w["rf"][pl.ds(z * 256 + c, 32, stride=8), :] = kr[z, CH + c].astype(F32)
    w["k2"][...] = w["kf"][...].astype(BF16)
    w["rg"][...] = w["rf"][...].astype(BF16)
    w["m"][...] = jnp.full((I, J), -3e38, F32)

    @pl.loop(0, 16)
    def _(n):
        at = pl.ds(pl.multiple_of(n * 128, 128), 128)
        qb = jnp.concatenate([w["q2"][:, at], w["b2"][:, at]], axis=1)
        kk = jnp.concatenate([w["k2"][at, :], jnp.ones((128, J), BF16)], axis=0)
        lhs = jnp.concatenate([qb * w["mt"][t:t + 1, :] for t in range(16)], axis=0)
        raw = dot(lhs, kk).reshape(16, I, J)
        top = w["m"][...]
        for t in range(16):
            top = jnp.maximum(top, raw[t])
        w["m"][...] = top
        w["s"][pl.ds(n * 16, 16)] = raw


def forward(gg, f, mixed, w):
    @pl.loop(0, 4)
    def _(ip):
        rows = pl.ds(pl.multiple_of(ip * 16, 16), 16)
        top = w["m"][rows, :]

        def step(n, carry):
            total, acc = carry
            acc = list(acc)
            tile = w["lb16"][rows, pl.ds(pl.multiple_of(n * 128, 128), 128)]
            lhs = jnp.concatenate([tile * w["mt"][t:t + 1, :128] for t in range(16)], axis=0)
            spread = dot(lhs, w["wc"][...])
            for t in range(16):
                lv = n * 16 + t
                wt = jnp.exp(f * (w["s"][lv, rows, :] - top))
                w["s"][lv, rows, :] = wt
                total = total + wt
                rr = w["rf"][pl.ds(pl.multiple_of(lv * 8, 8), 8), :]
                for c in range(CH):
                    lb = spread[t * 16:t * 16 + 16, c * 128:c * 128 + 128]
                    acc[c] = acc[c] + (wt * rr[c:c + 1, :]) * lb
            return total, tuple(acc)

        zero = jnp.zeros((16, J), F32)
        total, acc = lax.fori_loop(0, 16, step, (zero, (zero,) * CH))
        inv = 1.0 / total
        delta = zero
        for c in range(CH):
            gc = gg[ip >> 1, c, pl.ds(pl.multiple_of((ip & 1) * 16, 16), 16), :].astype(F32)
            mc = acc[c] * inv
            mixed[c, rows, :] = mc.astype(BF16)
            delta = delta + gc * mc
            w["gs"][c, rows, :] = gc * inv
        w["ds"][rows, :] = delta * inv


def backward(n, block, f, bq2, bl2, w):
    at = pl.ds(pl.multiple_of(n * 128, 128), 128)
    bl2[:, at] = jnp.zeros((I, 128), F32)

    rg = w["rg"][at, :]
    rdup = jnp.concatenate([rg, rg], axis=1)

    @pl.loop(0, 16, unroll=4)
    def _(t):
        lv = n * 16 + t
        lanes64 = lax.broadcasted_iota(jnp.int32, (I, 128), 1)
        pick = jnp.where((lanes64 >> 3) == t, 1.0, 0.0).astype(BF16)
        spread = dot(w["lb16"][:, at] * pick, w["wc"][...])
        rr = w["rf"][pl.ds(pl.multiple_of(lv * 8, 8), 8), :]
        rb = [jnp.broadcast_to(rr[c:c + 1, :], (8, J)) for c in range(CH)]
        br = [jnp.zeros((8, J), F32) for c in range(CH)]
        base = t * 8
        halves = [[] for c in range(CH)]
        for it in range(8):
            rows = slice(it * 8, it * 8 + 8)
            wt = w["s"][lv, rows, :]
            pgp = None
            for c in range(CH):
                x = wt * w["gs"][c, rows, :]
                xl = x * spread[rows, c * 128:c * 128 + 128]
                br[c] = br[c] + xl
                term = xl * rb[c]
                pgp = term if pgp is None else pgp + term
                halves[c].append(x)
            w["e"][t, rows, :] = pgp - wt * w["ds"][rows, :]
        blt = bl2[:, at]
        for c in range(CH):
            if c < NX:
                red = jnp.sum(jnp.concatenate(halves[c], axis=0) * rr[c:c + 1, :], axis=1, keepdims=True)
            else:
                xc = jnp.concatenate(halves[c], axis=0)
                xh = xc.astype(BF16)
                xo = (xc - xh.astype(F32)).astype(BF16)
                red = dot(jnp.concatenate([xh, xo], axis=1), rdup, NT)
            blt = jnp.where(lanes64 == base + c, red, blt)
        bl2[:, at] = blt
        slot = lax.rem(t, 2)
        for c in range(CH):
            w["br8"][slot, c * 8:c * 8 + 8, :] = br[c]
        tot = w["br8"][slot, pl.ds(0, 8, stride=8), :]
        for z in range(1, 8):
            tot = tot + w["br8"][slot, pl.ds(z, 8, stride=8), :]
        w["br2"][pl.ds(pl.multiple_of(block * 128 + t * 8, 8), 8), :] = tot

    ev = w["e"][...].reshape(16 * I, J)
    hi = ev.astype(BF16)
    lo = (ev - hi.astype(F32)).astype(BF16)
    kt = w["k2"][at, :]
    bqw = dot(jnp.concatenate([hi, lo], axis=1), jnp.concatenate([kt, kt], axis=1), NT)
    tot = jnp.zeros((I, 128), F32)
    lane2 = lax.broadcasted_iota(jnp.int32, (I, 128), 1)
    for t in range(16):
        tot = jnp.where((lane2 >> 3) == t, bqw[t * I:(t + 1) * I, :], tot)
    bq2[:, at] = f * tot
    sub_r = lax.broadcasted_iota(jnp.int32, (32, 256), 0)
    sub_c = lax.broadcasted_iota(jnp.int32, (32, 256), 1)
    keep = jnp.where((sub_r >> 3) == (sub_c >> 6), 1.0, 0.0).astype(BF16)
    for u in range(4):
        qrow = w["qt"][pl.ds(pl.multiple_of(n * 128 + u * 32, 32), 32), :]
        lhs = jnp.concatenate([qrow, qrow], axis=1) * keep
        part = dot(jnp.concatenate([lhs, lhs], axis=1), jnp.concatenate([hi[u * 256:u * 256 + 256], lo[u * 256:u * 256 + 256]], axis=0))
        w["bk2"][pl.ds(pl.multiple_of(block * 128 + u * 32, 32), 32), :] = f * part


def greet(groups):
    barrier = pltpu.get_barrier_semaphore()
    for axis, n in groups:
        me = lax.axis_index(axis)

        @pl.loop(1, n)
        def _(s):
            pl.semaphore_signal(barrier, inc=1, device_id={axis: lax.rem(me + s, n)}, device_id_type=MESH)


class Trade:
    def __init__(self, axis, n, src, dst, send_sem, recv_sem):
        self.axis, self.n, self.src, self.dst, self.send_sem, self.recv_sem = axis, n, src, dst, send_sem, recv_sem
        self.me = lax.axis_index(axis)

    def copy(self, s):
        peer = lax.rem(self.me + s, self.n)
        return pltpu.make_async_remote_copy(
            src_ref=self.src(peer), dst_ref=self.dst(self.me), send_sem=self.send_sem.at[s], recv_sem=self.recv_sem.at[s],
            device_id={self.axis: peer}, device_id_type=MESH)

    def start(self):
        @pl.loop(1, self.n)
        def _(s):
            self.copy(s).start()

    def finish(self):
        @pl.loop(1, self.n)
        def _(s):
            self.copy(s).wait_recv()

    def drain(self):
        @pl.loop(1, self.n)
        def _(s):
            self.copy(s).wait_send()


def to_pairs(wide, stage, count, pad=0):
    for i in range(32):
        for z in range(2):
            at = (i % 2) * 256 + z * 128
            piece = wide[z, pl.ds(i, count, stride=32), :]
            if pad:
                piece = jnp.concatenate([piece, jnp.zeros((pad, 128), F32)], axis=0)
            stage[i // 2, :, at:at + 128] = piece.astype(BF16)


def from_pairs(recv, wide, count):
    for i in range(32):
        for z in range(2):
            at = (i % 2) * 256 + z * 128
            wide[z, pl.ds(i, count, stride=32), :] = recv[i // 2, :, at:at + 128][:count].astype(F32)


def layer(names, x, u, wq, wk, wl, wr, wf, allowance, fac, grads, gq, gk, gl, gr, go, *scratch):
    w = dict(zip(names, scratch))
    me, row = lax.axis_index("head"), lax.axis_index("row")
    jb = lax.rem(row, 2)
    partner, pj = row + 1 - 2 * jb, 1 - jb
    other = pl.ds(pl.multiple_of(pj * 32, 32), 32)
    own = pl.ds(pl.multiple_of(jb * 32, 32), 32)
    hs, rs, ps = w["hs"], w["rs"], w["ps"]

    def half(j):
        return pl.ds(pl.multiple_of(j * 128, 128), 128)

    def over_head(n, src, dst):
        return Trade("head", HEADS, src, dst, hs.at[2 * n], hs.at[2 * n + 1])

    def over_row(n, src, dst):
        return Trade("row", ROWS, src, dst, rs.at[2 * n], rs.at[2 * n + 1])

    def to_partner(n, src, dst):
        return pltpu.make_async_remote_copy(src_ref=src, dst_ref=dst, send_sem=ps.at[0, n], recv_sem=ps.at[1, n],
                                            device_id={"row": partner}, device_id_type=MESH)

    greet([("head", HEADS), ("row", ROWS)])
    wself, wall, wide = w["wself"], w["wall"], w["wide"]
    wself[...] = jnp.concatenate([wk[...], wr[...], wq[...], wl[...], wf[...], jnp.zeros((8, 128), BF16)], axis=0)
    for z in range(2):
        wide[z, 0:256, :] = x[:, :, z * 128:z * 128 + 128].reshape(256, 128).astype(F32)
        wide[z, 256:512, :] = u[:, :, z * 128:z * 128 + 128].reshape(256, 128).astype(F32)
    to_pairs(wide, w["stage1"], 16)
    pl.semaphore_wait(pltpu.get_barrier_semaphore(), HEADS + ROWS - 2)
    inputs = over_head(0, lambda p: w["stage1"].at[p], lambda p: w["recv1"].at[p])
    weights = over_head(1, lambda p: wself, lambda p: wall.at[p])
    weights.start()
    inputs.start()
    w["recv1"][me] = w["stage1"][me]
    wall[me] = wself[...]
    constants(w)
    node = row * 32 + lax.broadcasted_iota(jnp.int32, (32, 256), 0)
    valid = (allowance[...] == 1) | (node == lax.broadcasted_iota(jnp.int32, (32, 256), 1))
    w["bias"][...] = jnp.where(valid, 0.0, -1e30).astype(BF16)
    bias_out = to_partner(0, w["bias"], w["ql"].at[jb, 16])
    bias_out.start()
    w["ql"][jb, 16] = w["bias"][...]
    inputs.finish()
    both = w["recv1"][...].astype(F32)
    w["xp"][...] = both[:, 0:8].reshape(128, 512).astype(BF16)
    w["up"][...] = both[:, 8:16].reshape(128, 512).astype(BF16)
    weights.finish()

    mapped = over_head(2, lambda p: w["stage2"].at[p], lambda p: w["recv2"].at[p])
    for first in range(0, HEADS, 4):
        peers = [lax.rem(me + first + a, HEADS) for a in range(4)]
        of_x = dot(jnp.concatenate([wall[p, 0:32] for p in peers], axis=0), w["xp"][...]).astype(BF16)
        of_u = dot(jnp.concatenate([wall[p, 32:48] for p in peers], axis=0), w["up"][...]).astype(BF16)
        for a, p in enumerate(peers):
            w["stage2"][p, 0:32] = of_x[a * 32:a * 32 + 32]
            w["stage2"][p, 32:48] = of_u[a * 16:a * 16 + 16]
            if first + a:
                mapped.copy(first + a).start()
            else:
                w["recv2"][me] = w["stage2"][me]
    mapped.finish()
    from_pairs(w["recv2"], wide, 40)
    nat = w["nat"]
    for z in range(2):
        nat[:, :, z * 128:z * 128 + 128] = wide[z, 0:1280, :].astype(BF16).reshape(40, 32, 128)

    ql, kr, gg = w["ql"], w["kr"], w["gg"]
    pairs_in = over_row(0, lambda p: nat.at[pl.ds(0, 16), :, half(lax.rem(p, 2))], lambda p: kr.at[p])
    ahead = [to_partner(1, nat.at[pl.ds(16, 16)], ql.at[jb, pl.ds(0, 16)]),
             to_partner(2, nat.at[pl.ds(32, 8), :, half(pj)], gg.at[jb])]
    pairs_in.start()
    for copy in ahead:
        copy.start()
    ql[jb, 0:16] = nat[16:32]
    gg[jb] = nat[32:40, :, half(jb)]
    kr[row] = nat[0:16, :, half(jb)]
    bias_out.wait()
    for copy in ahead:
        copy.wait()
    pairs_in.finish()

    f = fac[0]
    scores(ql, kr, w)
    forward(gg, f, w["mx"], w)
    mixed_out = to_partner(3, w["mx"].at[:, other], w["mixin"])
    mixed_out.start()
    ql2, qlin, kro, krin = w["ql2"], w["qlin"], w["kro"], w["krin"]
    pairs_out = over_row(1, lambda p: kro.at[p], lambda p: krin.at[p])
    mixed = over_head(3, lambda p: w["stagem"].at[p], lambda p: w["recvm"].at[p])

    def block_out(k, z):
        part = pl.ds(pl.multiple_of(z * 256, 256), 256)
        return to_partner(4 + k, ql2.at[:, other, part], qlin.at[:, :, part])

    @pl.loop(0, ROWS)
    def _(k):
        z = lax.rem(row + 1 + k, ROWS)

        @pl.loop(0, 2)
        def _(block):
            backward(2 * z + block, block, f, ql2.at[0], ql2.at[1], w)

        for c in range(CH):
            kro[z, c] = w["bk2"][pl.ds(c, 32, stride=8), :]
            kro[z, CH + c] = w["br2"][pl.ds(c, 32, stride=8), :]
        block_out(k, z).start()

        @pl.when(k < ROWS - 1)
        def _():
            pairs_out.copy(k + 1).start()

        @pl.when(k == ROWS - 1)
        def _():
            krin[row] = kro[row]

        @pl.when(k == 0)
        def _():
            mixed_out.wait()
            mixf = w["mixf"]
            for c in range(CH):
                mixf[jb, c * 32:c * 32 + 32, :] = w["mx"][c, own, :].astype(F32)
                mixf[pj, c * 32:c * 32 + 32, :] = w["mixin"][c].astype(F32)
            to_pairs(mixf, w["stagem"], 8, 8)
            mixed.start()
            w["recvm"][me] = w["stagem"][me]

    @pl.loop(0, ROWS)
    def _(k):
        block_out(k, lax.rem(row + 1 + k, ROWS)).wait()

    total = (ql2[:, own, :] + qlin[...]).astype(BF16).reshape(64, 2048)
    for h in range(2):
        plain = dot(total[:, h * 1024:h * 1024 + 1024], w["pt"][...])
        for c in range(CH):
            wide[h, 512 + c * 32:544 + c * 32, :] = plain[0:32, c * 128:c * 128 + 128]
            wide[h, 768 + c * 32:800 + c * 32, :] = plain[32:64, c * 128:c * 128 + 128]
    mixed.finish()
    gu = dot(w["recvm"][...].reshape(256, 512), w["up"][...], NT).reshape(16, 16, 128)
    gws = w["gws"]
    gws[:, 32:40, :] = gu[:, 0:8]
    pairs_out.finish()
    for j in range(2):
        total = krin[j] + krin[2 + j] + krin[4 + j] + krin[6 + j]
        wide[j, 0:512, :] = total.reshape(512, 128)
    to_pairs(wide, w["stage3"], 32)
    backs = over_head(4, lambda p: w["stage3"].at[p], lambda p: w["recv3"].at[p])
    backs.start()
    w["recv3"][me] = w["stage3"][me]
    backs.finish()

    every = w["recv3"][...].reshape(512, 512)
    gws[:, 0:32, :] = dot(every, w["xp"][...], NT).reshape(16, 32, 128)
    sums = over_head(5, lambda p: gws.at[p], lambda p: w["gwin"].at[p])
    sums.start()
    w["gwin"][me] = gws[me]
    image = dot(wall[:, 0:32, :].reshape(512, 128), every, TN).reshape(16, 8, 512)
    w["stage4"][...] = jnp.concatenate([image, jnp.zeros((16, 8, 512), F32)], axis=1).astype(BF16)
    images = over_head(6, lambda p: w["stage4"].at[p], lambda p: w["recv4"].at[p])
    images.start()
    w["recv4"][me] = w["stage4"][me]
    sums.finish()
    total = w["gwin"][0]
    for p in range(1, HEADS):
        total = total + w["gwin"][p]
    w["part"][...] = total
    last = over_row(2, lambda p: w["part"], lambda p: w["gwrow"].at[p])
    last.start()
    w["gwrow"][row] = total
    images.finish()
    from_pairs(w["recv4"], wide, 8)
    for z in range(2):
        grads[:, :, z * 128:z * 128 + 128] = wide[z, 0:256, :].astype(BF16).reshape(8, 32, 128)
    last.finish()
    total = w["gwrow"][0]
    for p in range(1, ROWS):
        total = total + w["gwrow"][p]
    total = total * (1.0 / 256.0)
    for n, out in enumerate((gk, gr, gq, gl, go)):
        out[...] = total[8 * n:8 * n + 8]
    for trade in (inputs, weights, mapped, pairs_in, pairs_out, mixed, backs, sums, images, last):
        trade.drain()


def layer_scratch():
    vmem, dma = pltpu.VMEM, pltpu.SemaphoreType.DMA
    return dict(
        core_scratch(),
        wide=vmem((2, 1280, 128), F32), wself=vmem((48, 128), BF16), wall=vmem((16, 48, 128), BF16),
        stage1=vmem((16, 16, 512), BF16), recv1=vmem((16, 16, 512), BF16), xp=vmem((128, 512), BF16), up=vmem((128, 512), BF16),
        stage2=vmem((16, 48, 512), BF16), recv2=vmem((16, 48, 512), BF16), nat=vmem((40, 32, 256), BF16), bias=vmem((32, 256), BF16),
        ql=vmem((2, 17, 32, 256), BF16), kr=vmem((8, 16, 32, 128), BF16), gg=vmem((2, 8, 32, 128), BF16),
        ql2=vmem((2, 64, 2048), F32), qlin=vmem((2, 32, 2048), F32), kro=vmem((8, 16, 32, 128), F32), krin=vmem((8, 16, 32, 128), F32),
        mx=vmem((8, 64, 128), BF16), mixin=vmem((8, 32, 128), BF16), mixf=vmem((2, 256, 128), F32),
        stagem=vmem((16, 16, 512), BF16), recvm=vmem((16, 16, 512), BF16),
        stage3=vmem((16, 32, 512), BF16), recv3=vmem((16, 32, 512), BF16), stage4=vmem((16, 16, 512), BF16), recv4=vmem((16, 16, 512), BF16),
        gws=vmem((16, 40, 128), F32), gwin=vmem((16, 40, 128), F32), part=vmem((40, 128), F32), gwrow=vmem((8, 40, 128), F32),
        hs=dma((14, 16)), rs=dma((6, 8)), ps=dma((2, 12)),
    )


def local(x, allowance, asking, lookup, first_content, second_content, final, scaling, upstream):
    vm = pl.BlockSpec(memory_space=pltpu.VMEM)
    names = layer_scratch()
    grads, gq, gk, gl, gr, go = pl.pallas_call(
        functools.partial(layer, list(names)),
        out_shape=[jax.ShapeDtypeStruct((8, 32, 256), BF16)] + [jax.ShapeDtypeStruct((8, 128), F32)] * 5,
        in_specs=[vm] * 8 + [pl.BlockSpec(memory_space=pltpu.SMEM)], out_specs=[vm] * 6,
        scratch_shapes=list(names.values()),
        compiler_params=pltpu.CompilerParams(collective_id=0, has_side_effects=True, vmem_limit_bytes=56 * 2 ** 20),
        name="layer",
    )(x, upstream, asking.T, lookup.T, first_content.T, second_content.T, final, allowance, scaling)
    return grads, gq.T, gk.T, gl.T, gr.T, go


def solution(mesh):
    pairs, columns = P("head", "row", None), P(None, "head")
    placed = (pairs, P("row", None), columns, columns, columns, columns, P("head", None), P("head"), pairs)
    return jax.shard_map(
        local, mesh=mesh, in_specs=placed,
        out_specs=(pairs, columns, columns, columns, columns, P("head", None)), check_vma=False,
    )
```

```python
import functools

import jax
import jax.numpy as jnp
from jax import lax
from jax.experimental import pallas as pl
from jax.experimental.pallas import tpu as pltpu
from jax.sharding import PartitionSpec as P

F32, BF16 = jnp.float32, jnp.bfloat16
MESH = pl.DeviceIdType.MESH
NT = (((1,), (1,)), ((), ()))
NN = (((1,), (0,)), ((), ()))
TN = (((0,), (0,)), ((), ()))
CH, I, L, J = 8, 64, 256, 128
HEADS, ROWS = 16, 8


def dot(a, b, dims=NN):
    return lax.dot_general(a, b, dims, preferred_element_type=F32)


def core_scratch():
    return dict(
        pt=pltpu.VMEM((1024, 1024), BF16),
        q2=pltpu.VMEM((I, 2048), BF16), b2=pltpu.VMEM((I, 2048), BF16),
        qt=pltpu.VMEM((2048, 128), BF16), kf=pltpu.VMEM((2048, J), F32), rf=pltpu.VMEM((2048, J), F32),
        k2=pltpu.VMEM((2048, J), BF16), mt=pltpu.VMEM((16, 256), BF16), wc=pltpu.VMEM((128, 1024), BF16), lb16=pltpu.VMEM((I, 2048), BF16),
        s=pltpu.VMEM((L, I, J), F32), m=pltpu.VMEM((I, J), F32), gs=pltpu.VMEM((CH, I, J), F32), ds=pltpu.VMEM((I, J), F32),

        e=pltpu.VMEM((16, I, J), F32), br8=pltpu.VMEM((2, 64, J), F32),
    )


def permutation(pt):
    @pl.loop(0, 8)
    def _(n):
        a = lax.broadcasted_iota(jnp.int32, (128, 1024), 0) + n * 128
        b = lax.broadcasted_iota(jnp.int32, (128, 1024), 1)
        hit = ((a >> 3) == (b & 127)) & ((a & 7) == (b >> 7))
        pt[pl.ds(pl.multiple_of(n * 128, 128), 128), :] = jnp.where(hit, 1.0, 0.0).astype(BF16)


def constants(w):
    permutation(w["pt"])
    row = lax.broadcasted_iota(jnp.int32, (16, 256), 0)
    lane = lax.broadcasted_iota(jnp.int32, (16, 256), 1)
    w["mt"][...] = jnp.where(((lane & 127) >> 3) == row, 1.0, 0.0).astype(BF16)
    ra = lax.broadcasted_iota(jnp.int32, (128, 1024), 0)
    rb_ = lax.broadcasted_iota(jnp.int32, (128, 1024), 1)
    w["wc"][...] = jnp.where((ra & 7) == (rb_ >> 7), 1.0, 0.0).astype(BF16)


def prepare(wide, w):
    pt = w["pt"]
    for half in range(2):
        out = slice(half * 1024, half * 1024 + 1024)
        qcat = jnp.concatenate([wide[half, c * I:c * I + I, :] for c in range(CH)], axis=1).astype(BF16)
        lcat = jnp.concatenate([wide[half, c * I:c * I + I, :] for c in range(CH, 2 * CH)], axis=1).astype(BF16)
        bcat = jnp.concatenate([wide[half, 24 * I:25 * I, :].astype(BF16), jnp.zeros((I, 896), BF16)], axis=1)
        got = dot(jnp.concatenate([qcat, lcat, bcat], axis=0), pt[...], NT)
        w["q2"][:, out] = got[:I].astype(BF16)
        w["lb16"][:, out] = got[I:2 * I].astype(BF16)
        w["b2"][:, out] = got[2 * I:].astype(BF16)
        w["qt"][out, :] = dot(pt[...], jnp.concatenate([qcat, qcat], axis=0), NT).astype(BF16)
    w["m"][...] = jnp.full((I, J), -3e38, F32)


def scores(n, w):
    at = pl.ds(pl.multiple_of(n * 128, 128), 128)
    k2 = w["kf"][at, :].astype(BF16)
    w["k2"][at, :] = k2
    qb = jnp.concatenate([w["q2"][:, at], w["b2"][:, at]], axis=1)
    kk = jnp.concatenate([k2, jnp.ones((128, J), BF16)], axis=0)
    lhs = jnp.concatenate([qb * w["mt"][t:t + 1, :] for t in range(16)], axis=0)
    raw = dot(lhs, kk).reshape(16, I, J)
    top = w["m"][...]
    for t in range(16):
        top = jnp.maximum(top, raw[t])
    w["m"][...] = top
    w["s"][pl.ds(n * 16, 16)] = raw


def forward(wide, mine, f, mixed, w):
    @pl.loop(0, 4)
    def _(ip):
        rows = pl.ds(pl.multiple_of(ip * 16, 16), 16)
        top = w["m"][rows, :]

        def step(n, carry):
            total, acc = carry
            acc = list(acc)
            tile = w["lb16"][rows, pl.ds(pl.multiple_of(n * 128, 128), 128)]
            lhs = jnp.concatenate([tile * w["mt"][t:t + 1, :128] for t in range(16)], axis=0)
            spread = dot(lhs, w["wc"][...])
            for t in range(16):
                lv = n * 16 + t
                wt = jnp.exp(f * (w["s"][lv, rows, :] - top))
                w["s"][lv, rows, :] = wt
                total = total + wt
                rr = w["rf"][pl.ds(pl.multiple_of(lv * 8, 8), 8), :]
                for c in range(CH):
                    lb = spread[t * 16:t * 16 + 16, c * 128:c * 128 + 128]
                    acc[c] = acc[c] + (wt * rr[c:c + 1, :]) * lb
            return total, tuple(acc)

        zero = jnp.zeros((16, J), F32)
        total, acc = lax.fori_loop(0, 16, step, (zero, (zero,) * CH))
        inv = 1.0 / total
        delta = zero
        for c in range(CH):
            gc = wide[mine, pl.ds(pl.multiple_of((16 + c) * I + ip * 16, 16), 16), :]
            mc = acc[c] * inv
            mixed[c, rows, :] = mc.astype(BF16)
            delta = delta + gc * mc
            w["gs"][c, rows, :] = gc * inv
        w["ds"][rows, :] = delta * inv


def backward(n, chip, place, f, bq2, bl2, kro, w):
    at = pl.ds(pl.multiple_of(n * 128, 128), 128)
    bl2[:, at] = jnp.zeros((I, 128), F32)

    @pl.loop(0, 16, unroll=4)
    def _(t):
        lv = n * 16 + t
        lanes64 = lax.broadcasted_iota(jnp.int32, (I, 128), 1)
        pick = jnp.where((lanes64 >> 3) == t, 1.0, 0.0).astype(BF16)
        spread = dot(w["lb16"][:, at] * pick, w["wc"][...])
        rr = w["rf"][pl.ds(pl.multiple_of(lv * 8, 8), 8), :]
        rb = [jnp.broadcast_to(rr[c:c + 1, :], (8, J)) for c in range(CH)]
        br = [jnp.zeros((8, J), F32) for c in range(CH)]
        base = t * 8
        halves = [[] for c in range(CH)]
        for it in range(8):
            rows = slice(it * 8, it * 8 + 8)
            wt = w["s"][lv, rows, :]
            pgp = None
            for c in range(CH):
                x = wt * w["gs"][c, rows, :]
                xl = x * spread[rows, c * 128:c * 128 + 128]
                br[c] = br[c] + xl
                term = xl * rb[c]
                pgp = term if pgp is None else pgp + term
                halves[c].append(x)
            w["e"][t, rows, :] = pgp - wt * w["ds"][rows, :]
        blt = bl2[:, at]
        for c in range(CH):
            red = jnp.sum(jnp.concatenate(halves[c], axis=0) * rr[c:c + 1, :], axis=1, keepdims=True)
            blt = jnp.where(lanes64 == base + c, red, blt)
        bl2[:, at] = blt
        slot = lax.rem(t, 2)
        for c in range(CH):
            w["br8"][slot, c * 8:c * 8 + 8, :] = br[c]
        tot = w["br8"][slot, pl.ds(0, 8, stride=8), :]
        for z in range(1, 8):
            tot = tot + w["br8"][slot, pl.ds(z, 8, stride=8), :]
        kro[2 * chip + lax.rem(t // 2, 2), place + (t // 4) * 4 + lax.rem(t, 2), 8:16, :] = tot

    ev = w["e"][...].reshape(16 * I, J)
    hi = ev.astype(BF16)
    lo = (ev - hi.astype(F32)).astype(BF16)
    kt = w["k2"][at, :]
    bqw = dot(jnp.concatenate([hi, lo], axis=1), jnp.concatenate([kt, kt], axis=1), NT)
    tot = jnp.zeros((I, 128), F32)
    lane2 = lax.broadcasted_iota(jnp.int32, (I, 128), 1)
    for t in range(16):
        tot = jnp.where((lane2 >> 3) == t, bqw[t * I:(t + 1) * I, :], tot)
    bq2[:, at] = f * tot
    sub_r = lax.broadcasted_iota(jnp.int32, (32, 256), 0)
    sub_c = lax.broadcasted_iota(jnp.int32, (32, 256), 1)
    keep = jnp.where((sub_r >> 3) == (sub_c >> 6), 1.0, 0.0).astype(BF16)
    for u in range(4):
        qrow = w["qt"][pl.ds(pl.multiple_of(n * 128 + u * 32, 32), 32), :]
        lhs = jnp.concatenate([qrow, qrow], axis=1) * keep
        part = dot(jnp.concatenate([lhs, lhs], axis=1), jnp.concatenate([hi[u * 256:u * 256 + 256], lo[u * 256:u * 256 + 256]], axis=0))
        part = f * part
        for core in range(2):
            for a in range(2):
                first = (core * 2 + a) * 8
                kro[2 * chip + core, place + u * 4 + a, 0:8, :] = part[first:first + 8]


def greet(groups):
    barrier = pltpu.get_barrier_semaphore()
    for n, peer in groups:
        @pl.loop(1, n)
        def _(s):
            pl.semaphore_signal(barrier, inc=1, device_id=peer(s), device_id_type=MESH)


class Trade:
    def __init__(self, n, peer, src, dst, send_sem, recv_sem):
        self.n, self.peer, self.src, self.dst, self.send_sem, self.recv_sem = n, peer, src, dst, send_sem, recv_sem

    def copy(self, s):
        return pltpu.make_async_remote_copy(
            src_ref=self.src(s), dst_ref=self.dst, send_sem=self.send_sem.at[s], recv_sem=self.recv_sem.at[s],
            device_id=self.peer(s), device_id_type=MESH)

    def start(self):
        @pl.loop(1, self.n)
        def _(s):
            self.copy(s).start()

    def finish(self):
        @pl.loop(1, self.n)
        def _(s):
            self.copy(s).wait_recv()

    def drain(self):
        @pl.loop(1, self.n)
        def _(s):
            self.copy(s).wait_send()


def lane_of(i, z):
    return z * 256 + (i % 2) * 128


def to_pairs(wide, stage, count, rows, first=0):
    for i in range(32):
        for z in range(2):
            at = lane_of(i, z)
            piece = wide[z, pl.ds(i, count, stride=32), :]
            if count % 16:
                piece = jnp.concatenate([piece, jnp.zeros((16 - count % 16, 128), F32)], axis=0)
            stage[i // 2, first:first + rows, at:at + 128] = piece.astype(BF16)


def from_pairs(recv, lo, hi, wide, offset, stride):
    for i in range(32):
        for z in range(2):
            at = lane_of(i, z)
            wide[z, pl.ds(offset + i, hi - lo, stride=stride), :] = recv[i // 2, lo:hi, at:at + 128].astype(F32)


def layer(names, x, u, wq, wk, wl, wr, wf, allowance, fac, grads, gq, gk, gl, gr, go, *scratch):
    w = dict(zip(names, scratch))
    me, row = lax.axis_index("head"), lax.axis_index("row")
    core = lax.rem(me, 2)
    x_hi, x_lo, y_lo = lax.rem(row // 2, 2), lax.rem(row, 2), row // 4
    slot = (me // 2) * 2 + x_hi
    part = y_lo * 4 + x_lo * 2 + core
    block = part // 2

    def head_peer(s):
        return {"head": lax.rem(me + s, HEADS), "row": row}

    def row_peer(s):
        return {"head": me, "row": lax.rem(row + s, ROWS)}

    def slot_at(s):
        return lax.rem(slot // 4 + s // 4, 4) * 4 + lax.rem(slot + s, 4)

    def slot_peer(s):
        to = slot_at(s)
        return {"head": (to // 2) * 2 + core, "row": y_lo * 4 + lax.rem(to, 2) * 2 + x_lo}

    def part_peer(s):
        to = lax.rem(part + s, 8)
        return {"head": (me // 2) * 2 + lax.rem(to, 2), "row": (to // 4) * 4 + x_hi * 2 + lax.rem(to // 2, 2)}

    partner = {"head": me + 1 - 2 * core, "row": row}
    hs, rs, ps = w["hs"], w["rs"], w["ps"]

    def over(n, size, peer, src, dst):
        sems = hs if size == HEADS else rs
        return Trade(size, peer, src, dst, sems.at[2 * n], sems.at[2 * n + 1])

    def to_partner(n, src, dst):
        return pltpu.make_async_remote_copy(src_ref=src, dst_ref=dst, send_sem=ps.at[0, n], recv_sem=ps.at[1, n],
                                            device_id=partner, device_id_type=MESH)

    def head_at(s):
        return lax.rem(me + s, HEADS)

    greet([(HEADS, head_peer), (ROWS, row_peer), (HEADS, slot_peer), (8, part_peer)])
    wself, wall, wide = w["wself"], w["wall"], w["wide"]
    f0 = jnp.full((8, 128), fac[0], F32)
    f1 = f0 - f0.astype(BF16).astype(F32)
    f2 = f1 - f1.astype(BF16).astype(F32)
    tile = lax.broadcasted_iota(jnp.int32, (8, 128), 0)
    factor = jnp.where(tile == 0, f0, jnp.where(tile == 1, f1, jnp.where(tile == 2, f2, 0.0)))
    wself[...] = jnp.concatenate([wk[...], wr[...], wq[...], wl[...], wf[...], factor.astype(BF16)], axis=0)
    for z in range(2):
        wide[z, 0:256, :] = x[:, :, z * 128:z * 128 + 128].reshape(256, 128).astype(F32)
        wide[z, 256:512, :] = u[:, :, z * 128:z * 128 + 128].reshape(256, 128).astype(F32)
    to_pairs(wide, w["stage1"], 16, 16)
    pl.semaphore_wait(pltpu.get_barrier_semaphore(), 2 * HEADS + ROWS + 8 - 4)
    inputs = over(0, HEADS, head_peer, lambda s: w["stage1"].at[head_at(s)], w["recv1"].at[me])
    weights = over(1, HEADS, head_peer, lambda s: wself, wall.at[me])
    weights.start()
    inputs.start()
    w["recv1"][me] = w["stage1"][me]
    wall[me] = wself[...]
    constants(w)
    node = row * 32 + lax.broadcasted_iota(jnp.int32, (32, 128), 0)
    column = lax.broadcasted_iota(jnp.int32, (32, 128), 1)
    for z in range(2):
        valid = (allowance[:, z * 128:z * 128 + 128] == 1) | (node == column + z * 128)
        w["mask"][z] = jnp.where(valid, 0.0, -1e30)
    bias = jnp.concatenate([w["mask"][z, pl.ds(2 * me + a, 1), :] for z in range(2) for a in range(2)], axis=1)
    bias = jnp.broadcast_to(bias, (8, 512))
    inputs.finish()
    both = w["recv1"][...].astype(F32)
    w["xp"][...] = both[:, 0:8].reshape(128, 512).astype(BF16)
    w["up"][...] = both[:, 8:16].reshape(128, 512).astype(BF16)
    weights.finish()

    stage2, recv2, kr = w["stage2"], w["recv2"], w["kr"]
    mapped = over(2, HEADS, slot_peer, lambda s: stage2.at[slot_at(s)], recv2.at[slot])
    for first in range(0, HEADS, 4):
        peers = [slot_at(first + a) for a in range(4)]
        of_x = dot(jnp.concatenate([wall[p, 0:32] for p in peers], axis=0), w["xp"][...]).astype(BF16)
        of_u = dot(jnp.concatenate([wall[p, 32:48] for p in peers], axis=0), w["up"][...])
        for a, p in enumerate(peers):
            stage2[p, 0:32] = of_x[a * 32:a * 32 + 32]
            stage2[p, 32:48] = jnp.concatenate([of_u[a * 16:a * 16 + 8], bias], axis=0).astype(BF16)
            if first + a:
                mapped.copy(first + a).start()
            else:
                recv2[slot] = stage2[slot]

    def kr_copy(g, s):
        four = pl.ds(lax.rem(slot // 4 + 4 - g, 4) * 4, 4)
        to = lax.rem(part + s, 8)
        return pltpu.make_async_remote_copy(
            src_ref=recv2.at[four, pl.ds(0, 16), pl.ds(pl.multiple_of(lax.rem(to, 2) * 256, 128), 256)], dst_ref=kr.at[part, four],
            send_sem=w["ks"].at[0, g, s], recv_sem=w["ks"].at[1, g, s], device_id=part_peer(s), device_id_type=MESH)

    def near_copy(g):
        four = pl.ds(lax.rem(slot // 4 + 4 - g, 4) * 4, 4)
        return to_partner(g, recv2.at[four, pl.ds(16, 32)], w["near"].at[four])

    @pl.loop(0, 4)
    def _(g):
        @pl.loop(0, 4)
        def _(a):
            @pl.when(g * 4 + a > 0)
            def _():
                mapped.copy(g * 4 + a).wait_recv()

        near_copy(g).start()

        @pl.loop(1, 8)
        def _(s):
            kr_copy(g, s).start()

    near = w["near"]
    wide2 = w["wide2"]
    own = pl.multiple_of(core * 32, 32)
    from_pairs(recv2, 16, 48, wide2, core * 32, I)

    @pl.loop(0, 4)
    def _(g):
        near_copy(g).wait_recv()

    from_pairs(near, 0, 32, wide2, 32 - core * 32, I)
    prepare(wide2, w)

    f = jnp.sum(wall[slot, 32:48].astype(F32)[8:16], axis=0, keepdims=True)

    def groups(chip):
        for hi in range(2):
            for y in range(2):
                yield 2 * ((chip // 2) * 4 + hi * 2 + lax.rem(chip, 2)) + y, y * 8 + hi

    @pl.loop(0, 4)
    def _(k):
        chip = lax.rem(block + 4 - k, 4)
        for c in range(2):
            @pl.when(2 * chip + c != part)
            def _():
                @pl.loop(0, 4)
                def _(g):
                    kr_copy(g, lax.rem(part + 8 - 2 * chip - c, 8)).wait_recv()

            @pl.when(2 * chip + c == part)
            def _():
                kr[part] = recv2[:, 0:16, pl.ds(pl.multiple_of(core * 256, 128), 256)]

        for n, first in groups(chip):
            for t in range(16):
                at = (first + (t // 4) * 2)
                tile = kr[2 * chip + (t // 2) % 2, at, :, (t % 2) * 128:(t % 2) * 128 + 128].astype(F32)
                rows = pl.ds(pl.multiple_of(n * 128 + t * 8, 8), 8)
                w["kf"][rows, :] = tile[0:8]
                w["rf"][rows, :] = tile[8:16]
            scores(n, w)

    forward(wide2, core, f, w["mx"], w)
    mine, other = pl.ds(own, 32), pl.ds(pl.multiple_of(32 - core * 32, 32), 32)
    mixed_out = to_partner(4, w["mx"].at[:, other], w["mixin"])
    mixed_out.start()
    ql2, qlin, kro, krin = w["ql2"], w["qlin"], w["kro"], w["krin"]
    pairs_out = over(0, 8, part_peer, lambda s: kro.at[lax.rem(part + s, 8)], krin.at[part])
    mixed = over(3, HEADS, slot_peer, lambda s: w["stagem"].at[slot_at(s)], w["recvm"].at[slot])

    def group_out(n):
        lanes = pl.ds(pl.multiple_of(n * 128, 128), 128)
        return to_partner(5 + n, ql2.at[:, other, lanes], qlin.at[:, :, lanes])

    @pl.loop(0, 4)
    def _(k):
        chip = lax.rem(block + 1 + k, 4)

        @pl.loop(0, 4)
        def _(j):
            n = 2 * ((chip // 2) * 4 + (j // 2) * 2 + lax.rem(chip, 2)) + lax.rem(j, 2)
            backward(n, chip, lax.rem(j, 2) * 16 + (j // 2) * 2, f, ql2.at[0], ql2.at[1], kro, w)
            group_out(n).start()

        for c in range(2):
            to = 2 * chip + c

            @pl.when(to != part)
            def _():
                pairs_out.copy(lax.rem(to + 8 - part, 8)).start()

            @pl.when(to == part)
            def _():
                krin[part] = kro[part]

        @pl.when(k == 0)
        def _():
            mixed_out.wait()
            mixf = w["mixf"]
            for c in range(CH):
                mixf[core, c * 32:c * 32 + 32, :] = w["mx"][c, mine, :].astype(F32)
                mixf[1 - core, c * 32:c * 32 + 32, :] = w["mixin"][c].astype(F32)
            to_pairs(mixf, w["stagem"], 8, 16)
            mixed.start()
            w["recvm"][slot] = w["stagem"][slot]

    @pl.loop(0, 16)
    def _(n):
        group_out(n).wait()

    total = (ql2[:, mine, :] + qlin[...]).astype(BF16).reshape(64, 2048)
    for h in range(2):
        plain = dot(total[:, h * 1024:h * 1024 + 1024], w["pt"][...])
        for c in range(CH):
            wide[h, c * 32:c * 32 + 32, :] = plain[0:32, c * 128:c * 128 + 128]
            wide[h, 256 + c * 32:288 + c * 32, :] = plain[32:64, c * 128:c * 128 + 128]
    to_pairs(wide, w["stage3"], 16, 16, 16)
    mixed.finish()
    gu = dot(w["recvm"][...].reshape(256, 512), w["up"][...], NT).reshape(16, 16, 128)
    gws = w["gws"]
    gws[:, 32:40, :] = gu[:, 0:8]
    pairs_out.finish()
    for j in range(2):
        total = krin[j] + krin[2 + j] + krin[4 + j] + krin[6 + j]
        total = total.astype(BF16).reshape(16, 2, 16, 128)
        for a in range(2):
            w["stage3"][:, 0:16, j * 256 + a * 128:j * 256 + a * 128 + 128] = total[:, a]
    backs = over(4, HEADS, slot_peer, lambda s: w["stage3"].at[slot_at(s)], w["recv3"].at[slot])
    backs.start()
    w["recv3"][slot] = w["stage3"][slot]
    backs.finish()

    every = w["recv3"][...].reshape(512, 512)
    gws[:, 0:32, :] = dot(every, w["xp"][...], NT).reshape(16, 32, 128)
    sums = over(5, HEADS, head_peer, lambda s: gws.at[head_at(s)], w["gwin"].at[me])
    sums.start()
    w["gwin"][me] = gws[me]
    image = dot(wall[:, 0:32, :].reshape(512, 128), every, TN).reshape(16, 8, 512)
    w["stage4"][...] = jnp.concatenate([image, jnp.zeros((16, 8, 512), F32)], axis=1).astype(BF16)
    images = over(6, HEADS, head_peer, lambda s: w["stage4"].at[head_at(s)], w["recv4"].at[me])
    images.start()
    w["recv4"][me] = w["stage4"][me]
    sums.finish()
    total = w["gwin"][0]
    for p in range(1, HEADS):
        total = total + w["gwin"][p]
    w["part"][...] = total
    last = over(1, ROWS, row_peer, lambda s: w["part"], w["gwrow"].at[row])
    last.start()
    w["gwrow"][row] = total
    images.finish()
    from_pairs(w["recv4"], 0, 16, wide, 0, 32)
    for z in range(2):
        grads[:, :, z * 128:z * 128 + 128] = wide[z, 0:256, :].astype(BF16).reshape(8, 32, 128)
    last.finish()
    total = w["gwrow"][0]
    for p in range(1, ROWS):
        total = total + w["gwrow"][p]
    total = total * (1.0 / 256.0)
    for n, out in enumerate((gk, gr, gq, gl, go)):
        out[...] = total[8 * n:8 * n + 8]
    for trade in (inputs, weights, mapped, pairs_out, mixed, backs, sums, images, last):
        trade.drain()

    @pl.loop(0, 4)
    def _(g):
        near_copy(g).wait_send()

        @pl.loop(1, 8)
        def _(s):
            kr_copy(g, s).wait_send()


def layer_scratch():
    vmem, dma = pltpu.VMEM, pltpu.SemaphoreType.DMA
    return dict(
        core_scratch(),
        wide=vmem((2, 1024, 128), F32), wide2=vmem((2, 2048, 128), F32), wself=vmem((48, 128), BF16), wall=vmem((16, 48, 128), BF16),
        stage1=vmem((16, 16, 512), BF16), recv1=vmem((16, 16, 512), BF16), xp=vmem((128, 512), BF16), up=vmem((128, 512), BF16),
        stage2=vmem((16, 48, 512), BF16), recv2=vmem((16, 48, 512), BF16), near=vmem((16, 32, 512), BF16), mask=vmem((2, 32, 128), F32),
        kr=vmem((8, 16, 16, 256), BF16),
        ql2=vmem((2, 64, 2048), F32), qlin=vmem((2, 32, 2048), F32), kro=vmem((8, 32, 16, 128), F32), krin=vmem((8, 32, 16, 128), F32),
        mx=vmem((8, 64, 128), BF16), mixin=vmem((8, 32, 128), BF16), mixf=vmem((2, 256, 128), F32),
        stagem=vmem((16, 16, 512), BF16), recvm=vmem((16, 16, 512), BF16),
        stage3=vmem((16, 32, 512), BF16), recv3=vmem((16, 32, 512), BF16), stage4=vmem((16, 16, 512), BF16), recv4=vmem((16, 16, 512), BF16),
        gws=vmem((16, 40, 128), F32), gwin=vmem((16, 40, 128), F32), part=vmem((40, 128), F32), gwrow=vmem((8, 40, 128), F32),
        hs=dma((14, 16)), rs=dma((4, 8)), ps=dma((2, 21)), ks=dma((2, 4, 8)),
    )


def local(x, allowance, asking, lookup, first_content, second_content, final, scaling, upstream):
    vm = pl.BlockSpec(memory_space=pltpu.VMEM)
    names = layer_scratch()
    grads, gq, gk, gl, gr, go = pl.pallas_call(
        functools.partial(layer, list(names)),
        out_shape=[jax.ShapeDtypeStruct((8, 32, 256), BF16)] + [jax.ShapeDtypeStruct((8, 128), F32)] * 5,
        in_specs=[vm] * 8 + [pl.BlockSpec(memory_space=pltpu.SMEM)], out_specs=[vm] * 6,
        scratch_shapes=list(names.values()),
        compiler_params=pltpu.CompilerParams(collective_id=0, has_side_effects=True, vmem_limit_bytes=56 * 2 ** 20),
        name="layer",
    )(x, upstream, asking.T, lookup.T, first_content.T, second_content.T, final, allowance, scaling)
    return grads, gq.T, gk.T, gl.T, gr.T, go


def solution(mesh):
    pairs, columns = P("head", "row", None), P(None, "head")
    placed = (pairs, P("row", None), columns, columns, columns, columns, P("head", None), P("head"), pairs)
    return jax.shard_map(
        local, mesh=mesh, in_specs=placed,
        out_specs=(pairs, columns, columns, columns, columns, P("head", None)), check_vma=False,
    )
```

```python
import functools

import jax
import jax.numpy as jnp
from jax import lax
from jax.experimental import pallas as pl
from jax.experimental.pallas import tpu as pltpu
from jax.sharding import PartitionSpec as P

F32, BF16 = jnp.float32, jnp.bfloat16
MESH = pl.DeviceIdType.MESH
NT = (((1,), (1,)), ((), ()))
NN = (((1,), (0,)), ((), ()))
TN = (((0,), (0,)), ((), ()))
CH, I, L, J = 8, 64, 256, 128
HEADS, ROWS = 16, 8


def dot(a, b, dims=NN):
    return lax.dot_general(a, b, dims, preferred_element_type=F32)


def core_scratch():
    return dict(
        pt=pltpu.VMEM((1024, 1024), BF16),
        q2=pltpu.VMEM((I, 2048), BF16), b2=pltpu.VMEM((I, 2048), BF16),
        qt=pltpu.VMEM((2048, 128), BF16), kf=pltpu.VMEM((2048, J), F32), rf=pltpu.VMEM((2048, J), F32),
        k2=pltpu.VMEM((2048, J), BF16), mt=pltpu.VMEM((16, 256), BF16), wc=pltpu.VMEM((128, 1024), BF16), lb16=pltpu.VMEM((I, 2048), BF16),
        s=pltpu.VMEM((L, I, J), F32), m=pltpu.VMEM((I, J), F32), gs=pltpu.VMEM((CH, I, J), F32), ds=pltpu.VMEM((I, J), F32),

        e=pltpu.VMEM((16, I, J), F32), br8=pltpu.VMEM((2, 64, J), F32),
    )


def permutation(pt):
    @pl.loop(0, 8)
    def _(n):
        a = lax.broadcasted_iota(jnp.int32, (128, 1024), 0) + n * 128
        b = lax.broadcasted_iota(jnp.int32, (128, 1024), 1)
        hit = ((a >> 3) == (b & 127)) & ((a & 7) == (b >> 7))
        pt[pl.ds(pl.multiple_of(n * 128, 128), 128), :] = jnp.where(hit, 1.0, 0.0).astype(BF16)


def constants(w):
    permutation(w["pt"])
    row = lax.broadcasted_iota(jnp.int32, (16, 256), 0)
    lane = lax.broadcasted_iota(jnp.int32, (16, 256), 1)
    w["mt"][...] = jnp.where(((lane & 127) >> 3) == row, 1.0, 0.0).astype(BF16)
    ra = lax.broadcasted_iota(jnp.int32, (128, 1024), 0)
    rb_ = lax.broadcasted_iota(jnp.int32, (128, 1024), 1)
    w["wc"][...] = jnp.where((ra & 7) == (rb_ >> 7), 1.0, 0.0).astype(BF16)


def prepare(wide, w):
    pt = w["pt"]
    for half in range(2):
        out = slice(half * 1024, half * 1024 + 1024)
        qcat = jnp.concatenate([wide[half, c * I:c * I + I, :] for c in range(CH)], axis=1).astype(BF16)
        lcat = jnp.concatenate([wide[half, c * I:c * I + I, :] for c in range(CH, 2 * CH)], axis=1).astype(BF16)
        bcat = jnp.concatenate([wide[half, 24 * I:25 * I, :].astype(BF16), jnp.zeros((I, 896), BF16)], axis=1)
        got = dot(jnp.concatenate([qcat, lcat, bcat], axis=0), pt[...], NT)
        w["q2"][:, out] = got[:I].astype(BF16)
        w["lb16"][:, out] = got[I:2 * I].astype(BF16)
        w["b2"][:, out] = got[2 * I:].astype(BF16)
        w["qt"][out, :] = dot(pt[...], jnp.concatenate([qcat, qcat], axis=0), NT).astype(BF16)
    w["m"][...] = jnp.full((I, J), -3e38, F32)


def scores(n, w):
    at = pl.ds(pl.multiple_of(n * 128, 128), 128)
    k2 = w["kf"][at, :].astype(BF16)
    w["k2"][at, :] = k2
    qb = jnp.concatenate([w["q2"][:, at], w["b2"][:, at]], axis=1)
    kk = jnp.concatenate([k2, jnp.ones((128, J), BF16)], axis=0)
    lhs = jnp.concatenate([qb * w["mt"][t:t + 1, :] for t in range(16)], axis=0)
    raw = dot(lhs, kk).reshape(16, I, J)
    top = w["m"][...]
    for t in range(16):
        top = jnp.maximum(top, raw[t])
    w["m"][...] = top
    w["s"][pl.ds(n * 16, 16)] = raw


def forward(wide, mine, f, mixed, w):
    @pl.loop(0, 2)
    def _(ip):
        rows = pl.ds(pl.multiple_of(ip * 32, 32), 32)
        top = w["m"][rows, :]

        def step(n, carry):
            total, acc = carry
            acc = list(acc)
            tile = w["lb16"][rows, pl.ds(pl.multiple_of(n * 128, 128), 128)]
            lhs = jnp.concatenate([tile * w["mt"][t:t + 1, :128] for t in range(16)], axis=0)
            rg = w["rf"][pl.ds(pl.multiple_of(n * 128, 128), 128), :].astype(BF16)
            both = dot(lhs, jnp.concatenate([rg] * CH, axis=1) * w["wc"][...])
            for t in range(16):
                lv = n * 16 + t
                wt = jnp.exp(f * (w["s"][lv, rows, :] - top))
                w["s"][lv, rows, :] = wt
                total = total + wt
                for c in range(CH):
                    acc[c] = acc[c] + wt * both[t * 32:t * 32 + 32, c * 128:c * 128 + 128]
            return total, tuple(acc)

        zero = jnp.zeros((32, J), F32)
        total, acc = lax.fori_loop(0, 16, step, (zero, (zero,) * CH), unroll=4)
        inv = 1.0 / total
        delta = zero
        for c in range(CH):
            gc = wide[mine, pl.ds(pl.multiple_of((16 + c) * I + ip * 32, 32), 32), :]
            mc = acc[c] * inv
            mixed[c, rows, :] = mc.astype(BF16)
            delta = delta + gc * mc
            w["gs"][c, rows, :] = gc * inv
        w["ds"][rows, :] = delta * inv


def backward(n, chip, place, f, bq2, bl2, kro, w):
    at = pl.ds(pl.multiple_of(n * 128, 128), 128)
    bl2[:, at] = jnp.zeros((I, 128), F32)

    @pl.loop(0, 16, unroll=4)
    def _(t):
        lv = n * 16 + t
        lanes64 = lax.broadcasted_iota(jnp.int32, (I, 128), 1)
        pick = jnp.where((lanes64 >> 3) == t, 1.0, 0.0).astype(BF16)
        spread = dot(w["lb16"][:, at] * pick, w["wc"][...])
        rr = w["rf"][pl.ds(pl.multiple_of(lv * 8, 8), 8), :]
        rb = [jnp.broadcast_to(rr[c:c + 1, :], (8, J)) for c in range(CH)]
        br = [jnp.zeros((8, J), F32) for c in range(CH)]
        base = t * 8
        lanes8 = lax.broadcasted_iota(jnp.int32, (8, 128), 1)
        for it in range(8):
            rows = slice(it * 8, it * 8 + 8)
            wt = w["s"][lv, rows, :]
            blt = bl2[rows, at]
            pgp = None
            for c in range(CH):
                x = wt * w["gs"][c, rows, :]
                xl = x * spread[rows, c * 128:c * 128 + 128]
                br[c] = br[c] + xl
                term = xl * rb[c]
                pgp = term if pgp is None else pgp + term
                red = jnp.sum(x * rb[c], axis=1, keepdims=True)
                blt = jnp.where(lanes8 == base + c, red, blt)
            w["e"][t, rows, :] = pgp - wt * w["ds"][rows, :]
            bl2[rows, at] = blt
        slot = lax.rem(t, 2)
        for c in range(CH):
            w["br8"][slot, c * 8:c * 8 + 8, :] = br[c]
        tot = w["br8"][slot, pl.ds(0, 8, stride=8), :]
        for z in range(1, 8):
            tot = tot + w["br8"][slot, pl.ds(z, 8, stride=8), :]
        kro[2 * chip + lax.rem(t // 2, 2), place + (t // 4) * 4 + lax.rem(t, 2), 8:16, :] = tot

    ev = w["e"][...].reshape(16 * I, J)
    hi = ev.astype(BF16)
    lo = (ev - hi.astype(F32)).astype(BF16)
    kt = w["k2"][at, :]
    bqw = dot(jnp.concatenate([hi, lo], axis=1), jnp.concatenate([kt, kt], axis=1), NT)
    tot = jnp.zeros((I, 128), F32)
    lane2 = lax.broadcasted_iota(jnp.int32, (I, 128), 1)
    for t in range(16):
        tot = jnp.where((lane2 >> 3) == t, bqw[t * I:(t + 1) * I, :], tot)
    bq2[:, at] = f * tot
    sub_r = lax.broadcasted_iota(jnp.int32, (32, 256), 0)
    sub_c = lax.broadcasted_iota(jnp.int32, (32, 256), 1)
    keep = jnp.where((sub_r >> 3) == (sub_c >> 6), 1.0, 0.0).astype(BF16)
    for u in range(4):
        qrow = w["qt"][pl.ds(pl.multiple_of(n * 128 + u * 32, 32), 32), :]
        lhs = jnp.concatenate([qrow, qrow], axis=1) * keep
        part = dot(jnp.concatenate([lhs, lhs], axis=1), jnp.concatenate([hi[u * 256:u * 256 + 256], lo[u * 256:u * 256 + 256]], axis=0))
        part = f * part
        for core in range(2):
            for a in range(2):
                first = (core * 2 + a) * 8
                kro[2 * chip + core, place + u * 4 + a, 0:8, :] = part[first:first + 8]


def greet(groups):
    barrier = pltpu.get_barrier_semaphore()
    for n, peer in groups:
        @pl.loop(1, n)
        def _(s):
            pl.semaphore_signal(barrier, inc=1, device_id=peer(s), device_id_type=MESH)


class Trade:
    def __init__(self, n, peer, src, dst, send_sem, recv_sem):
        self.n, self.peer, self.src, self.dst, self.send_sem, self.recv_sem = n, peer, src, dst, send_sem, recv_sem

    def copy(self, s):
        return pltpu.make_async_remote_copy(
            src_ref=self.src(s), dst_ref=self.dst, send_sem=self.send_sem.at[s], recv_sem=self.recv_sem.at[s],
            device_id=self.peer(s), device_id_type=MESH)

    def start(self):
        @pl.loop(1, self.n)
        def _(s):
            self.copy(s).start()

    def finish(self):
        @pl.loop(1, self.n)
        def _(s):
            self.copy(s).wait_recv()

    def drain(self):
        @pl.loop(1, self.n)
        def _(s):
            self.copy(s).wait_send()


def lane_of(i, z):
    return z * 256 + (i % 2) * 128


def to_pairs(wide, stage, count, rows, first=0):
    for i in range(32):
        for z in range(2):
            at = lane_of(i, z)
            piece = wide[z, pl.ds(i, count, stride=32), :]
            if count % 16:
                piece = jnp.concatenate([piece, jnp.zeros((16 - count % 16, 128), F32)], axis=0)
            stage[i // 2, first:first + rows, at:at + 128] = piece.astype(BF16)


def from_pairs(recv, lo, hi, wide, offset, stride, first=0, count=16):
    for i in range(2 * count):
        for z in range(2):
            at = lane_of(i, z)
            rows = pl.ds(offset + first * 2 + i, hi - lo, stride=stride)
            wide[z, rows, :] = recv[first + i // 2, lo:hi, at:at + 128].astype(F32)


def layer(names, x, u, wq, wk, wl, wr, wf, allowance, fac, grads, gw, *scratch):
    w = dict(zip(names, scratch))
    me, row = lax.axis_index("head"), lax.axis_index("row")
    core = lax.rem(me, 2)
    x_hi, x_lo, y_lo = lax.rem(row // 2, 2), lax.rem(row, 2), row // 4
    slot = (me // 2) * 2 + x_hi
    part = y_lo * 4 + x_lo * 2 + core
    block = part // 2

    def head_peer(s):
        return {"head": lax.rem(me + s, HEADS), "row": row}

    def row_peer(s):
        return {"head": me, "row": lax.rem(row + s, ROWS)}

    def slot_at(s):
        return lax.rem(slot // 4 + s // 4, 4) * 4 + lax.rem(slot + s, 4)

    def slot_peer(s):
        to = slot_at(s)
        return {"head": (to // 2) * 2 + core, "row": y_lo * 4 + lax.rem(to, 2) * 2 + x_lo}

    def part_peer(s):
        to = lax.rem(part + s, 8)
        return {"head": (me // 2) * 2 + lax.rem(to, 2), "row": (to // 4) * 4 + x_hi * 2 + lax.rem(to // 2, 2)}

    partner = {"head": me + 1 - 2 * core, "row": row}
    hs, rs, ps = w["hs"], w["rs"], w["ps"]

    def over(n, size, peer, src, dst):
        sems = hs if size == HEADS else rs
        return Trade(size, peer, src, dst, sems.at[2 * n], sems.at[2 * n + 1])

    def to_partner(n, src, dst):
        return pltpu.make_async_remote_copy(src_ref=src, dst_ref=dst, send_sem=ps.at[0, n], recv_sem=ps.at[1, n],
                                            device_id=partner, device_id_type=MESH)

    def head_at(s):
        return lax.rem(me + s, HEADS)

    greet([(HEADS, head_peer), (ROWS, row_peer), (HEADS, slot_peer), (8, part_peer)])
    wself, wall, wide = w["wself"], w["wall"], w["wide"]
    f0 = jnp.full((8, 128), fac[0], F32)
    f1 = f0 - f0.astype(BF16).astype(F32)
    f2 = f1 - f1.astype(BF16).astype(F32)
    tile = lax.broadcasted_iota(jnp.int32, (8, 128), 0)
    factor = jnp.where(tile == 0, f0, jnp.where(tile == 1, f1, jnp.where(tile == 2, f2, 0.0)))
    wself[...] = jnp.concatenate([wk[...], wr[...], wq[...], wl[...], wf[...], factor.astype(BF16)], axis=0)
    for z in range(2):
        wide[z, 0:256, :] = x[:, :, z * 128:z * 128 + 128].reshape(256, 128).astype(F32)
        wide[z, 256:512, :] = u[:, :, z * 128:z * 128 + 128].reshape(256, 128).astype(F32)
    to_pairs(wide, w["stage1"], 16, 16)
    pl.semaphore_wait(pltpu.get_barrier_semaphore(), 2 * HEADS + ROWS + 8 - 4)
    inputs = over(0, HEADS, head_peer, lambda s: w["stage1"].at[head_at(s)], w["recv1"].at[me])
    weights = over(1, HEADS, head_peer, lambda s: wself, wall.at[me])
    weights.start()
    inputs.start()
    w["recv1"][me] = w["stage1"][me]
    wall[me] = wself[...]
    constants(w)
    node = row * 32 + lax.broadcasted_iota(jnp.int32, (32, 128), 0)
    column = lax.broadcasted_iota(jnp.int32, (32, 128), 1)
    for z in range(2):
        valid = (allowance[:, z * 128:z * 128 + 128] == 1) | (node == column + z * 128)
        w["mask"][z] = jnp.where(valid, 0.0, -1e30)
    bias = jnp.concatenate([w["mask"][z, pl.ds(2 * me + a, 1), :] for z in range(2) for a in range(2)], axis=1)
    bias = jnp.broadcast_to(bias, (8, 512))
    inputs.finish()
    both = w["recv1"][...].astype(F32)
    w["xp"][...] = both[:, 0:8].reshape(128, 512).astype(BF16)
    w["up"][...] = both[:, 8:16].reshape(128, 512).astype(BF16)
    weights.finish()

    stage2, recv2, kr = w["stage2"], w["recv2"], w["kr"]
    mapped = over(2, HEADS, slot_peer, lambda s: stage2.at[slot_at(s)], recv2.at[slot])
    for first in range(0, HEADS, 4):
        peers = [slot_at(first + a) for a in range(4)]
        of_x = dot(jnp.concatenate([wall[p, 0:32] for p in peers], axis=0), w["xp"][...]).astype(BF16)
        of_u = dot(jnp.concatenate([wall[p, 32:48] for p in peers], axis=0), w["up"][...])
        for a, p in enumerate(peers):
            stage2[p, 0:32] = of_x[a * 32:a * 32 + 32]
            stage2[p, 32:48] = jnp.concatenate([of_u[a * 16:a * 16 + 8], bias], axis=0).astype(BF16)
            if first + a:
                mapped.copy(first + a).start()
            else:
                recv2[slot] = stage2[slot]

    near, wide2 = w["near"], w["wide2"]

    def four(g):
        return lax.rem(slot // 4 + 4 - g, 4) * 4

    def kr_copy(g, s):
        some = pl.ds(four(g), 4)
        to = lax.rem(part + s, 8)
        return pltpu.make_async_remote_copy(
            src_ref=recv2.at[some, pl.ds(0, 16), pl.ds(pl.multiple_of(lax.rem(to, 2) * 256, 128), 256)], dst_ref=kr.at[part, some],
            send_sem=w["ks"].at[0, g, s], recv_sem=w["ks"].at[1, g, s], device_id=part_peer(s), device_id_type=MESH)

    def near_copy(g):
        some = pl.ds(four(g), 4)
        return to_partner(g, recv2.at[some, pl.ds(16, 32)], near.at[some])

    def unpack_near(g):
        near_copy(g).wait_recv()
        from_pairs(near, 0, 32, wide2, 32 - core * 32, I, four(g), 4)

    @pl.loop(0, 4)
    def _(g):
        @pl.loop(0, 4)
        def _(a):
            @pl.when(g * 4 + a > 0)
            def _():
                mapped.copy(g * 4 + a).wait_recv()

        near_copy(g).start()

        @pl.loop(1, 8)
        def _(s):
            kr_copy(g, s).start()

        from_pairs(recv2, 16, 48, wide2, core * 32, I, four(g), 4)

        @pl.when(g > 0)
        def _():
            unpack_near(g - 1)

    unpack_near(3)
    own = pl.multiple_of(core * 32, 32)
    prepare(wide2, w)

    f = jnp.sum(wall[slot, 32:48].astype(F32)[8:16], axis=0, keepdims=True)

    def groups(chip):
        for hi in range(2):
            for y in range(2):
                yield 2 * ((chip // 2) * 4 + hi * 2 + lax.rem(chip, 2)) + y, y * 8 + hi

    @pl.loop(0, 4)
    def _(k):
        chip = lax.rem(block + 4 - k, 4)
        for c in range(2):
            @pl.when(2 * chip + c != part)
            def _():
                @pl.loop(0, 4)
                def _(g):
                    kr_copy(g, lax.rem(part + 8 - 2 * chip - c, 8)).wait_recv()

            @pl.when(2 * chip + c == part)
            def _():
                kr[part] = recv2[:, 0:16, pl.ds(pl.multiple_of(core * 256, 128), 256)]

        for n, first in groups(chip):
            for t in range(16):
                at = (first + (t // 4) * 2)
                tile = kr[2 * chip + (t // 2) % 2, at, :, (t % 2) * 128:(t % 2) * 128 + 128].astype(F32)
                rows = pl.ds(pl.multiple_of(n * 128 + t * 8, 8), 8)
                w["kf"][rows, :] = tile[0:8]
                w["rf"][rows, :] = tile[8:16]
            scores(n, w)

    forward(wide2, core, f, w["mx"], w)
    mine, other = pl.ds(own, 32), pl.ds(pl.multiple_of(32 - core * 32, 32), 32)
    mixed_out = to_partner(4, w["mx"].at[:, other], w["mixin"])
    mixed_out.start()
    ql2, qlin, kro, krin = w["ql2"], w["qlin"], w["kro"], w["krin"]
    pairs_out = over(0, 8, part_peer, lambda s: kro.at[lax.rem(part + s, 8)], krin.at[part])
    mixed = over(3, HEADS, slot_peer, lambda s: w["stagem"].at[slot_at(s)], w["recvm"].at[slot])

    def group_out(n):
        lanes = pl.ds(pl.multiple_of(n * 128, 128), 128)
        return to_partner(5 + n, ql2.at[:, other, lanes], qlin.at[:, :, lanes])

    @pl.loop(0, 4)
    def _(k):
        chip = lax.rem(block + 1 + k, 4)

        @pl.loop(0, 4)
        def _(j):
            n = 2 * ((chip // 2) * 4 + (j // 2) * 2 + lax.rem(chip, 2)) + lax.rem(j, 2)
            backward(n, chip, lax.rem(j, 2) * 16 + (j // 2) * 2, f, ql2.at[0], ql2.at[1], kro, w)
            group_out(n).start()

        for c in range(2):
            to = 2 * chip + c

            @pl.when(to != part)
            def _():
                pairs_out.copy(lax.rem(to + 8 - part, 8)).start()

            @pl.when(to == part)
            def _():
                krin[part] = kro[part]

        @pl.when(k == 0)
        def _():
            mixed_out.wait()
            mixf = w["mixf"]
            for c in range(CH):
                mixf[core, c * 32:c * 32 + 32, :] = w["mx"][c, mine, :].astype(F32)
                mixf[1 - core, c * 32:c * 32 + 32, :] = w["mixin"][c].astype(F32)
            to_pairs(mixf, w["stagem"], 8, 16)
            mixed.start()
            w["recvm"][slot] = w["stagem"][slot]

    @pl.loop(0, 16)
    def _(n):
        group_out(n).wait()

    total = (ql2[:, mine, :] + qlin[...]).astype(BF16).reshape(64, 2048)
    for h in range(2):
        plain = dot(total[:, h * 1024:h * 1024 + 1024], w["pt"][...])
        for c in range(CH):
            wide[h, c * 32:c * 32 + 32, :] = plain[0:32, c * 128:c * 128 + 128]
            wide[h, 256 + c * 32:288 + c * 32, :] = plain[32:64, c * 128:c * 128 + 128]
    stage3, recv3 = w["stage3"], w["recv3"]
    to_pairs(wide, stage3.at[1], 16, 16)
    backs = [over(4 + 3 * n, HEADS, slot_peer, lambda s, n=n: stage3.at[n, slot_at(s)], recv3.at[n, slot]) for n in range(2)]
    backs[1].start()
    recv3[1, slot] = stage3[1, slot]
    mixed.finish()
    gws = w["gws"]
    gws[:, 32:40, :] = dot(w["recvm"][...].reshape(256, 512), w["up"][...], NT).reshape(16, 16, 128)[:, 0:8]
    pairs_out.finish()
    for j in range(2):
        total = krin[j] + krin[2 + j] + krin[4 + j] + krin[6 + j]
        total = total.astype(BF16).reshape(16, 2, 16, 128)
        for a in range(2):
            stage3[0, :, :, j * 256 + a * 128:j * 256 + a * 128 + 128] = total[:, a]
    backs[0].start()
    recv3[0, slot] = stage3[0, slot]

    image = None
    for n in (1, 0):
        backs[n].finish()
        every = recv3[n].reshape(256, 512)
        gws[:, 16 * n:16 * n + 16, :] = dot(every, w["xp"][...], NT).reshape(16, 16, 128)
        term = dot(wall[:, 16 * n:16 * n + 16, :].reshape(256, 128), every, TN)
        image = term if image is None else image + term
    sums = over(5, HEADS, head_peer, lambda s: gws.at[head_at(s)], w["gwin"].at[me])
    sums.start()
    w["gwin"][me] = gws[me]
    image = image.reshape(16, 8, 512)
    w["stage4"][...] = jnp.concatenate([image, jnp.zeros((16, 8, 512), F32)], axis=1).astype(BF16)
    images = over(6, HEADS, head_peer, lambda s: w["stage4"].at[head_at(s)], w["recv4"].at[me])
    images.start()
    w["recv4"][me] = w["stage4"][me]
    sums.finish()
    total = w["gwin"][0]
    for p in range(1, HEADS):
        total = total + w["gwin"][p]
    w["part"][...] = total
    last = over(1, ROWS, row_peer, lambda s: w["part"], w["gwrow"].at[row])
    last.start()
    w["gwrow"][row] = total
    images.finish()
    from_pairs(w["recv4"], 0, 16, wide, 0, 32)
    for z in range(2):
        grads[:, :, z * 128:z * 128 + 128] = wide[z, 0:256, :].astype(BF16).reshape(8, 32, 128)
    last.finish()
    total = w["gwrow"][0]
    for p in range(1, ROWS):
        total = total + w["gwrow"][p]
    gw[...] = total * (1.0 / 256.0)
    for trade in (inputs, weights, mapped, pairs_out, mixed, *backs, sums, images, last):
        trade.drain()

    @pl.loop(0, 4)
    def _(g):
        near_copy(g).wait_send()

        @pl.loop(1, 8)
        def _(s):
            kr_copy(g, s).wait_send()


def results(grads, gw, out, gq, gk, gl, gr, go):
    out[...] = grads[...]
    for n, ref in enumerate((gk, gr, gq, gl, go)):
        ref[...] = gw[8 * n:8 * n + 8, :]


def layer_scratch():
    vmem, dma = pltpu.VMEM, pltpu.SemaphoreType.DMA
    return dict(
        core_scratch(),
        wide=vmem((2, 1024, 128), F32), wide2=vmem((2, 2048, 128), F32), wself=vmem((48, 128), BF16), wall=vmem((16, 48, 128), BF16),
        stage1=vmem((16, 16, 512), BF16), recv1=vmem((16, 16, 512), BF16), xp=vmem((128, 512), BF16), up=vmem((128, 512), BF16),
        stage2=vmem((16, 48, 512), BF16), recv2=vmem((16, 48, 512), BF16), near=vmem((16, 32, 512), BF16), mask=vmem((2, 32, 128), F32),
        kr=vmem((8, 16, 16, 256), BF16),
        ql2=vmem((2, 64, 2048), F32), qlin=vmem((2, 32, 2048), F32), kro=vmem((8, 32, 16, 128), F32), krin=vmem((8, 32, 16, 128), F32),
        mx=vmem((8, 64, 128), BF16), mixin=vmem((8, 32, 128), BF16), mixf=vmem((2, 256, 128), F32),
        stagem=vmem((16, 16, 512), BF16), recvm=vmem((16, 16, 512), BF16),
        stage3=vmem((2, 16, 16, 512), BF16), recv3=vmem((2, 16, 16, 512), BF16), stage4=vmem((16, 16, 512), BF16), recv4=vmem((16, 16, 512), BF16),
        gws=vmem((16, 40, 128), F32), gwin=vmem((16, 40, 128), F32), part=vmem((40, 128), F32), gwrow=vmem((8, 40, 128), F32),
        hs=dma((16, 16)), rs=dma((4, 8)), ps=dma((2, 21)), ks=dma((2, 4, 8)),
    )


def local(x, allowance, asking, lookup, first_content, second_content, final, scaling, upstream):
    vm = pl.BlockSpec(memory_space=pltpu.VMEM)
    names = layer_scratch()
    grads, gw = pl.pallas_call(
        functools.partial(layer, list(names)),
        out_shape=[jax.ShapeDtypeStruct((8, 32, 256), BF16), jax.ShapeDtypeStruct((40, 128), F32)],
        in_specs=[vm] * 8 + [pl.BlockSpec(memory_space=pltpu.SMEM)], out_specs=[vm] * 2,
        scratch_shapes=list(names.values()),
        compiler_params=pltpu.CompilerParams(collective_id=0, has_side_effects=True, vmem_limit_bytes=56 * 2 ** 20),
        name="layer",
    )(x, upstream, asking.T, lookup.T, first_content.T, second_content.T, final, allowance, scaling)
    grads, gq, gk, gl, gr, go = pl.pallas_call(
        results, out_shape=[jax.ShapeDtypeStruct((8, 32, 256), BF16)] + [jax.ShapeDtypeStruct((8, 128), F32)] * 5,
        in_specs=[vm] * 2, out_specs=[vm] * 6, name="results",
    )(grads, gw)
    return grads, gq.T, gk.T, gl.T, gr.T, go


def solution(mesh):
    pairs, columns = P("head", "row", None), P(None, "head")
    placed = (pairs, P("row", None), columns, columns, columns, columns, P("head", None), P("head"), pairs)
    return jax.shard_map(
        local, mesh=mesh, in_specs=placed,
        out_specs=(pairs, columns, columns, columns, columns, P("head", None)), check_vma=False,
    )
```

```python
import functools

import jax
import jax.numpy as jnp
from jax import lax
from jax.experimental import pallas as pl
from jax.experimental.pallas import tpu as pltpu
from jax.sharding import PartitionSpec as P

F32, BF16 = jnp.float32, jnp.bfloat16
MESH = pl.DeviceIdType.MESH
NT = (((1,), (1,)), ((), ()))
NN = (((1,), (0,)), ((), ()))
TN = (((0,), (0,)), ((), ()))
CH, I, L, J = 8, 64, 256, 128
HEADS, ROWS = 16, 8


def dot(a, b, dims=NN):
    return lax.dot_general(a, b, dims, preferred_element_type=F32)


def core_scratch():
    return dict(
        pt=pltpu.VMEM((1024, 1024), BF16),
        q2=pltpu.VMEM((I, 2048), BF16), b2=pltpu.VMEM((I, 2048), BF16),
        qt=pltpu.VMEM((2048, 128), BF16), kf=pltpu.VMEM((2048, J), F32), rf=pltpu.VMEM((2048, J), F32),
        k2=pltpu.VMEM((2048, J), BF16), mt=pltpu.VMEM((16, 256), BF16), wc=pltpu.VMEM((128, 1024), BF16), lb16=pltpu.VMEM((I, 2048), BF16),
        s=pltpu.VMEM((L, I, J), F32), m=pltpu.VMEM((I, J), F32), gs=pltpu.VMEM((CH, I, J), F32), ds=pltpu.VMEM((I, J), F32),

        e=pltpu.VMEM((16, I, J), F32), br8=pltpu.VMEM((16, 64, J), F32),
    )


def permutation(pt):
    @pl.loop(0, 8)
    def _(n):
        a = lax.broadcasted_iota(jnp.int32, (128, 1024), 0) + n * 128
        b = lax.broadcasted_iota(jnp.int32, (128, 1024), 1)
        hit = ((a >> 3) == (b & 127)) & ((a & 7) == (b >> 7))
        pt[pl.ds(pl.multiple_of(n * 128, 128), 128), :] = jnp.where(hit, 1.0, 0.0).astype(BF16)


def constants(w):
    permutation(w["pt"])
    row = lax.broadcasted_iota(jnp.int32, (16, 256), 0)
    lane = lax.broadcasted_iota(jnp.int32, (16, 256), 1)
    w["mt"][...] = jnp.where(((lane & 127) >> 3) == row, 1.0, 0.0).astype(BF16)
    ra = lax.broadcasted_iota(jnp.int32, (128, 1024), 0)
    rb_ = lax.broadcasted_iota(jnp.int32, (128, 1024), 1)
    w["wc"][...] = jnp.where((ra & 7) == (rb_ >> 7), 1.0, 0.0).astype(BF16)


def prepare(wide, w):
    pt = w["pt"]
    for half in range(2):
        out = slice(half * 1024, half * 1024 + 1024)
        qcat = jnp.concatenate([wide[half, c * I:c * I + I, :] for c in range(CH)], axis=1).astype(BF16)
        lcat = jnp.concatenate([wide[half, c * I:c * I + I, :] for c in range(CH, 2 * CH)], axis=1).astype(BF16)
        bcat = jnp.concatenate([wide[half, 24 * I:25 * I, :].astype(BF16), jnp.zeros((I, 896), BF16)], axis=1)
        got = dot(jnp.concatenate([qcat, lcat, bcat], axis=0), pt[...], NT)
        w["q2"][:, out] = got[:I].astype(BF16)
        w["lb16"][:, out] = got[I:2 * I].astype(BF16)
        w["b2"][:, out] = got[2 * I:].astype(BF16)
        w["qt"][out, :] = dot(pt[...], jnp.concatenate([qcat, qcat], axis=0), NT).astype(BF16)
    w["m"][...] = jnp.full((I, J), -3e38, F32)


def scores(n, w):
    at = pl.ds(pl.multiple_of(n * 128, 128), 128)
    k2 = w["kf"][at, :].astype(BF16)
    w["k2"][at, :] = k2
    qb = jnp.concatenate([w["q2"][:, at], w["b2"][:, at]], axis=1)
    kk = jnp.concatenate([k2, jnp.ones((128, J), BF16)], axis=0)
    lhs = jnp.concatenate([qb * w["mt"][t:t + 1, :] for t in range(16)], axis=0)
    raw = dot(lhs, kk).reshape(16, I, J)
    top = w["m"][...]
    for t in range(16):
        top = jnp.maximum(top, raw[t])
    w["m"][...] = top
    w["s"][pl.ds(n * 16, 16)] = raw


def forward(wide, mine, f, mixed, w):
    @pl.loop(0, 2)
    def _(ip):
        rows = pl.ds(pl.multiple_of(ip * 32, 32), 32)
        top = w["m"][rows, :]

        def step(n, carry):
            total, acc = carry
            acc = list(acc)
            tile = w["lb16"][rows, pl.ds(pl.multiple_of(n * 128, 128), 128)]
            lhs = jnp.concatenate([tile * w["mt"][t:t + 1, :128] for t in range(16)], axis=0)
            rg = w["rf"][pl.ds(pl.multiple_of(n * 128, 128), 128), :].astype(BF16)
            both = dot(lhs, jnp.concatenate([rg] * CH, axis=1) * w["wc"][...])
            for t in range(16):
                lv = n * 16 + t
                wt = jnp.exp(f * (w["s"][lv, rows, :] - top))
                w["s"][lv, rows, :] = wt
                total = total + wt
                for c in range(CH):
                    acc[c] = acc[c] + wt * both[t * 32:t * 32 + 32, c * 128:c * 128 + 128]
            return total, tuple(acc)

        zero = jnp.zeros((32, J), F32)
        total, acc = lax.fori_loop(0, 16, step, (zero, (zero,) * CH), unroll=4)
        inv = 1.0 / total
        delta = zero
        for c in range(CH):
            gc = wide[mine, pl.ds(pl.multiple_of((16 + c) * I + ip * 32, 32), 32), :]
            mc = acc[c] * inv
            mixed[c, rows, :] = mc.astype(BF16)
            delta = delta + gc * mc
            w["gs"][c, rows, :] = gc * inv
        w["ds"][rows, :] = delta * inv


def backward(n, chip, place, f, bq2, bl2, kro, w):
    at = pl.ds(pl.multiple_of(n * 128, 128), 128)
    bl2[:, at] = jnp.zeros((I, 128), F32)

    @pl.loop(0, 16, unroll=4)
    def _(t):
        lv = n * 16 + t
        lanes64 = lax.broadcasted_iota(jnp.int32, (I, 128), 1)
        pick = jnp.where((lanes64 >> 3) == t, 1.0, 0.0).astype(BF16)
        spread = dot(w["lb16"][:, at] * pick, w["wc"][...])
        rr = w["rf"][pl.ds(pl.multiple_of(lv * 8, 8), 8), :]
        rb = [jnp.broadcast_to(rr[c:c + 1, :], (16, J)) for c in range(CH)]
        br = [jnp.zeros((16, J), F32) for c in range(CH)]
        base = t * 8
        lanes16 = lax.broadcasted_iota(jnp.int32, (16, 128), 1)
        for it in range(4):
            rows = slice(it * 16, it * 16 + 16)
            wt = w["s"][lv, rows, :]
            blt = bl2[rows, at]
            pgp = None
            for c in range(CH):
                x = wt * w["gs"][c, rows, :]
                xl = x * spread[rows, c * 128:c * 128 + 128]
                br[c] = br[c] + xl
                term = xl * rb[c]
                pgp = term if pgp is None else pgp + term
                red = jnp.sum(x * rb[c], axis=1, keepdims=True)
                blt = jnp.where(lanes16 == base + c, red, blt)
            w["e"][t, rows, :] = pgp - wt * w["ds"][rows, :]
            bl2[rows, at] = blt
        for c in range(CH):
            w["br8"][t, c * 8:c * 8 + 8, :] = br[c][:8] + br[c][8:]

    for t in range(16):
        tot = w["br8"][t, pl.ds(0, 8, stride=8), :]
        for z in range(1, 8):
            tot = tot + w["br8"][t, pl.ds(z, 8, stride=8), :]
        kro[2 * chip + (t // 2) % 2, place + (t // 4) * 4 + t % 2, 8:16, :] = tot
    ev = w["e"][...].reshape(16 * I, J)
    hi = ev.astype(BF16)
    lo = (ev - hi.astype(F32)).astype(BF16)
    kt = w["k2"][at, :]
    bqw = dot(jnp.concatenate([hi, lo], axis=1), jnp.concatenate([kt, kt], axis=1), NT)
    tot = jnp.zeros((I, 128), F32)
    lane2 = lax.broadcasted_iota(jnp.int32, (I, 128), 1)
    for t in range(16):
        tot = jnp.where((lane2 >> 3) == t, bqw[t * I:(t + 1) * I, :], tot)
    bq2[:, at] = f * tot
    sub_r = lax.broadcasted_iota(jnp.int32, (32, 256), 0)
    sub_c = lax.broadcasted_iota(jnp.int32, (32, 256), 1)
    keep = jnp.where((sub_r >> 3) == (sub_c >> 6), 1.0, 0.0).astype(BF16)
    for u in range(4):
        qrow = w["qt"][pl.ds(pl.multiple_of(n * 128 + u * 32, 32), 32), :]
        lhs = jnp.concatenate([qrow, qrow], axis=1) * keep
        part = dot(jnp.concatenate([lhs, lhs], axis=1), jnp.concatenate([hi[u * 256:u * 256 + 256], lo[u * 256:u * 256 + 256]], axis=0))
        part = f * part
        for core in range(2):
            for a in range(2):
                first = (core * 2 + a) * 8
                kro[2 * chip + core, place + u * 4 + a, 0:8, :] = part[first:first + 8]


def greet(groups):
    barrier = pltpu.get_barrier_semaphore()
    for n, peer in groups:
        @pl.loop(1, n)
        def _(s):
            pl.semaphore_signal(barrier, inc=1, device_id=peer(s), device_id_type=MESH)


class Trade:
    def __init__(self, n, peer, src, dst, send_sem, recv_sem):
        self.n, self.peer, self.src, self.dst, self.send_sem, self.recv_sem = n, peer, src, dst, send_sem, recv_sem

    def copy(self, s):
        return pltpu.make_async_remote_copy(
            src_ref=self.src(s), dst_ref=self.dst, send_sem=self.send_sem.at[s], recv_sem=self.recv_sem.at[s],
            device_id=self.peer(s), device_id_type=MESH)

    def start(self):
        @pl.loop(1, self.n)
        def _(s):
            self.copy(s).start()

    def finish(self):
        @pl.loop(1, self.n)
        def _(s):
            self.copy(s).wait_recv()

    def drain(self):
        @pl.loop(1, self.n)
        def _(s):
            self.copy(s).wait_send()


def lane_of(i, z):
    return z * 256 + (i % 2) * 128


def to_pairs(wide, stage, count, rows, first=0):
    for i in range(32):
        for z in range(2):
            at = lane_of(i, z)
            piece = wide[z, pl.ds(i, count, stride=32), :]
            if count % 16:
                piece = jnp.concatenate([piece, jnp.zeros((16 - count % 16, 128), F32)], axis=0)
            stage[i // 2, first:first + rows, at:at + 128] = piece.astype(BF16)


def from_pairs(recv, lo, hi, wide, offset, stride, first=0, count=16):
    for i in range(2 * count):
        for z in range(2):
            at = lane_of(i, z)
            rows = pl.ds(offset + first * 2 + i, hi - lo, stride=stride)
            wide[z, rows, :] = recv[first + i // 2, lo:hi, at:at + 128].astype(F32)


def layer(names, x, u, wq, wk, wl, wr, wf, allowance, fac, grads, gw, *scratch):
    w = dict(zip(names, scratch))
    me, row = lax.axis_index("head"), lax.axis_index("row")
    core = lax.rem(me, 2)
    x_hi, x_lo, y_lo = lax.rem(row // 2, 2), lax.rem(row, 2), row // 4
    slot = (me // 2) * 2 + x_hi
    part = y_lo * 4 + x_lo * 2 + core
    block = part // 2

    def head_peer(s):
        return {"head": lax.rem(me + s, HEADS), "row": row}

    def row_peer(s):
        return {"head": me, "row": lax.rem(row + s, ROWS)}

    def slot_at(s):
        return lax.rem(slot // 4 + s // 4, 4) * 4 + lax.rem(slot + s, 4)

    def slot_peer(s):
        to = slot_at(s)
        return {"head": (to // 2) * 2 + core, "row": y_lo * 4 + lax.rem(to, 2) * 2 + x_lo}

    def part_peer(s):
        to = lax.rem(part + s, 8)
        return {"head": (me // 2) * 2 + lax.rem(to, 2), "row": (to // 4) * 4 + x_hi * 2 + lax.rem(to // 2, 2)}

    partner = {"head": me + 1 - 2 * core, "row": row}
    hs, rs, ps = w["hs"], w["rs"], w["ps"]

    def over(n, size, peer, src, dst):
        sems = hs if size == HEADS else rs
        return Trade(size, peer, src, dst, sems.at[2 * n], sems.at[2 * n + 1])

    def to_partner(n, src, dst):
        return pltpu.make_async_remote_copy(src_ref=src, dst_ref=dst, send_sem=ps.at[0, n], recv_sem=ps.at[1, n],
                                            device_id=partner, device_id_type=MESH)

    def head_at(s):
        return lax.rem(me + s, HEADS)

    greet([(HEADS, head_peer), (ROWS, row_peer), (HEADS, slot_peer), (8, part_peer)])
    wself, wall, wide = w["wself"], w["wall"], w["wide"]
    f0 = jnp.full((8, 128), fac[0], F32)
    f1 = f0 - f0.astype(BF16).astype(F32)
    f2 = f1 - f1.astype(BF16).astype(F32)
    tile = lax.broadcasted_iota(jnp.int32, (8, 128), 0)
    factor = jnp.where(tile == 0, f0, jnp.where(tile == 1, f1, jnp.where(tile == 2, f2, 0.0)))
    wself[...] = jnp.concatenate([wk[...], wr[...], wq[...], wl[...], wf[...], factor.astype(BF16)], axis=0)
    for z in range(2):
        wide[z, 0:256, :] = x[:, :, z * 128:z * 128 + 128].reshape(256, 128).astype(F32)
        wide[z, 256:512, :] = u[:, :, z * 128:z * 128 + 128].reshape(256, 128).astype(F32)
    to_pairs(wide, w["stage1"], 16, 16)
    pl.semaphore_wait(pltpu.get_barrier_semaphore(), 2 * HEADS + ROWS + 8 - 4)
    inputs = over(0, HEADS, head_peer, lambda s: w["stage1"].at[head_at(s)], w["recv1"].at[me])
    weights = over(1, HEADS, head_peer, lambda s: wself, wall.at[me])
    weights.start()
    inputs.start()
    w["recv1"][me] = w["stage1"][me]
    wall[me] = wself[...]
    constants(w)
    node = row * 32 + lax.broadcasted_iota(jnp.int32, (32, 128), 0)
    column = lax.broadcasted_iota(jnp.int32, (32, 128), 1)
    for z in range(2):
        valid = (allowance[:, z * 128:z * 128 + 128] == 1) | (node == column + z * 128)
        w["mask"][z] = jnp.where(valid, 0.0, -1e30)
    bias = jnp.concatenate([w["mask"][z, pl.ds(2 * me + a, 1), :] for z in range(2) for a in range(2)], axis=1)
    bias = jnp.broadcast_to(bias, (8, 512))
    inputs.finish()
    both = w["recv1"][...].astype(F32)
    w["xp"][...] = both[:, 0:8].reshape(128, 512).astype(BF16)
    w["up"][...] = both[:, 8:16].reshape(128, 512).astype(BF16)
    weights.finish()

    stage2, recv2, kr = w["stage2"], w["recv2"], w["kr"]
    mapped = over(2, HEADS, slot_peer, lambda s: stage2.at[slot_at(s)], recv2.at[slot])
    for first in range(0, HEADS, 4):
        peers = [slot_at(first + a) for a in range(4)]
        of_x = dot(jnp.concatenate([wall[p, 0:32] for p in peers], axis=0), w["xp"][...]).astype(BF16)
        of_u = dot(jnp.concatenate([wall[p, 32:48] for p in peers], axis=0), w["up"][...])
        for a, p in enumerate(peers):
            stage2[p, 0:32] = of_x[a * 32:a * 32 + 32]
            stage2[p, 32:48] = jnp.concatenate([of_u[a * 16:a * 16 + 8], bias], axis=0).astype(BF16)
            if first + a:
                mapped.copy(first + a).start()
            else:
                recv2[slot] = stage2[slot]

    near, wide2 = w["near"], w["wide2"]

    def four(g):
        return lax.rem(slot // 4 + 4 - g, 4) * 4

    def kr_copy(g, s):
        some = pl.ds(four(g), 4)
        to = lax.rem(part + s, 8)
        return pltpu.make_async_remote_copy(
            src_ref=recv2.at[some, pl.ds(0, 16), pl.ds(pl.multiple_of(lax.rem(to, 2) * 256, 128), 256)], dst_ref=kr.at[part, some],
            send_sem=w["ks"].at[0, g, s], recv_sem=w["ks"].at[1, g, s], device_id=part_peer(s), device_id_type=MESH)

    def near_copy(g):
        some = pl.ds(four(g), 4)
        return to_partner(g, recv2.at[some, pl.ds(16, 32)], near.at[some])

    def unpack_near(g):
        near_copy(g).wait_recv()
        from_pairs(near, 0, 32, wide2, 32 - core * 32, I, four(g), 4)

    @pl.loop(0, 4)
    def _(g):
        @pl.loop(0, 4)
        def _(a):
            @pl.when(g * 4 + a > 0)
            def _():
                mapped.copy(g * 4 + a).wait_recv()

        near_copy(g).start()

        @pl.loop(1, 8)
        def _(s):
            kr_copy(g, s).start()

        from_pairs(recv2, 16, 48, wide2, core * 32, I, four(g), 4)

        @pl.when(g > 0)
        def _():
            unpack_near(g - 1)

    unpack_near(3)
    own = pl.multiple_of(core * 32, 32)
    prepare(wide2, w)

    f = jnp.sum(wall[slot, 32:48].astype(F32)[8:16], axis=0, keepdims=True)

    def groups(chip):
        for hi in range(2):
            for y in range(2):
                yield 2 * ((chip // 2) * 4 + hi * 2 + lax.rem(chip, 2)) + y, y * 8 + hi

    @pl.loop(0, 4)
    def _(k):
        chip = lax.rem(block + 4 - k, 4)
        for c in range(2):
            @pl.when(2 * chip + c != part)
            def _():
                @pl.loop(0, 4)
                def _(g):
                    kr_copy(g, lax.rem(part + 8 - 2 * chip - c, 8)).wait_recv()

            @pl.when(2 * chip + c == part)
            def _():
                kr[part] = recv2[:, 0:16, pl.ds(pl.multiple_of(core * 256, 128), 256)]

        for n, first in groups(chip):
            for t in range(16):
                at = (first + (t // 4) * 2)
                tile = kr[2 * chip + (t // 2) % 2, at, :, (t % 2) * 128:(t % 2) * 128 + 128].astype(F32)
                rows = pl.ds(pl.multiple_of(n * 128 + t * 8, 8), 8)
                w["kf"][rows, :] = tile[0:8]
                w["rf"][rows, :] = tile[8:16]
            scores(n, w)

    forward(wide2, core, f, w["mx"], w)
    mine, other = pl.ds(own, 32), pl.ds(pl.multiple_of(32 - core * 32, 32), 32)
    mixed_out = to_partner(4, w["mx"].at[:, other], w["mixin"])
    mixed_out.start()
    ql2, qlin, kro, krin = w["ql2"], w["qlin"], w["kro"], w["krin"]
    stageq, recvq = w["stageq"], w["recvq"]

    def out_copy(y, to):
        s = lax.rem(to + 8 - part, 8)
        rows = pl.ds(y * 16, 16)
        return pltpu.make_async_remote_copy(
            src_ref=kro.at[to, rows], dst_ref=krin.at[part, rows], send_sem=w["os"].at[y, 0, s], recv_sem=w["os"].at[y, 1, s],
            device_id=part_peer(s), device_id_type=MESH)

    mixed = over(3, HEADS, slot_peer, lambda s: w["stagem"].at[slot_at(s)], w["recvm"].at[slot])

    def group_out(n):
        lanes = pl.ds(pl.multiple_of(n * 128, 128), 128)
        return to_partner(5 + n, ql2.at[:, other, lanes], qlin.at[:, :, lanes])

    def half_out(h, n):
        @pl.loop(0, 8)
        def _(g):
            group_out(8 * h + g).wait()

        lanes = pl.ds(pl.multiple_of(h * 1024, 1024), 1024)
        total = (ql2[:, mine, lanes] + qlin[:, :, lanes]).astype(BF16).reshape(64, 1024)
        plain = dot(total, w["pt"][...])
        for c in range(CH):
            wide[n, c * 32:c * 32 + 32, :] = plain[0:32, c * 128:c * 128 + 128]
            wide[n, 256 + c * 32:288 + c * 32, :] = plain[32:64, c * 128:c * 128 + 128]
        for i in range(32):
            stageq[n, i // 2, :, (i % 2) * 128:(i % 2) * 128 + 128] = wide[n, pl.ds(i, 16, stride=32), :].astype(BF16)
        halves[n].start()
        recvq[h, slot] = stageq[n, slot]

    far = 1 - y_lo
    halves = [over(4 + 3 * n, HEADS, slot_peer, lambda s, n=n: stageq.at[n, slot_at(s)], recvq.at[h, slot]) for n, h in enumerate((far, y_lo))]

    @pl.loop(0, 4)
    def _(k):
        cy, cx = lax.rem(y_lo + 1 + k // 2, 2), lax.rem(x_lo + (k + 1) // 2, 2)
        chip = cy * 2 + cx

        @pl.loop(0, 4)
        def _(j):
            n = 2 * (cy * 4 + lax.rem(j, 2) * 2 + cx) + j // 2
            backward(n, chip, (j // 2) * 16 + lax.rem(j, 2) * 2, f, ql2.at[0], ql2.at[1], kro, w)
            group_out(n).start()

            @pl.when(lax.rem(j, 2) == 1)
            def _():
                for c in range(2):
                    to = 2 * chip + c

                    @pl.when(to != part)
                    def _():
                        out_copy(j // 2, to).start()

        @pl.when(k == 3)
        def _():
            krin[part] = kro[part]

        @pl.when(k == 2)
        def _():
            half_out(far, 0)

        @pl.when(k == 0)
        def _():
            mixed_out.wait()
            mixf = w["mixf"]
            for c in range(CH):
                mixf[core, c * 32:c * 32 + 32, :] = w["mx"][c, mine, :].astype(F32)
                mixf[1 - core, c * 32:c * 32 + 32, :] = w["mixin"][c].astype(F32)
            to_pairs(mixf, w["stagem"], 8, 16)
            mixed.start()
            w["recvm"][slot] = w["stagem"][slot]

    half_out(y_lo, 1)
    mixed.finish()
    gws = w["gws"]
    gws[:, 32:40, :] = dot(w["recvm"][...].reshape(256, 512), w["up"][...], NT).reshape(16, 16, 128)[:, 0:8]

    @pl.loop(1, 8)
    def _(s):
        for y in range(2):
            out_copy(y, lax.rem(part + s, 8)).wait_recv()

    stage3, recv3 = w["stage3"], w["recv3"]
    for j in range(2):
        total = krin[j] + krin[2 + j] + krin[4 + j] + krin[6 + j]
        total = total.astype(BF16).reshape(16, 2, 16, 128)
        for a in range(2):
            stage3[:, :, j * 256 + a * 128:j * 256 + a * 128 + 128] = total[:, a]
    backs = over(8, HEADS, slot_peer, lambda s: stage3.at[slot_at(s)], recv3.at[slot])
    backs.start()
    recv3[slot] = stage3[slot]

    image = None
    for n in (1, 0):
        if n:
            halves[0].finish()
            halves[1].finish()
            every = jnp.concatenate([recvq[0].reshape(256, 256), recvq[1].reshape(256, 256)], axis=1)
        else:
            backs.finish()
            every = recv3[...].reshape(256, 512)
        gws[:, 16 * n:16 * n + 16, :] = dot(every, w["xp"][...], NT).reshape(16, 16, 128)
        term = dot(wall[:, 16 * n:16 * n + 16, :].reshape(256, 128), every, TN)
        image = term if image is None else image + term
    sums = over(5, HEADS, head_peer, lambda s: gws.at[head_at(s)], w["gwin"].at[me])
    sums.start()
    w["gwin"][me] = gws[me]
    image = image.reshape(16, 8, 512)
    w["stage4"][...] = jnp.concatenate([image[:, :, 0:256], image[:, :, 256:512]], axis=1).astype(BF16)
    images = over(6, HEADS, head_peer, lambda s: w["stage4"].at[head_at(s)], w["recv4"].at[me])
    images.start()
    w["recv4"][me] = w["stage4"][me]
    sums.finish()
    total = w["gwin"][0]
    for p in range(1, HEADS):
        total = total + w["gwin"][p]
    w["part"][...] = total
    last = over(1, ROWS, row_peer, lambda s: w["part"], w["gwrow"].at[row])
    last.start()
    w["gwrow"][row] = total
    images.finish()
    for i in range(32):
        two = w["recv4"][i // 2, :, (i % 2) * 128:(i % 2) * 128 + 128].astype(F32)
        for z in range(2):
            wide[z, pl.ds(i, 8, stride=32), :] = two[z * 8:z * 8 + 8]
    for z in range(2):
        grads[:, :, z * 128:z * 128 + 128] = wide[z, 0:256, :].astype(BF16).reshape(8, 32, 128)
    last.finish()
    total = w["gwrow"][0]
    for p in range(1, ROWS):
        total = total + w["gwrow"][p]
    gw[...] = total * (1.0 / 256.0)
    for trade in (inputs, weights, mapped, mixed, *halves, backs, sums, images, last):
        trade.drain()

    @pl.loop(0, 4)
    def _(g):
        near_copy(g).wait_send()

        @pl.loop(1, 8)
        def _(s):
            kr_copy(g, s).wait_send()

    @pl.loop(1, 8)
    def _(s):
        for y in range(2):
            out_copy(y, lax.rem(part + s, 8)).wait_send()


def results(grads, gw, out, gq, gk, gl, gr, go):
    out[...] = grads[...]
    for n, ref in enumerate((gk, gr, gq, gl, go)):
        ref[...] = gw[8 * n:8 * n + 8, :]


def layer_scratch():
    vmem, dma = pltpu.VMEM, pltpu.SemaphoreType.DMA
    return dict(
        core_scratch(),
        wide=vmem((2, 1024, 128), F32), wide2=vmem((2, 2048, 128), F32), wself=vmem((48, 128), BF16), wall=vmem((16, 48, 128), BF16),
        stage1=vmem((16, 16, 512), BF16), recv1=vmem((16, 16, 512), BF16), xp=vmem((128, 512), BF16), up=vmem((128, 512), BF16),
        stage2=vmem((16, 48, 512), BF16), recv2=vmem((16, 48, 512), BF16), near=vmem((16, 32, 512), BF16), mask=vmem((2, 32, 128), F32),
        kr=vmem((8, 16, 16, 256), BF16),
        ql2=vmem((2, 64, 2048), F32), qlin=vmem((2, 32, 2048), F32), kro=vmem((8, 32, 16, 128), F32), krin=vmem((8, 32, 16, 128), F32),
        mx=vmem((8, 64, 128), BF16), mixin=vmem((8, 32, 128), BF16), mixf=vmem((2, 256, 128), F32),
        stagem=vmem((16, 16, 512), BF16), recvm=vmem((16, 16, 512), BF16),
        stage3=vmem((16, 16, 512), BF16), recv3=vmem((16, 16, 512), BF16), stageq=vmem((2, 16, 16, 256), BF16), recvq=vmem((2, 16, 16, 256), BF16), stage4=vmem((16, 16, 256), BF16), recv4=vmem((16, 16, 256), BF16),
        gws=vmem((16, 40, 128), F32), gwin=vmem((16, 40, 128), F32), part=vmem((40, 128), F32), gwrow=vmem((8, 40, 128), F32),
        os=dma((2, 2, 8)), hs=dma((18, 16)), rs=dma((4, 8)), ps=dma((2, 21)), ks=dma((2, 4, 8)),
    )


def local(x, allowance, asking, lookup, first_content, second_content, final, scaling, upstream):
    vm = pl.BlockSpec(memory_space=pltpu.VMEM)
    names = layer_scratch()
    grads, gw = pl.pallas_call(
        functools.partial(layer, list(names)),
        out_shape=[jax.ShapeDtypeStruct((8, 32, 256), BF16), jax.ShapeDtypeStruct((40, 128), F32)],
        in_specs=[vm] * 8 + [pl.BlockSpec(memory_space=pltpu.SMEM)], out_specs=[vm] * 2,
        scratch_shapes=list(names.values()),
        compiler_params=pltpu.CompilerParams(collective_id=0, has_side_effects=True, vmem_limit_bytes=56 * 2 ** 20),
        name="layer",
    )(x, upstream, asking.T, lookup.T, first_content.T, second_content.T, final, allowance, scaling)
    grads, gq, gk, gl, gr, go = pl.pallas_call(
        results, out_shape=[jax.ShapeDtypeStruct((8, 32, 256), BF16)] + [jax.ShapeDtypeStruct((8, 128), F32)] * 5,
        in_specs=[vm] * 2, out_specs=[vm] * 6, name="results",
    )(grads, gw)
    return grads, gq.T, gk.T, gl.T, gr.T, go


def solution(mesh):
    pairs, columns = P("head", "row", None), P(None, "head")
    placed = (pairs, P("row", None), columns, columns, columns, columns, P("head", None), P("head"), pairs)
    return jax.shard_map(
        local, mesh=mesh, in_specs=placed,
        out_specs=(pairs, columns, columns, columns, columns, P("head", None)), check_vma=False,
    )
```

```python
import functools

import jax
import jax.numpy as jnp
from jax import lax
from jax.experimental import pallas as pl
from jax.experimental.pallas import tpu as pltpu
from jax.sharding import PartitionSpec as P

F32, BF16 = jnp.float32, jnp.bfloat16
MESH = pl.DeviceIdType.MESH
NT = (((1,), (1,)), ((), ()))
NN = (((1,), (0,)), ((), ()))
TN = (((0,), (0,)), ((), ()))
CH, I, L, J = 8, 64, 256, 128
HEADS, ROWS = 16, 8


def dot(a, b, dims=NN):
    return lax.dot_general(a, b, dims, preferred_element_type=F32)


def core_scratch():
    return dict(
        pt=pltpu.VMEM((1024, 1024), BF16),
        q2=pltpu.VMEM((I, 2048), BF16), b2=pltpu.VMEM((I, 2048), BF16),
        qt=pltpu.VMEM((2048, 128), BF16), kf=pltpu.VMEM((2048, J), F32), rf=pltpu.VMEM((2048, J), F32),
        k2=pltpu.VMEM((2048, J), BF16), mt=pltpu.VMEM((16, 256), BF16), wc=pltpu.VMEM((128, 1024), BF16), lb16=pltpu.VMEM((I, 2048), BF16),
        s=pltpu.VMEM((L, I, J), F32), m=pltpu.VMEM((I, J), F32), gs=pltpu.VMEM((CH, I, J), F32), ds=pltpu.VMEM((I, J), F32),

        e=pltpu.VMEM((16, I, J), F32), br8=pltpu.VMEM((16, 64, J), F32),
    )


def permutation(pt):
    @pl.loop(0, 8)
    def _(n):
        a = lax.broadcasted_iota(jnp.int32, (128, 1024), 0) + n * 128
        b = lax.broadcasted_iota(jnp.int32, (128, 1024), 1)
        hit = ((a >> 3) == (b & 127)) & ((a & 7) == (b >> 7))
        pt[pl.ds(pl.multiple_of(n * 128, 128), 128), :] = jnp.where(hit, 1.0, 0.0).astype(BF16)


def constants(w):
    permutation(w["pt"])
    row = lax.broadcasted_iota(jnp.int32, (16, 256), 0)
    lane = lax.broadcasted_iota(jnp.int32, (16, 256), 1)
    w["mt"][...] = jnp.where(((lane & 127) >> 3) == row, 1.0, 0.0).astype(BF16)
    ra = lax.broadcasted_iota(jnp.int32, (128, 1024), 0)
    rb_ = lax.broadcasted_iota(jnp.int32, (128, 1024), 1)
    w["wc"][...] = jnp.where((ra & 7) == (rb_ >> 7), 1.0, 0.0).astype(BF16)


def prepare(wide, w):
    pt = w["pt"]
    for half in range(2):
        out = slice(half * 1024, half * 1024 + 1024)
        qcat = jnp.concatenate([wide[half, c * I:c * I + I, :] for c in range(CH)], axis=1).astype(BF16)
        lcat = jnp.concatenate([wide[half, c * I:c * I + I, :] for c in range(CH, 2 * CH)], axis=1).astype(BF16)
        bcat = jnp.concatenate([wide[half, 24 * I:25 * I, :].astype(BF16), jnp.zeros((I, 896), BF16)], axis=1)
        got = dot(jnp.concatenate([qcat, lcat, bcat], axis=0), pt[...], NT)
        w["q2"][:, out] = got[:I].astype(BF16)
        w["lb16"][:, out] = got[I:2 * I].astype(BF16)
        w["b2"][:, out] = got[2 * I:].astype(BF16)
        w["qt"][out, :] = dot(pt[...], jnp.concatenate([qcat, qcat], axis=0), NT).astype(BF16)
    w["m"][...] = jnp.full((I, J), -3e38, F32)


def scores(n, w):
    at = pl.ds(pl.multiple_of(n * 128, 128), 128)
    k2 = w["kf"][at, :].astype(BF16)
    w["k2"][at, :] = k2
    qb = jnp.concatenate([w["q2"][:, at], w["b2"][:, at]], axis=1)
    kk = jnp.concatenate([k2, jnp.ones((128, J), BF16)], axis=0)
    lhs = jnp.concatenate([qb * w["mt"][t:t + 1, :] for t in range(16)], axis=0)
    raw = dot(lhs, kk).reshape(16, I, J)
    top = w["m"][...]
    for t in range(16):
        top = jnp.maximum(top, raw[t])
    w["m"][...] = top
    w["s"][pl.ds(n * 16, 16)] = raw


def forward(wide, mine, f, mixed, w):
    @pl.loop(0, 2)
    def _(ip):
        rows = pl.ds(pl.multiple_of(ip * 32, 32), 32)
        top = w["m"][rows, :]

        def step(n, carry):
            total, acc = carry
            acc = list(acc)
            tile = w["lb16"][rows, pl.ds(pl.multiple_of(n * 128, 128), 128)]
            lhs = jnp.concatenate([tile * w["mt"][t:t + 1, :128] for t in range(16)], axis=0)
            rg = w["rf"][pl.ds(pl.multiple_of(n * 128, 128), 128), :].astype(BF16)
            both = dot(lhs, jnp.concatenate([rg] * CH, axis=1) * w["wc"][...])
            for t in range(16):
                lv = n * 16 + t
                wt = jnp.exp(f * (w["s"][lv, rows, :] - top))
                w["s"][lv, rows, :] = wt
                total = total + wt
                for c in range(CH):
                    acc[c] = acc[c] + wt * both[t * 32:t * 32 + 32, c * 128:c * 128 + 128]
            return total, tuple(acc)

        zero = jnp.zeros((32, J), F32)
        total, acc = lax.fori_loop(0, 16, step, (zero, (zero,) * CH), unroll=4)
        inv = 1.0 / total
        delta = zero
        for c in range(CH):
            gc = wide[mine, pl.ds(pl.multiple_of((16 + c) * I + ip * 32, 32), 32), :]
            mc = acc[c] * inv
            mixed[c, rows, :] = mc.astype(BF16)
            delta = delta + gc * mc
            w["gs"][c, rows, :] = gc * inv
        w["ds"][rows, :] = delta * inv


def backward(n, chip, place, f, bq2, bl2, kro, w):
    at = pl.ds(pl.multiple_of(n * 128, 128), 128)
    bl2[:, at] = jnp.zeros((I, 128), F32)

    @pl.loop(0, 16, unroll=4)
    def _(t):
        lv = n * 16 + t
        lanes64 = lax.broadcasted_iota(jnp.int32, (I, 128), 1)
        pick = jnp.where((lanes64 >> 3) == t, 1.0, 0.0).astype(BF16)
        spread = dot(w["lb16"][:, at] * pick, w["wc"][...])
        rr = w["rf"][pl.ds(pl.multiple_of(lv * 8, 8), 8), :]
        rb = [jnp.broadcast_to(rr[c:c + 1, :], (16, J)) for c in range(CH)]
        br = [jnp.zeros((16, J), F32) for c in range(CH)]
        base = t * 8
        lanes16 = lax.broadcasted_iota(jnp.int32, (16, 128), 1)
        for it in range(4):
            rows = slice(it * 16, it * 16 + 16)
            wt = w["s"][lv, rows, :]
            blt = bl2[rows, at]
            pgp = None
            for c in range(CH):
                x = wt * w["gs"][c, rows, :]
                xl = x * spread[rows, c * 128:c * 128 + 128]
                br[c] = br[c] + xl
                term = xl * rb[c]
                pgp = term if pgp is None else pgp + term
                red = jnp.sum(x * rb[c], axis=1, keepdims=True)
                blt = jnp.where(lanes16 == base + c, red, blt)
            w["e"][t, rows, :] = pgp - wt * w["ds"][rows, :]
            bl2[rows, at] = blt
        for c in range(CH):
            w["br8"][t, c * 8:c * 8 + 8, :] = br[c][:8] + br[c][8:]

    for t in range(16):
        tot = w["br8"][t, pl.ds(0, 8, stride=8), :]
        for z in range(1, 8):
            tot = tot + w["br8"][t, pl.ds(z, 8, stride=8), :]
        kro[2 * chip + (t // 2) % 2, place + (t // 4) * 4 + t % 2, 8:16, :] = tot
    ev = w["e"][...].reshape(16 * I, J)
    hi = ev.astype(BF16)
    lo = (ev - hi.astype(F32)).astype(BF16)
    kt = w["k2"][at, :]
    bqw = dot(jnp.concatenate([hi, lo], axis=1), jnp.concatenate([kt, kt], axis=1), NT)
    tot = jnp.zeros((I, 128), F32)
    lane2 = lax.broadcasted_iota(jnp.int32, (I, 128), 1)
    for t in range(16):
        tot = jnp.where((lane2 >> 3) == t, bqw[t * I:(t + 1) * I, :], tot)
    bq2[:, at] = f * tot
    sub_r = lax.broadcasted_iota(jnp.int32, (32, 256), 0)
    sub_c = lax.broadcasted_iota(jnp.int32, (32, 256), 1)
    keep = jnp.where((sub_r >> 3) == (sub_c >> 6), 1.0, 0.0).astype(BF16)
    for u in range(4):
        qrow = w["qt"][pl.ds(pl.multiple_of(n * 128 + u * 32, 32), 32), :]
        lhs = jnp.concatenate([qrow, qrow], axis=1) * keep
        part = dot(jnp.concatenate([lhs, lhs], axis=1), jnp.concatenate([hi[u * 256:u * 256 + 256], lo[u * 256:u * 256 + 256]], axis=0))
        part = f * part
        for core in range(2):
            for a in range(2):
                first = (core * 2 + a) * 8
                kro[2 * chip + core, place + u * 4 + a, 0:8, :] = part[first:first + 8]


def greet(groups):
    barrier = pltpu.get_barrier_semaphore()
    for n, peer in groups:
        @pl.loop(1, n)
        def _(s):
            pl.semaphore_signal(barrier, inc=1, device_id=peer(s), device_id_type=MESH)


class Trade:
    def __init__(self, n, peer, src, dst, send_sem, recv_sem):
        self.n, self.peer, self.src, self.dst, self.send_sem, self.recv_sem = n, peer, src, dst, send_sem, recv_sem

    def copy(self, s):
        return pltpu.make_async_remote_copy(
            src_ref=self.src(s), dst_ref=self.dst, send_sem=self.send_sem.at[s], recv_sem=self.recv_sem.at[s],
            device_id=self.peer(s), device_id_type=MESH)

    def start(self):
        @pl.loop(1, self.n)
        def _(s):
            self.copy(s).start()

    def finish(self):
        @pl.loop(1, self.n)
        def _(s):
            self.copy(s).wait_recv()

    def drain(self):
        @pl.loop(1, self.n)
        def _(s):
            self.copy(s).wait_send()


def lane_of(i, z):
    return z * 256 + (i % 2) * 128


def to_pairs(wide, stage, count, rows, first=0):
    for i in range(32):
        for z in range(2):
            at = lane_of(i, z)
            piece = wide[z, pl.ds(i, count, stride=32), :]
            if count % 16:
                piece = jnp.concatenate([piece, jnp.zeros((16 - count % 16, 128), F32)], axis=0)
            stage[i // 2, first:first + rows, at:at + 128] = piece.astype(BF16)


def from_pairs(recv, lo, hi, wide, offset, stride, first=0, count=16):
    for i in range(2 * count):
        for z in range(2):
            at = lane_of(i, z)
            rows = pl.ds(offset + first * 2 + i, hi - lo, stride=stride)
            wide[z, rows, :] = recv[first + i // 2, lo:hi, at:at + 128].astype(F32)


def layer(names, x, u, wq, wk, wl, wr, wf, allowance, fac, grads, gw, *scratch):
    w = dict(zip(names, scratch))
    me, row = lax.axis_index("head"), lax.axis_index("row")
    core = lax.rem(me, 2)
    x_hi, x_lo, y_lo = lax.rem(row // 2, 2), lax.rem(row, 2), row // 4
    slot = (me // 2) * 2 + x_hi
    part = y_lo * 4 + x_lo * 2 + core
    block = part // 2

    def head_peer(s):
        return {"head": lax.rem(me + s, HEADS), "row": row}

    def row_peer(s):
        return {"head": me, "row": lax.rem(row + s, ROWS)}

    def slot_at(s):
        return lax.rem(slot // 4 + s // 4, 4) * 4 + lax.rem(slot + s, 4)

    def slot_peer(s):
        to = slot_at(s)
        return {"head": (to // 2) * 2 + core, "row": y_lo * 4 + lax.rem(to, 2) * 2 + x_lo}

    def part_peer(s):
        to = lax.rem(part + s, 8)
        return {"head": (me // 2) * 2 + lax.rem(to, 2), "row": (to // 4) * 4 + x_hi * 2 + lax.rem(to // 2, 2)}

    partner = {"head": me + 1 - 2 * core, "row": row}
    hs, rs, ps = w["hs"], w["rs"], w["ps"]

    def over(n, size, peer, src, dst):
        sems = hs if size == HEADS else rs
        return Trade(size, peer, src, dst, sems.at[2 * n], sems.at[2 * n + 1])

    def to_partner(n, src, dst):
        return pltpu.make_async_remote_copy(src_ref=src, dst_ref=dst, send_sem=ps.at[0, n], recv_sem=ps.at[1, n],
                                            device_id=partner, device_id_type=MESH)

    def head_at(s):
        return lax.rem(me + s, HEADS)

    greet([(HEADS, head_peer), (ROWS, row_peer), (HEADS, slot_peer), (8, part_peer)])
    wself, wall, wide = w["wself"], w["wall"], w["wide"]
    f0 = jnp.full((8, 128), fac[0], F32)
    f1 = f0 - f0.astype(BF16).astype(F32)
    f2 = f1 - f1.astype(BF16).astype(F32)
    tile = lax.broadcasted_iota(jnp.int32, (8, 128), 0)
    factor = jnp.where(tile == 0, f0, jnp.where(tile == 1, f1, jnp.where(tile == 2, f2, 0.0)))
    wself[...] = jnp.concatenate([wk[...], wr[...], wq[...], wl[...], wf[...], factor.astype(BF16)], axis=0)
    for z in range(2):
        wide[z, 0:256, :] = x[:, :, z * 128:z * 128 + 128].reshape(256, 128).astype(F32)
        wide[z, 256:512, :] = u[:, :, z * 128:z * 128 + 128].reshape(256, 128).astype(F32)
    to_pairs(wide, w["stage1"], 16, 16)
    pl.semaphore_wait(pltpu.get_barrier_semaphore(), 2 * HEADS + ROWS + 8 - 4)
    inputs = over(0, HEADS, head_peer, lambda s: w["stage1"].at[head_at(s)], w["recv1"].at[me])
    weights = over(1, HEADS, head_peer, lambda s: wself, wall.at[me])
    weights.start()
    inputs.start()
    w["recv1"][me] = w["stage1"][me]
    wall[me] = wself[...]
    constants(w)
    node = row * 32 + lax.broadcasted_iota(jnp.int32, (32, 128), 0)
    column = lax.broadcasted_iota(jnp.int32, (32, 128), 1)
    for z in range(2):
        valid = (allowance[:, z * 128:z * 128 + 128] == 1) | (node == column + z * 128)
        w["mask"][z] = jnp.where(valid, 0.0, -1e30)
    bias = jnp.concatenate([w["mask"][z, pl.ds(2 * me + a, 1), :] for z in range(2) for a in range(2)], axis=1)
    bias = jnp.broadcast_to(bias, (8, 512))
    inputs.finish()
    both = w["recv1"][...].astype(F32)
    w["xp"][...] = both[:, 0:8].reshape(128, 512).astype(BF16)
    w["up"][...] = both[:, 8:16].reshape(128, 512).astype(BF16)
    weights.finish()

    stage2, recv2, kr = w["stage2"], w["recv2"], w["kr"]
    mapped = over(2, HEADS, slot_peer, lambda s: stage2.at[slot_at(s)], recv2.at[slot])
    for first in range(0, HEADS, 4):
        peers = [slot_at(first + a) for a in range(4)]
        of_x = dot(jnp.concatenate([wall[p, 0:32] for p in peers], axis=0), w["xp"][...]).astype(BF16)
        of_u = dot(jnp.concatenate([wall[p, 32:48] for p in peers], axis=0), w["up"][...])
        for a, p in enumerate(peers):
            stage2[p, 0:32] = of_x[a * 32:a * 32 + 32]
            stage2[p, 32:48] = jnp.concatenate([of_u[a * 16:a * 16 + 8], bias], axis=0).astype(BF16)
            if first + a:
                mapped.copy(first + a).start()
            else:
                recv2[slot] = stage2[slot]

    near, wide2 = w["near"], w["wide2"]

    def four(g):
        return lax.rem(slot // 4 + 4 - g, 4) * 4

    def kr_copy(g, s):
        some = pl.ds(four(g), 4)
        to = lax.rem(part + s, 8)
        return pltpu.make_async_remote_copy(
            src_ref=recv2.at[some, pl.ds(0, 16), pl.ds(pl.multiple_of(lax.rem(to, 2) * 256, 128), 256)], dst_ref=kr.at[part, some],
            send_sem=w["ks"].at[0, g, s], recv_sem=w["ks"].at[1, g, s], device_id=part_peer(s), device_id_type=MESH)

    def near_copy(g):
        some = pl.ds(four(g), 4)
        return to_partner(g, recv2.at[some, pl.ds(16, 32)], near.at[some])

    def unpack_near(g):
        near_copy(g).wait_recv()
        from_pairs(near, 0, 32, wide2, 32 - core * 32, I, four(g), 4)

    @pl.loop(0, 4)
    def _(g):
        @pl.loop(0, 4)
        def _(a):
            @pl.when(g * 4 + a > 0)
            def _():
                mapped.copy(g * 4 + a).wait_recv()

        near_copy(g).start()

        @pl.loop(1, 8)
        def _(s):
            kr_copy(g, s).start()

        from_pairs(recv2, 16, 48, wide2, core * 32, I, four(g), 4)

        @pl.when(g > 0)
        def _():
            unpack_near(g - 1)

    unpack_near(3)
    own = pl.multiple_of(core * 32, 32)
    prepare(wide2, w)

    f = jnp.sum(wall[slot, 32:48].astype(F32)[8:16], axis=0, keepdims=True)

    def groups(chip):
        for hi in range(2):
            for y in range(2):
                yield 2 * ((chip // 2) * 4 + hi * 2 + lax.rem(chip, 2)) + y, y * 8 + hi

    @pl.loop(0, 4)
    def _(k):
        chip = lax.rem(block + 4 - k, 4)
        for c in range(2):
            @pl.when(2 * chip + c != part)
            def _():
                @pl.loop(0, 4)
                def _(g):
                    kr_copy(g, lax.rem(part + 8 - 2 * chip - c, 8)).wait_recv()

            @pl.when(2 * chip + c == part)
            def _():
                kr[part] = recv2[:, 0:16, pl.ds(pl.multiple_of(core * 256, 128), 256)]

        for n, first in groups(chip):
            for t in range(16):
                at = (first + (t // 4) * 2)
                tile = kr[2 * chip + (t // 2) % 2, at, :, (t % 2) * 128:(t % 2) * 128 + 128].astype(F32)
                rows = pl.ds(pl.multiple_of(n * 128 + t * 8, 8), 8)
                w["kf"][rows, :] = tile[0:8]
                w["rf"][rows, :] = tile[8:16]
            scores(n, w)

    forward(wide2, core, f, w["mx"], w)
    mine, other = pl.ds(own, 32), pl.ds(pl.multiple_of(32 - core * 32, 32), 32)
    mixed_out = to_partner(4, w["mx"].at[:, other], w["mixin"])
    mixed_out.start()
    ql2, qlin, kro, krin = w["ql2"], w["qlin"], w["kro"], w["krin"]
    stageq, recvq = w["stageq"], w["recvq"]

    def out_copy(y, to):
        s = lax.rem(to + 8 - part, 8)
        rows = pl.ds(y * 16, 16)
        return pltpu.make_async_remote_copy(
            src_ref=kro.at[to, rows], dst_ref=krin.at[part, rows], send_sem=w["os"].at[y, 0, s], recv_sem=w["os"].at[y, 1, s],
            device_id=part_peer(s), device_id_type=MESH)

    mixed = over(3, HEADS, slot_peer, lambda s: w["stagem"].at[slot_at(s)], w["recvm"].at[slot])

    def group_out(n):
        lanes = pl.ds(pl.multiple_of(n * 128, 128), 128)
        return to_partner(5 + n, ql2.at[:, other, lanes], qlin.at[:, :, lanes])

    def half_out(h, n):
        @pl.loop(0, 8)
        def _(g):
            group_out(8 * h + g).wait()

        lanes = pl.ds(pl.multiple_of(h * 1024, 1024), 1024)
        total = (ql2[:, mine, lanes] + qlin[:, :, lanes]).astype(BF16).reshape(64, 1024)
        plain = dot(total, w["pt"][...])
        for c in range(CH):
            wide[n, c * 32:c * 32 + 32, :] = plain[0:32, c * 128:c * 128 + 128]
            wide[n, 256 + c * 32:288 + c * 32, :] = plain[32:64, c * 128:c * 128 + 128]
        for i in range(32):
            stageq[n, i // 2, :, (i % 2) * 128:(i % 2) * 128 + 128] = wide[n, pl.ds(i, 16, stride=32), :].astype(BF16)
        halves[n].start()
        recvq[h, slot] = stageq[n, slot]

    far = 1 - y_lo
    halves = [over(4 + 3 * n, HEADS, slot_peer, lambda s, n=n: stageq.at[n, slot_at(s)], recvq.at[h, slot]) for n, h in enumerate((far, y_lo))]

    @pl.loop(0, 8)
    def _(k):
        first, last_two, odd = 1 - (k + 6) // 8, k // 6, lax.rem(k, 2)
        between = 1 - first - last_two
        cy = lax.rem(y_lo + first + between * (1 - odd), 2)
        cx = lax.rem(x_lo + first + between * odd, 2)
        yh = (first + last_two) * odd + between * (k // 2 - 1)
        chip = cy * 2 + cx

        @pl.loop(0, 2)
        def _(j):
            n = 2 * (cy * 4 + j * 2 + cx) + yh
            backward(n, chip, yh * 16 + j * 2, f, ql2.at[0], ql2.at[1], kro, w)
            group_out(n).start()

        for c in range(2):
            to = 2 * chip + c

            @pl.when(to != part)
            def _():
                out_copy(yh, to).start()

        @pl.when(k == 7)
        def _():
            krin[part] = kro[part]

        @pl.when(k == 5)
        def _():
            half_out(far, 0)

        @pl.when(k == 1)
        def _():
            mixed_out.wait()
            mixf = w["mixf"]
            for c in range(CH):
                mixf[core, c * 32:c * 32 + 32, :] = w["mx"][c, mine, :].astype(F32)
                mixf[1 - core, c * 32:c * 32 + 32, :] = w["mixin"][c].astype(F32)
            to_pairs(mixf, w["stagem"], 8, 16)
            mixed.start()
            w["recvm"][slot] = w["stagem"][slot]

    @pl.loop(1, 8)
    def _(s):
        for y in range(2):
            out_copy(y, lax.rem(part + s, 8)).wait_recv()

    stage3, recv3 = w["stage3"], w["recv3"]
    for j in range(2):
        total = krin[j] + krin[2 + j] + krin[4 + j] + krin[6 + j]
        total = total.astype(BF16).reshape(16, 2, 16, 128)
        for a in range(2):
            stage3[:, :, j * 256 + a * 128:j * 256 + a * 128 + 128] = total[:, a]
    backs = over(8, HEADS, slot_peer, lambda s: stage3.at[slot_at(s)], recv3.at[slot])
    backs.start()
    recv3[slot] = stage3[slot]
    half_out(y_lo, 1)
    mixed.finish()
    gws = w["gws"]
    gws[:, 32:40, :] = dot(w["recvm"][...].reshape(256, 512), w["up"][...], NT).reshape(16, 16, 128)[:, 0:8]

    spans = (pl.ds(0, 16), pl.ds(16, 24))
    sums = [over(5 + 4 * n, HEADS, head_peer, lambda s, c=c: gws.at[head_at(s), c], w["gwin"].at[me, c]) for n, c in enumerate(spans)]
    image = None
    for n in (0, 1):
        if n:
            halves[0].finish()
            halves[1].finish()
            every = jnp.concatenate([recvq[0].reshape(256, 256), recvq[1].reshape(256, 256)], axis=1)
        else:
            backs.finish()
            every = recv3[...].reshape(256, 512)
        gws[:, 16 * n:16 * n + 16, :] = dot(every, w["xp"][...], NT).reshape(16, 16, 128)
        sums[n].start()
        term = dot(wall[:, 16 * n:16 * n + 16, :].reshape(256, 128), every, TN)
        image = term if image is None else image + term
    w["gwin"][me] = gws[me]
    image = image.reshape(16, 8, 512)
    w["stage4"][...] = jnp.concatenate([image[:, :, 0:256], image[:, :, 256:512]], axis=1).astype(BF16)
    images = over(6, HEADS, head_peer, lambda s: w["stage4"].at[head_at(s)], w["recv4"].at[me])
    images.start()
    w["recv4"][me] = w["stage4"][me]
    for trade in sums:
        trade.finish()
    total = w["gwin"][0]
    for p in range(1, HEADS):
        total = total + w["gwin"][p]
    w["part"][...] = total
    last = over(1, ROWS, row_peer, lambda s: w["part"], w["gwrow"].at[row])
    last.start()
    w["gwrow"][row] = total
    images.finish()
    for i in range(32):
        two = w["recv4"][i // 2, :, (i % 2) * 128:(i % 2) * 128 + 128].astype(F32)
        for z in range(2):
            wide[z, pl.ds(i, 8, stride=32), :] = two[z * 8:z * 8 + 8]
    for z in range(2):
        grads[:, :, z * 128:z * 128 + 128] = wide[z, 0:256, :].astype(BF16).reshape(8, 32, 128)
    last.finish()
    total = w["gwrow"][0]
    for p in range(1, ROWS):
        total = total + w["gwrow"][p]
    gw[...] = total * (1.0 / 256.0)
    for trade in (inputs, weights, mapped, mixed, *halves, backs, *sums, images, last):
        trade.drain()

    @pl.loop(0, 4)
    def _(g):
        near_copy(g).wait_send()

        @pl.loop(1, 8)
        def _(s):
            kr_copy(g, s).wait_send()

    @pl.loop(1, 8)
    def _(s):
        for y in range(2):
            out_copy(y, lax.rem(part + s, 8)).wait_send()


def results(grads, gw, out, gq, gk, gl, gr, go):
    out[...] = grads[...]
    for n, ref in enumerate((gk, gr, gq, gl, go)):
        ref[...] = gw[8 * n:8 * n + 8, :]


def layer_scratch():
    vmem, dma = pltpu.VMEM, pltpu.SemaphoreType.DMA
    return dict(
        core_scratch(),
        wide=vmem((2, 1024, 128), F32), wide2=vmem((2, 2048, 128), F32), wself=vmem((48, 128), BF16), wall=vmem((16, 48, 128), BF16),
        stage1=vmem((16, 16, 512), BF16), recv1=vmem((16, 16, 512), BF16), xp=vmem((128, 512), BF16), up=vmem((128, 512), BF16),
        stage2=vmem((16, 48, 512), BF16), recv2=vmem((16, 48, 512), BF16), near=vmem((16, 32, 512), BF16), mask=vmem((2, 32, 128), F32),
        kr=vmem((8, 16, 16, 256), BF16),
        ql2=vmem((2, 64, 2048), F32), qlin=vmem((2, 32, 2048), F32), kro=vmem((8, 32, 16, 128), F32), krin=vmem((8, 32, 16, 128), F32),
        mx=vmem((8, 64, 128), BF16), mixin=vmem((8, 32, 128), BF16), mixf=vmem((2, 256, 128), F32),
        stagem=vmem((16, 16, 512), BF16), recvm=vmem((16, 16, 512), BF16),
        stage3=vmem((16, 16, 512), BF16), recv3=vmem((16, 16, 512), BF16), stageq=vmem((2, 16, 16, 256), BF16), recvq=vmem((2, 16, 16, 256), BF16), stage4=vmem((16, 16, 256), BF16), recv4=vmem((16, 16, 256), BF16),
        gws=vmem((16, 40, 128), F32), gwin=vmem((16, 40, 128), F32), part=vmem((40, 128), F32), gwrow=vmem((8, 40, 128), F32),
        os=dma((2, 2, 8)), hs=dma((20, 16)), rs=dma((4, 8)), ps=dma((2, 21)), ks=dma((2, 4, 8)),
    )


def local(x, allowance, asking, lookup, first_content, second_content, final, scaling, upstream):
    vm = pl.BlockSpec(memory_space=pltpu.VMEM)
    names = layer_scratch()
    grads, gw = pl.pallas_call(
        functools.partial(layer, list(names)),
        out_shape=[jax.ShapeDtypeStruct((8, 32, 256), BF16), jax.ShapeDtypeStruct((40, 128), F32)],
        in_specs=[vm] * 8 + [pl.BlockSpec(memory_space=pltpu.SMEM)], out_specs=[vm] * 2,
        scratch_shapes=list(names.values()),
        compiler_params=pltpu.CompilerParams(collective_id=0, has_side_effects=True, vmem_limit_bytes=56 * 2 ** 20),
        name="layer",
    )(x, upstream, asking.T, lookup.T, first_content.T, second_content.T, final, allowance, scaling)
    grads, gq, gk, gl, gr, go = pl.pallas_call(
        results, out_shape=[jax.ShapeDtypeStruct((8, 32, 256), BF16)] + [jax.ShapeDtypeStruct((8, 128), F32)] * 5,
        in_specs=[vm] * 2, out_specs=[vm] * 6, name="results",
    )(grads, gw)
    return grads, gq.T, gk.T, gl.T, gr.T, go


def solution(mesh):
    pairs, columns = P("head", "row", None), P(None, "head")
    placed = (pairs, P("row", None), columns, columns, columns, columns, P("head", None), P("head"), pairs)
    return jax.shard_map(
        local, mesh=mesh, in_specs=placed,
        out_specs=(pairs, columns, columns, columns, columns, P("head", None)), check_vma=False,
    )
```

```python
import functools

import jax
import jax.numpy as jnp
from jax import lax
from jax.experimental import pallas as pl
from jax.experimental.pallas import tpu as pltpu
from jax.sharding import PartitionSpec as P

F32, BF16 = jnp.float32, jnp.bfloat16
MESH = pl.DeviceIdType.MESH
NT = (((1,), (1,)), ((), ()))
NN = (((1,), (0,)), ((), ()))
TN = (((0,), (0,)), ((), ()))
CH, I, L, J = 8, 64, 256, 128
HEADS, ROWS = 16, 8


def dot(a, b, dims=NN):
    return lax.dot_general(a, b, dims, preferred_element_type=F32)


def core_scratch():
    return dict(
        pt=pltpu.VMEM((1024, 1024), BF16),
        q2=pltpu.VMEM((I, 2048), BF16), b2=pltpu.VMEM((I, 2048), BF16),
        qt=pltpu.VMEM((2048, 128), BF16), kf=pltpu.VMEM((2048, J), F32), rf=pltpu.VMEM((2048, J), F32),
        k2=pltpu.VMEM((2048, J), BF16), mt=pltpu.VMEM((16, 256), BF16), wc=pltpu.VMEM((128, 1024), BF16), lb16=pltpu.VMEM((I, 2048), BF16),
        s=pltpu.VMEM((L, I, J), F32), m=pltpu.VMEM((I, J), F32), gs=pltpu.VMEM((CH, I, J), F32), ds=pltpu.VMEM((I, J), F32),

        e=pltpu.VMEM((16, I, J), F32), br8=pltpu.VMEM((16, 64, J), F32),
    )


def permutation(pt):
    @pl.loop(0, 8)
    def _(n):
        a = lax.broadcasted_iota(jnp.int32, (128, 1024), 0) + n * 128
        b = lax.broadcasted_iota(jnp.int32, (128, 1024), 1)
        hit = ((a >> 3) == (b & 127)) & ((a & 7) == (b >> 7))
        pt[pl.ds(pl.multiple_of(n * 128, 128), 128), :] = jnp.where(hit, 1.0, 0.0).astype(BF16)


def constants(w):
    permutation(w["pt"])
    row = lax.broadcasted_iota(jnp.int32, (16, 256), 0)
    lane = lax.broadcasted_iota(jnp.int32, (16, 256), 1)
    w["mt"][...] = jnp.where(((lane & 127) >> 3) == row, 1.0, 0.0).astype(BF16)
    ra = lax.broadcasted_iota(jnp.int32, (128, 1024), 0)
    rb_ = lax.broadcasted_iota(jnp.int32, (128, 1024), 1)
    w["wc"][...] = jnp.where((ra & 7) == (rb_ >> 7), 1.0, 0.0).astype(BF16)


def prepare(wide, w):
    pt = w["pt"]
    for half in range(2):
        out = slice(half * 1024, half * 1024 + 1024)
        qcat = jnp.concatenate([wide[half, c * I:c * I + I, :] for c in range(CH)], axis=1).astype(BF16)
        lcat = jnp.concatenate([wide[half, c * I:c * I + I, :] for c in range(CH, 2 * CH)], axis=1).astype(BF16)
        bcat = jnp.concatenate([wide[half, 24 * I:25 * I, :].astype(BF16), jnp.zeros((I, 896), BF16)], axis=1)
        got = dot(jnp.concatenate([qcat, lcat, bcat], axis=0), pt[...], NT)
        w["q2"][:, out] = got[:I].astype(BF16)
        w["lb16"][:, out] = got[I:2 * I].astype(BF16)
        w["b2"][:, out] = got[2 * I:].astype(BF16)
        w["qt"][out, :] = dot(pt[...], jnp.concatenate([qcat, qcat], axis=0), NT).astype(BF16)
    w["m"][...] = jnp.full((I, J), -3e38, F32)


def scores(n, w):
    at = pl.ds(pl.multiple_of(n * 128, 128), 128)
    k2 = w["kf"][at, :].astype(BF16)
    w["k2"][at, :] = k2
    qb = jnp.concatenate([w["q2"][:, at], w["b2"][:, at]], axis=1)
    kk = jnp.concatenate([k2, jnp.ones((128, J), BF16)], axis=0)
    lhs = jnp.concatenate([qb * w["mt"][t:t + 1, :] for t in range(16)], axis=0)
    raw = dot(lhs, kk).reshape(16, I, J)
    top = w["m"][...]
    for t in range(16):
        top = jnp.maximum(top, raw[t])
    w["m"][...] = top
    w["s"][pl.ds(n * 16, 16)] = raw


def forward(wide, mine, f, mixed, w):
    @pl.loop(0, 2)
    def _(ip):
        rows = pl.ds(pl.multiple_of(ip * 32, 32), 32)
        top = w["m"][rows, :]

        def step(n, carry):
            total, acc = carry
            acc = list(acc)
            tile = w["lb16"][rows, pl.ds(pl.multiple_of(n * 128, 128), 128)]
            lhs = jnp.concatenate([tile * w["mt"][t:t + 1, :128] for t in range(16)], axis=0)
            rg = w["rf"][pl.ds(pl.multiple_of(n * 128, 128), 128), :].astype(BF16)
            both = dot(lhs, jnp.concatenate([rg] * CH, axis=1) * w["wc"][...])
            for t in range(16):
                lv = n * 16 + t
                wt = jnp.exp(f * (w["s"][lv, rows, :] - top))
                w["s"][lv, rows, :] = wt
                total = total + wt
                for c in range(CH):
                    acc[c] = acc[c] + wt * both[t * 32:t * 32 + 32, c * 128:c * 128 + 128]
            return total, tuple(acc)

        zero = jnp.zeros((32, J), F32)
        total, acc = lax.fori_loop(0, 16, step, (zero, (zero,) * CH), unroll=4)
        inv = 1.0 / total
        delta = zero
        for c in range(CH):
            gc = wide[mine, pl.ds(pl.multiple_of((16 + c) * I + ip * 32, 32), 32), :]
            mc = acc[c] * inv
            mixed[c, rows, :] = mc.astype(BF16)
            delta = delta + gc * mc
            w["gs"][c, rows, :] = gc * inv
        w["ds"][rows, :] = delta * inv


def backward(n, chip, place, f, bq2, bl2, kro, w):
    at = pl.ds(pl.multiple_of(n * 128, 128), 128)
    bl2[:, at] = jnp.zeros((I, 128), F32)

    @pl.loop(0, 16, unroll=4)
    def _(t):
        lv = n * 16 + t
        lanes64 = lax.broadcasted_iota(jnp.int32, (I, 128), 1)
        pick = jnp.where((lanes64 >> 3) == t, 1.0, 0.0).astype(BF16)
        spread = dot(w["lb16"][:, at] * pick, w["wc"][...])
        rr = w["rf"][pl.ds(pl.multiple_of(lv * 8, 8), 8), :]
        rb = [jnp.broadcast_to(rr[c:c + 1, :], (16, J)) for c in range(CH)]
        br = [jnp.zeros((16, J), F32) for c in range(CH)]
        base = t * 8
        lanes16 = lax.broadcasted_iota(jnp.int32, (16, 128), 1)
        for it in range(4):
            rows = slice(it * 16, it * 16 + 16)
            wt = w["s"][lv, rows, :]
            blt = bl2[rows, at]
            pgp = None
            for c in range(CH):
                x = wt * w["gs"][c, rows, :]
                xl = x * spread[rows, c * 128:c * 128 + 128]
                br[c] = br[c] + xl
                term = xl * rb[c]
                pgp = term if pgp is None else pgp + term
                red = jnp.sum(x * rb[c], axis=1, keepdims=True)
                blt = jnp.where(lanes16 == base + c, red, blt)
            w["e"][t, rows, :] = pgp - wt * w["ds"][rows, :]
            bl2[rows, at] = blt
        for c in range(CH):
            w["br8"][t, c * 8:c * 8 + 8, :] = br[c][:8] + br[c][8:]

    for t in range(16):
        tot = w["br8"][t, pl.ds(0, 8, stride=8), :]
        for z in range(1, 8):
            tot = tot + w["br8"][t, pl.ds(z, 8, stride=8), :]
        kro[2 * chip + (t // 2) % 2, place + (t // 4) * 4 + t % 2, 8:16, :] = tot
    ev = w["e"][...].reshape(16 * I, J)
    hi = ev.astype(BF16)
    lo = (ev - hi.astype(F32)).astype(BF16)
    kt = w["k2"][at, :]
    bqw = dot(jnp.concatenate([hi, lo], axis=1), jnp.concatenate([kt, kt], axis=1), NT)
    tot = jnp.zeros((I, 128), F32)
    lane2 = lax.broadcasted_iota(jnp.int32, (I, 128), 1)
    for t in range(16):
        tot = jnp.where((lane2 >> 3) == t, bqw[t * I:(t + 1) * I, :], tot)
    bq2[:, at] = f * tot
    sub_r = lax.broadcasted_iota(jnp.int32, (32, 256), 0)
    sub_c = lax.broadcasted_iota(jnp.int32, (32, 256), 1)
    keep = jnp.where((sub_r >> 3) == (sub_c >> 6), 1.0, 0.0).astype(BF16)
    for u in range(4):
        qrow = w["qt"][pl.ds(pl.multiple_of(n * 128 + u * 32, 32), 32), :]
        lhs = jnp.concatenate([qrow, qrow], axis=1) * keep
        part = dot(jnp.concatenate([lhs, lhs], axis=1), jnp.concatenate([hi[u * 256:u * 256 + 256], lo[u * 256:u * 256 + 256]], axis=0))
        part = f * part
        for core in range(2):
            for a in range(2):
                first = (core * 2 + a) * 8
                kro[2 * chip + core, place + u * 4 + a, 0:8, :] = part[first:first + 8]


def greet(groups):
    barrier = pltpu.get_barrier_semaphore()
    for n, peer in groups:
        @pl.loop(1, n)
        def _(s):
            pl.semaphore_signal(barrier, inc=1, device_id=peer(s), device_id_type=MESH)


class Trade:
    def __init__(self, n, peer, src, dst, send_sem, recv_sem):
        self.n, self.peer, self.src, self.dst, self.send_sem, self.recv_sem = n, peer, src, dst, send_sem, recv_sem

    def copy(self, s):
        return pltpu.make_async_remote_copy(
            src_ref=self.src(s), dst_ref=self.dst, send_sem=self.send_sem.at[s], recv_sem=self.recv_sem.at[s],
            device_id=self.peer(s), device_id_type=MESH)

    def start(self):
        @pl.loop(1, self.n)
        def _(s):
            self.copy(s).start()

    def finish(self):
        @pl.loop(1, self.n)
        def _(s):
            self.copy(s).wait_recv()

    def drain(self):
        @pl.loop(1, self.n)
        def _(s):
            self.copy(s).wait_send()


def lane_of(i, z):
    return z * 256 + (i % 2) * 128


def to_pairs(wide, stage, count, rows, first=0):
    for i in range(32):
        for z in range(2):
            at = lane_of(i, z)
            piece = wide[z, pl.ds(i, count, stride=32), :]
            if count % 16:
                piece = jnp.concatenate([piece, jnp.zeros((16 - count % 16, 128), F32)], axis=0)
            stage[i // 2, first:first + rows, at:at + 128] = piece.astype(BF16)


def from_pairs(recv, lo, hi, wide, offset, stride, first=0, count=16):
    for i in range(2 * count):
        for z in range(2):
            at = lane_of(i, z)
            rows = pl.ds(offset + first * 2 + i, hi - lo, stride=stride)
            wide[z, rows, :] = recv[first + i // 2, lo:hi, at:at + 128].astype(F32)


def layer(names, x, u, wq, wk, wl, wr, wf, allowance, fac, grads, gw, *scratch):
    w = dict(zip(names, scratch))
    me, row = lax.axis_index("head"), lax.axis_index("row")
    core = lax.rem(me, 2)
    x_hi, x_lo, y_lo = lax.rem(row // 2, 2), lax.rem(row, 2), row // 4
    slot = (me // 2) * 2 + x_hi
    part = y_lo * 4 + x_lo * 2 + core
    block = part // 2

    def head_peer(s):
        return {"head": lax.rem(me + s, HEADS), "row": row}

    def row_peer(s):
        return {"head": me, "row": lax.rem(row + s, ROWS)}

    def slot_at(s):
        return lax.rem(slot // 4 + s // 4, 4) * 4 + lax.rem(slot + s, 4)

    def slot_peer(s):
        to = slot_at(s)
        return {"head": (to // 2) * 2 + core, "row": y_lo * 4 + lax.rem(to, 2) * 2 + x_lo}

    def part_peer(s):
        to = lax.rem(part + s, 8)
        return {"head": (me // 2) * 2 + lax.rem(to, 2), "row": (to // 4) * 4 + x_hi * 2 + lax.rem(to // 2, 2)}

    partner = {"head": me + 1 - 2 * core, "row": row}
    hs, rs, ps = w["hs"], w["rs"], w["ps"]

    def over(n, size, peer, src, dst):
        sems = hs if size == HEADS else rs
        return Trade(size, peer, src, dst, sems.at[2 * n], sems.at[2 * n + 1])

    def to_partner(n, src, dst):
        return pltpu.make_async_remote_copy(src_ref=src, dst_ref=dst, send_sem=ps.at[0, n], recv_sem=ps.at[1, n],
                                            device_id=partner, device_id_type=MESH)

    def head_at(s):
        return lax.rem(me + s, HEADS)

    greet([(HEADS, head_peer), (ROWS, row_peer), (HEADS, slot_peer), (8, part_peer)])
    wall, wide, stage1, recv1 = w["wall"], w["wide"], w["stage1"], w["recv1"]
    f0 = jnp.full((8, 128), fac[0], F32)
    f1 = f0 - f0.astype(BF16).astype(F32)
    f2 = f1 - f1.astype(BF16).astype(F32)
    tile = lax.broadcasted_iota(jnp.int32, (8, 128), 0)
    factor = jnp.where(tile == 0, f0, jnp.where(tile == 1, f1, jnp.where(tile == 2, f2, 0.0)))
    pairs = ((wk[...], wr[...]), (wq[...], wl[...]), (wf[...], factor.astype(BF16)))
    weights = jnp.concatenate([jnp.concatenate(pair, axis=0) for pair in pairs], axis=1)
    for p in range(HEADS):
        stage1[p, :, 512:896] = weights
    for z in range(2):
        wide[z, 0:256, :] = x[:, :, z * 128:z * 128 + 128].reshape(256, 128).astype(F32)
        wide[z, 256:512, :] = u[:, :, z * 128:z * 128 + 128].reshape(256, 128).astype(F32)
    to_pairs(wide, stage1, 16, 16)
    pl.semaphore_wait(pltpu.get_barrier_semaphore(), 2 * HEADS + ROWS + 8 - 4)
    inputs = over(0, HEADS, head_peer, lambda s: stage1.at[head_at(s)], recv1.at[me])
    inputs.start()
    recv1[me] = stage1[me]
    constants(w)
    node = row * 32 + lax.broadcasted_iota(jnp.int32, (32, 128), 0)
    column = lax.broadcasted_iota(jnp.int32, (32, 128), 1)
    for z in range(2):
        valid = (allowance[:, z * 128:z * 128 + 128] == 1) | (node == column + z * 128)
        w["mask"][z] = jnp.where(valid, 0.0, -1e30)
    bias = jnp.concatenate([w["mask"][z, pl.ds(2 * me + a, 1), :] for z in range(2) for a in range(2)], axis=1)
    bias = jnp.broadcast_to(bias, (8, 512))
    inputs.finish()
    for n in range(3):
        wall[:, 16 * n:16 * n + 16, :] = recv1[:, :, 512 + 128 * n:640 + 128 * n]
    both = recv1[:, :, 0:512].astype(F32)
    w["xp"][...] = both[:, 0:8].reshape(128, 512).astype(BF16)
    w["up"][...] = both[:, 8:16].reshape(128, 512).astype(BF16)

    stage2, recv2, kr = w["stage2"], w["recv2"], w["kr"]
    mapped = over(2, HEADS, slot_peer, lambda s: stage2.at[slot_at(s)], recv2.at[slot])
    for first in range(0, HEADS, 4):
        peers = [slot_at(first + a) for a in range(4)]
        of_x = dot(jnp.concatenate([wall[p, 0:32] for p in peers], axis=0), w["xp"][...]).astype(BF16)
        of_u = dot(jnp.concatenate([wall[p, 32:48] for p in peers], axis=0), w["up"][...])
        for a, p in enumerate(peers):
            stage2[p, 0:32] = of_x[a * 32:a * 32 + 32]
            stage2[p, 32:48] = jnp.concatenate([of_u[a * 16:a * 16 + 8], bias], axis=0).astype(BF16)
            if first + a:
                mapped.copy(first + a).start()
            else:
                recv2[slot] = stage2[slot]

    near, wide2 = w["near"], w["wide2"]

    def four(g):
        return lax.rem(slot // 4 + 4 - g, 4) * 4

    def kr_copy(g, s):
        some = pl.ds(four(g), 4)
        to = lax.rem(part + s, 8)
        return pltpu.make_async_remote_copy(
            src_ref=recv2.at[some, pl.ds(0, 16), pl.ds(pl.multiple_of(lax.rem(to, 2) * 256, 128), 256)], dst_ref=kr.at[part, some],
            send_sem=w["ks"].at[0, g, s], recv_sem=w["ks"].at[1, g, s], device_id=part_peer(s), device_id_type=MESH)

    def near_copy(g):
        some = pl.ds(four(g), 4)
        return to_partner(g, recv2.at[some, pl.ds(16, 32)], near.at[some])

    def unpack_near(g):
        near_copy(g).wait_recv()
        from_pairs(near, 0, 32, wide2, 32 - core * 32, I, four(g), 4)

    @pl.loop(0, 4)
    def _(g):
        @pl.loop(0, 4)
        def _(a):
            @pl.when(g * 4 + a > 0)
            def _():
                mapped.copy(g * 4 + a).wait_recv()

        near_copy(g).start()

        @pl.loop(1, 8)
        def _(s):
            kr_copy(g, s).start()

        from_pairs(recv2, 16, 48, wide2, core * 32, I, four(g), 4)

        @pl.when(g > 0)
        def _():
            unpack_near(g - 1)

    unpack_near(3)
    own = pl.multiple_of(core * 32, 32)
    prepare(wide2, w)

    f = jnp.sum(wall[slot, 32:48].astype(F32)[8:16], axis=0, keepdims=True)

    def groups(chip):
        for hi in range(2):
            for y in range(2):
                yield 2 * ((chip // 2) * 4 + hi * 2 + lax.rem(chip, 2)) + y, y * 8 + hi

    @pl.loop(0, 4)
    def _(k):
        chip = lax.rem(block + 4 - k, 4)
        for c in range(2):
            @pl.when(2 * chip + c != part)
            def _():
                @pl.loop(0, 4)
                def _(g):
                    kr_copy(g, lax.rem(part + 8 - 2 * chip - c, 8)).wait_recv()

            @pl.when(2 * chip + c == part)
            def _():
                kr[part] = recv2[:, 0:16, pl.ds(pl.multiple_of(core * 256, 128), 256)]

        for n, first in groups(chip):
            for t in range(16):
                at = (first + (t // 4) * 2)
                tile = kr[2 * chip + (t // 2) % 2, at, :, (t % 2) * 128:(t % 2) * 128 + 128].astype(F32)
                rows = pl.ds(pl.multiple_of(n * 128 + t * 8, 8), 8)
                w["kf"][rows, :] = tile[0:8]
                w["rf"][rows, :] = tile[8:16]
            scores(n, w)

    forward(wide2, core, f, w["mx"], w)
    mine, other = pl.ds(own, 32), pl.ds(pl.multiple_of(32 - core * 32, 32), 32)
    mixed_out = to_partner(4, w["mx"].at[:, other], w["mixin"])
    mixed_out.start()
    ql2, qlin, kro, krin = w["ql2"], w["qlin"], w["kro"], w["krin"]
    stageq, recvq = w["stageq"], w["recvq"]

    def out_copy(y, to):
        s = lax.rem(to + 8 - part, 8)
        rows = pl.ds(y * 16, 16)
        return pltpu.make_async_remote_copy(
            src_ref=kro.at[to, rows], dst_ref=krin.at[part, rows], send_sem=w["os"].at[y, 0, s], recv_sem=w["os"].at[y, 1, s],
            device_id=part_peer(s), device_id_type=MESH)

    mixed = over(3, HEADS, slot_peer, lambda s: w["stagem"].at[slot_at(s)], w["recvm"].at[slot])

    def group_out(n):
        lanes = pl.ds(pl.multiple_of(n * 128, 128), 128)
        return to_partner(5 + n, ql2.at[:, other, lanes], qlin.at[:, :, lanes])

    def half_out(h, n):
        @pl.loop(0, 8)
        def _(g):
            group_out(8 * h + g).wait()

        lanes = pl.ds(pl.multiple_of(h * 1024, 1024), 1024)
        total = (ql2[:, mine, lanes] + qlin[:, :, lanes]).astype(BF16).reshape(64, 1024)
        plain = dot(total, w["pt"][...])
        for c in range(CH):
            wide[n, c * 32:c * 32 + 32, :] = plain[0:32, c * 128:c * 128 + 128]
            wide[n, 256 + c * 32:288 + c * 32, :] = plain[32:64, c * 128:c * 128 + 128]
        for i in range(32):
            stageq[n, i // 2, :, (i % 2) * 128:(i % 2) * 128 + 128] = wide[n, pl.ds(i, 16, stride=32), :].astype(BF16)
        halves[n].start()
        recvq[h, slot] = stageq[n, slot]

    far = 1 - y_lo
    halves = [over(4 + 3 * n, HEADS, slot_peer, lambda s, n=n: stageq.at[n, slot_at(s)], recvq.at[h, slot]) for n, h in enumerate((far, y_lo))]

    @pl.loop(0, 8)
    def _(k):
        first, last_two, odd = 1 - (k + 6) // 8, k // 6, lax.rem(k, 2)
        between = 1 - first - last_two
        cy = lax.rem(y_lo + first + between * (1 - odd), 2)
        cx = lax.rem(x_lo + first + between * odd, 2)
        yh = (first + last_two) * odd + between * (k // 2 - 1)
        chip = cy * 2 + cx

        @pl.loop(0, 2)
        def _(j):
            n = 2 * (cy * 4 + j * 2 + cx) + yh
            backward(n, chip, yh * 16 + j * 2, f, ql2.at[0], ql2.at[1], kro, w)
            group_out(n).start()

        for c in range(2):
            to = 2 * chip + c

            @pl.when(to != part)
            def _():
                out_copy(yh, to).start()

        @pl.when(k == 7)
        def _():
            krin[part] = kro[part]

        @pl.when(k == 5)
        def _():
            half_out(far, 0)

        @pl.when(k == 1)
        def _():
            mixed_out.wait()
            mixf = w["mixf"]
            for c in range(CH):
                mixf[core, c * 32:c * 32 + 32, :] = w["mx"][c, mine, :].astype(F32)
                mixf[1 - core, c * 32:c * 32 + 32, :] = w["mixin"][c].astype(F32)
            to_pairs(mixf, w["stagem"], 8, 16)
            mixed.start()
            w["recvm"][slot] = w["stagem"][slot]

    @pl.loop(1, 8)
    def _(s):
        for y in range(2):
            out_copy(y, lax.rem(part + s, 8)).wait_recv()

    stage3, recv3 = w["stage3"], w["recv3"]
    for j in range(2):
        total = krin[j] + krin[2 + j] + krin[4 + j] + krin[6 + j]
        total = total.astype(BF16).reshape(16, 2, 16, 128)
        for a in range(2):
            stage3[:, :, j * 256 + a * 128:j * 256 + a * 128 + 128] = total[:, a]
    backs = over(8, HEADS, slot_peer, lambda s: stage3.at[slot_at(s)], recv3.at[slot])
    backs.start()
    recv3[slot] = stage3[slot]
    half_out(y_lo, 1)
    mixed.finish()
    gws = w["gws"]
    gws[:, 32:40, :] = dot(w["recvm"][...].reshape(256, 512), w["up"][...], NT).reshape(16, 16, 128)[:, 0:8]

    spans = (pl.ds(0, 16), pl.ds(16, 24))
    sums = [over(5 + 4 * n, HEADS, head_peer, lambda s, c=c: gws.at[head_at(s), c], w["gwin"].at[me, c]) for n, c in enumerate(spans)]
    image = None
    for n in (0, 1):
        if n:
            halves[0].finish()
            halves[1].finish()
            every = jnp.concatenate([recvq[0].reshape(256, 256), recvq[1].reshape(256, 256)], axis=1)
        else:
            backs.finish()
            every = recv3[...].reshape(256, 512)
        gws[:, 16 * n:16 * n + 16, :] = dot(every, w["xp"][...], NT).reshape(16, 16, 128)
        sums[n].start()
        term = dot(wall[:, 16 * n:16 * n + 16, :].reshape(256, 128), every, TN)
        image = term if image is None else image + term
    w["gwin"][me] = gws[me]
    image = image.reshape(16, 8, 512)
    w["stage4"][...] = jnp.concatenate([image[:, :, 0:256], image[:, :, 256:512]], axis=1).astype(BF16)
    images = over(6, HEADS, head_peer, lambda s: w["stage4"].at[head_at(s)], w["recv4"].at[me])
    images.start()
    w["recv4"][me] = w["stage4"][me]
    for trade in sums:
        trade.finish()
    total = w["gwin"][0]
    for p in range(1, HEADS):
        total = total + w["gwin"][p]
    w["part"][...] = total
    last = over(1, ROWS, row_peer, lambda s: w["part"], w["gwrow"].at[row])
    last.start()
    w["gwrow"][row] = total
    images.finish()
    for i in range(32):
        two = w["recv4"][i // 2, :, (i % 2) * 128:(i % 2) * 128 + 128].astype(F32)
        for z in range(2):
            wide[z, pl.ds(i, 8, stride=32), :] = two[z * 8:z * 8 + 8]
    for z in range(2):
        grads[:, :, z * 128:z * 128 + 128] = wide[z, 0:256, :].astype(BF16).reshape(8, 32, 128)
    last.finish()
    total = w["gwrow"][0]
    for p in range(1, ROWS):
        total = total + w["gwrow"][p]
    gw[...] = total * (1.0 / 256.0)
    for trade in (inputs, mapped, mixed, *halves, backs, *sums, images, last):
        trade.drain()

    @pl.loop(0, 4)
    def _(g):
        near_copy(g).wait_send()

        @pl.loop(1, 8)
        def _(s):
            kr_copy(g, s).wait_send()

    @pl.loop(1, 8)
    def _(s):
        for y in range(2):
            out_copy(y, lax.rem(part + s, 8)).wait_send()


def results(grads, gw, out, gq, gk, gl, gr, go):
    out[...] = grads[...]
    for n, ref in enumerate((gk, gr, gq, gl, go)):
        ref[...] = gw[8 * n:8 * n + 8, :]


def layer_scratch():
    vmem, dma = pltpu.VMEM, pltpu.SemaphoreType.DMA
    return dict(
        core_scratch(),
        wide=vmem((2, 1024, 128), F32), wide2=vmem((2, 2048, 128), F32), wall=vmem((16, 48, 128), BF16),
        stage1=vmem((16, 16, 896), BF16), recv1=vmem((16, 16, 896), BF16), xp=vmem((128, 512), BF16), up=vmem((128, 512), BF16),
        stage2=vmem((16, 48, 512), BF16), recv2=vmem((16, 48, 512), BF16), near=vmem((16, 32, 512), BF16), mask=vmem((2, 32, 128), F32),
        kr=vmem((8, 16, 16, 256), BF16),
        ql2=vmem((2, 64, 2048), F32), qlin=vmem((2, 32, 2048), F32), kro=vmem((8, 32, 16, 128), F32), krin=vmem((8, 32, 16, 128), F32),
        mx=vmem((8, 64, 128), BF16), mixin=vmem((8, 32, 128), BF16), mixf=vmem((2, 256, 128), F32),
        stagem=vmem((16, 16, 512), BF16), recvm=vmem((16, 16, 512), BF16),
        stage3=vmem((16, 16, 512), BF16), recv3=vmem((16, 16, 512), BF16), stageq=vmem((2, 16, 16, 256), BF16), recvq=vmem((2, 16, 16, 256), BF16), stage4=vmem((16, 16, 256), BF16), recv4=vmem((16, 16, 256), BF16),
        gws=vmem((16, 40, 128), F32), gwin=vmem((16, 40, 128), F32), part=vmem((40, 128), F32), gwrow=vmem((8, 40, 128), F32),
        os=dma((2, 2, 8)), hs=dma((20, 16)), rs=dma((4, 8)), ps=dma((2, 21)), ks=dma((2, 4, 8)),
    )


def local(x, allowance, asking, lookup, first_content, second_content, final, scaling, upstream):
    vm = pl.BlockSpec(memory_space=pltpu.VMEM)
    names = layer_scratch()
    grads, gw = pl.pallas_call(
        functools.partial(layer, list(names)),
        out_shape=[jax.ShapeDtypeStruct((8, 32, 256), BF16), jax.ShapeDtypeStruct((40, 128), F32)],
        in_specs=[vm] * 8 + [pl.BlockSpec(memory_space=pltpu.SMEM)], out_specs=[vm] * 2,
        scratch_shapes=list(names.values()),
        compiler_params=pltpu.CompilerParams(collective_id=0, has_side_effects=True, vmem_limit_bytes=56 * 2 ** 20),
        name="layer",
    )(x, upstream, asking.T, lookup.T, first_content.T, second_content.T, final, allowance, scaling)
    grads, gq, gk, gl, gr, go = pl.pallas_call(
        results, out_shape=[jax.ShapeDtypeStruct((8, 32, 256), BF16)] + [jax.ShapeDtypeStruct((8, 128), F32)] * 5,
        in_specs=[vm] * 2, out_specs=[vm] * 6, name="results",
    )(grads, gw)
    return grads, gq.T, gk.T, gl.T, gr.T, go


def solution(mesh):
    pairs, columns = P("head", "row", None), P(None, "head")
    placed = (pairs, P("row", None), columns, columns, columns, columns, P("head", None), P("head"), pairs)
    return jax.shard_map(
        local, mesh=mesh, in_specs=placed,
        out_specs=(pairs, columns, columns, columns, columns, P("head", None)), check_vma=False,
    )
```

```python
import functools

import jax
import jax.numpy as jnp
from jax import lax
from jax.experimental import pallas as pl
from jax.experimental.pallas import tpu as pltpu
from jax.sharding import PartitionSpec as P

F32, BF16 = jnp.float32, jnp.bfloat16
MESH = pl.DeviceIdType.MESH
NT = (((1,), (1,)), ((), ()))
NN = (((1,), (0,)), ((), ()))
TN = (((0,), (0,)), ((), ()))
CH, I, L, J = 8, 64, 256, 128
HEADS, ROWS = 16, 8


def dot(a, b, dims=NN):
    return lax.dot_general(a, b, dims, preferred_element_type=F32)


def core_scratch():
    return dict(
        pt=pltpu.VMEM((1024, 1024), BF16),
        q2=pltpu.VMEM((I, 2048), BF16), b2=pltpu.VMEM((I, 2048), BF16),
        qt=pltpu.VMEM((2048, 128), BF16), kf=pltpu.VMEM((2048, J), F32), rf=pltpu.VMEM((2048, J), F32),
        k2=pltpu.VMEM((2048, J), BF16), mt=pltpu.VMEM((16, 256), BF16), wc=pltpu.VMEM((128, 1024), BF16), lb16=pltpu.VMEM((I, 2048), BF16),
        s=pltpu.VMEM((L, I, J), F32), m=pltpu.VMEM((I, J), F32), gs=pltpu.VMEM((CH, I, J), F32), ds=pltpu.VMEM((I, J), F32),

        e=pltpu.VMEM((16, I, J), F32), br8=pltpu.VMEM((16, 64, J), F32),
    )


def permutation(pt):
    @pl.loop(0, 8)
    def _(n):
        a = lax.broadcasted_iota(jnp.int32, (128, 1024), 0) + n * 128
        b = lax.broadcasted_iota(jnp.int32, (128, 1024), 1)
        hit = ((a >> 3) == (b & 127)) & ((a & 7) == (b >> 7))
        pt[pl.ds(pl.multiple_of(n * 128, 128), 128), :] = jnp.where(hit, 1.0, 0.0).astype(BF16)


def constants(w):
    permutation(w["pt"])
    row = lax.broadcasted_iota(jnp.int32, (16, 256), 0)
    lane = lax.broadcasted_iota(jnp.int32, (16, 256), 1)
    w["mt"][...] = jnp.where(((lane & 127) >> 3) == row, 1.0, 0.0).astype(BF16)
    ra = lax.broadcasted_iota(jnp.int32, (128, 1024), 0)
    rb_ = lax.broadcasted_iota(jnp.int32, (128, 1024), 1)
    w["wc"][...] = jnp.where((ra & 7) == (rb_ >> 7), 1.0, 0.0).astype(BF16)


def prepare(wide, w):
    pt = w["pt"]
    for half in range(2):
        out = slice(half * 1024, half * 1024 + 1024)
        qcat = jnp.concatenate([wide[half, c * I:c * I + I, :] for c in range(CH)], axis=1).astype(BF16)
        lcat = jnp.concatenate([wide[half, c * I:c * I + I, :] for c in range(CH, 2 * CH)], axis=1).astype(BF16)
        bcat = jnp.concatenate([wide[half, 24 * I:25 * I, :].astype(BF16), jnp.zeros((I, 896), BF16)], axis=1)
        got = dot(jnp.concatenate([qcat, lcat, bcat], axis=0), pt[...], NT)
        w["q2"][:, out] = got[:I].astype(BF16)
        w["lb16"][:, out] = got[I:2 * I].astype(BF16)
        w["b2"][:, out] = got[2 * I:].astype(BF16)
        w["qt"][out, :] = dot(pt[...], jnp.concatenate([qcat, qcat], axis=0), NT).astype(BF16)
    w["m"][...] = jnp.full((I, J), -3e38, F32)


def scores(n, w):
    at = pl.ds(pl.multiple_of(n * 128, 128), 128)
    k2 = w["kf"][at, :].astype(BF16)
    w["k2"][at, :] = k2
    qb = jnp.concatenate([w["q2"][:, at], w["b2"][:, at]], axis=1)
    kk = jnp.concatenate([k2, jnp.ones((128, J), BF16)], axis=0)
    lhs = jnp.concatenate([qb * w["mt"][t:t + 1, :] for t in range(16)], axis=0)
    raw = dot(lhs, kk).reshape(16, I, J)
    top = w["m"][...]
    for t in range(16):
        top = jnp.maximum(top, raw[t])
    w["m"][...] = top
    w["s"][pl.ds(n * 16, 16)] = raw


def forward(wide, mine, f, mixed, w):
    @pl.loop(0, 2)
    def _(ip):
        rows = pl.ds(pl.multiple_of(ip * 32, 32), 32)
        top = w["m"][rows, :]

        def step(n, carry):
            total, acc = carry
            acc = list(acc)
            tile = w["lb16"][rows, pl.ds(pl.multiple_of(n * 128, 128), 128)]
            lhs = jnp.concatenate([tile * w["mt"][t:t + 1, :128] for t in range(16)], axis=0)
            rg = w["rf"][pl.ds(pl.multiple_of(n * 128, 128), 128), :].astype(BF16)
            both = dot(lhs, jnp.concatenate([rg] * CH, axis=1) * w["wc"][...])
            for t in range(16):
                lv = n * 16 + t
                wt = jnp.exp(f * (w["s"][lv, rows, :] - top))
                w["s"][lv, rows, :] = wt
                total = total + wt
                for c in range(CH):
                    acc[c] = acc[c] + wt * both[t * 32:t * 32 + 32, c * 128:c * 128 + 128]
            return total, tuple(acc)

        zero = jnp.zeros((32, J), F32)
        total, acc = lax.fori_loop(0, 16, step, (zero, (zero,) * CH), unroll=4)
        inv = 1.0 / total
        delta = zero
        for c in range(CH):
            gc = wide[mine, pl.ds(pl.multiple_of((16 + c) * I + ip * 32, 32), 32), :]
            mc = acc[c] * inv
            mixed[c, rows, :] = mc.astype(BF16)
            delta = delta + gc * mc
            w["gs"][c, rows, :] = gc * inv
        w["ds"][rows, :] = delta * inv


def backward(n, chip, place, f, bq2, bl2, kro, w):
    at = pl.ds(pl.multiple_of(n * 128, 128), 128)
    bl2[:, at] = jnp.zeros((I, 128), F32)

    @pl.loop(0, 16, unroll=4)
    def _(t):
        lv = n * 16 + t
        lanes64 = lax.broadcasted_iota(jnp.int32, (I, 128), 1)
        pick = jnp.where((lanes64 >> 3) == t, 1.0, 0.0).astype(BF16)
        spread = dot(w["lb16"][:, at] * pick, w["wc"][...])
        rr = w["rf"][pl.ds(pl.multiple_of(lv * 8, 8), 8), :]
        rb = [jnp.broadcast_to(rr[c:c + 1, :], (16, J)) for c in range(CH)]
        br = [jnp.zeros((16, J), F32) for c in range(CH)]
        base = t * 8
        lanes16 = lax.broadcasted_iota(jnp.int32, (16, 128), 1)
        for it in range(4):
            rows = slice(it * 16, it * 16 + 16)
            wt = w["s"][lv, rows, :]
            blt = bl2[rows, at]
            pgp = None
            for c in range(CH):
                x = wt * w["gs"][c, rows, :]
                xl = x * spread[rows, c * 128:c * 128 + 128]
                br[c] = br[c] + xl
                term = xl * rb[c]
                pgp = term if pgp is None else pgp + term
                red = jnp.sum(x * rb[c], axis=1, keepdims=True)
                blt = jnp.where(lanes16 == base + c, red, blt)
            w["e"][t, rows, :] = pgp - wt * w["ds"][rows, :]
            bl2[rows, at] = blt
        for c in range(CH):
            w["br8"][t, c * 8:c * 8 + 8, :] = br[c][:8] + br[c][8:]

    for t in range(16):
        tot = w["br8"][t, pl.ds(0, 8, stride=8), :]
        for z in range(1, 8):
            tot = tot + w["br8"][t, pl.ds(z, 8, stride=8), :]
        kro[2 * chip + (t // 2) % 2, place + (t // 4) * 4 + t % 2, 8:16, :] = tot
    ev = w["e"][...].reshape(16 * I, J)
    hi = ev.astype(BF16)
    lo = (ev - hi.astype(F32)).astype(BF16)
    kt = w["k2"][at, :]
    bqw = dot(jnp.concatenate([hi, lo], axis=1), jnp.concatenate([kt, kt], axis=1), NT)
    tot = jnp.zeros((I, 128), F32)
    lane2 = lax.broadcasted_iota(jnp.int32, (I, 128), 1)
    for t in range(16):
        tot = jnp.where((lane2 >> 3) == t, bqw[t * I:(t + 1) * I, :], tot)
    bq2[:, at] = f * tot
    sub_r = lax.broadcasted_iota(jnp.int32, (32, 256), 0)
    sub_c = lax.broadcasted_iota(jnp.int32, (32, 256), 1)
    keep = jnp.where((sub_r >> 3) == (sub_c >> 6), 1.0, 0.0).astype(BF16)
    for u in range(4):
        qrow = w["qt"][pl.ds(pl.multiple_of(n * 128 + u * 32, 32), 32), :]
        lhs = jnp.concatenate([qrow, qrow], axis=1) * keep
        part = dot(jnp.concatenate([lhs, lhs], axis=1), jnp.concatenate([hi[u * 256:u * 256 + 256], lo[u * 256:u * 256 + 256]], axis=0))
        part = f * part
        for core in range(2):
            for a in range(2):
                first = (core * 2 + a) * 8
                kro[2 * chip + core, place + u * 4 + a, 0:8, :] = part[first:first + 8]


def greet(groups):
    barrier = pltpu.get_barrier_semaphore()
    for n, peer in groups:
        @pl.loop(1, n)
        def _(s):
            pl.semaphore_signal(barrier, inc=1, device_id=peer(s), device_id_type=MESH)


class Trade:
    def __init__(self, n, peer, src, dst, send_sem, recv_sem):
        self.n, self.peer, self.src, self.dst, self.send_sem, self.recv_sem = n, peer, src, dst, send_sem, recv_sem

    def copy(self, s):
        return pltpu.make_async_remote_copy(
            src_ref=self.src(s), dst_ref=self.dst, send_sem=self.send_sem.at[s], recv_sem=self.recv_sem.at[s],
            device_id=self.peer(s), device_id_type=MESH)

    def start(self):
        @pl.loop(1, self.n)
        def _(s):
            self.copy(s).start()

    def finish(self):
        @pl.loop(1, self.n)
        def _(s):
            self.copy(s).wait_recv()

    def drain(self):
        @pl.loop(1, self.n)
        def _(s):
            self.copy(s).wait_send()


def lane_of(i, z):
    return z * 256 + (i % 2) * 128


def to_pairs(wide, stage, count, rows, first=0):
    for i in range(32):
        for z in range(2):
            at = lane_of(i, z)
            piece = wide[z, pl.ds(i, count, stride=32), :]
            if count % 16:
                piece = jnp.concatenate([piece, jnp.zeros((16 - count % 16, 128), F32)], axis=0)
            stage[i // 2, first:first + rows, at:at + 128] = piece.astype(BF16)


def from_pairs(recv, lo, hi, wide, offset, stride, first=0, count=16):
    for i in range(2 * count):
        for z in range(2):
            at = lane_of(i, z)
            rows = pl.ds(offset + first * 2 + i, hi - lo, stride=stride)
            wide[z, rows, :] = recv[first + i // 2, lo:hi, at:at + 128].astype(F32)


def layer(names, x, u, wq, wk, wl, wr, wf, allowance, fac, grads, gw, *scratch):
    w = dict(zip(names, scratch))
    me, row = lax.axis_index("head"), lax.axis_index("row")
    core = lax.rem(me, 2)
    x_hi, x_lo, y_lo = lax.rem(row // 2, 2), lax.rem(row, 2), row // 4
    slot = (me // 2) * 2 + x_hi
    part = y_lo * 4 + x_lo * 2 + core
    block = part // 2

    def head_peer(s):
        return {"head": lax.rem(me + s, HEADS), "row": row}

    def row_peer(s):
        return {"head": me, "row": lax.rem(row + s, ROWS)}

    def slot_at(s):
        return lax.rem(slot // 4 + s // 4, 4) * 4 + lax.rem(slot + s, 4)

    def slot_peer(s):
        to = slot_at(s)
        return {"head": (to // 2) * 2 + core, "row": y_lo * 4 + lax.rem(to, 2) * 2 + x_lo}

    def part_peer(s):
        to = lax.rem(part + s, 8)
        return {"head": (me // 2) * 2 + lax.rem(to, 2), "row": (to // 4) * 4 + x_hi * 2 + lax.rem(to // 2, 2)}

    partner = {"head": me + 1 - 2 * core, "row": row}
    hs, rs, ps = w["hs"], w["rs"], w["ps"]

    def over(n, size, peer, src, dst):
        sems = hs if size == HEADS else rs
        return Trade(size, peer, src, dst, sems.at[2 * n], sems.at[2 * n + 1])

    def to_partner(n, src, dst):
        return pltpu.make_async_remote_copy(src_ref=src, dst_ref=dst, send_sem=ps.at[0, n], recv_sem=ps.at[1, n],
                                            device_id=partner, device_id_type=MESH)

    def head_at(s):
        return lax.rem(me + s, HEADS)

    greet([(HEADS, head_peer), (ROWS, row_peer), (HEADS, slot_peer), (8, part_peer)])
    wall, wide, stage1, recv1 = w["wall"], w["wide"], w["stage1"], w["recv1"]
    f0 = jnp.full((8, 128), fac[0], F32)
    f1 = f0 - f0.astype(BF16).astype(F32)
    f2 = f1 - f1.astype(BF16).astype(F32)
    tile = lax.broadcasted_iota(jnp.int32, (8, 128), 0)
    factor = jnp.where(tile == 0, f0, jnp.where(tile == 1, f1, jnp.where(tile == 2, f2, 0.0)))
    pairs = ((wk[...], wr[...]), (wq[...], wl[...]), (wf[...], factor.astype(BF16)))
    weights = jnp.concatenate([jnp.concatenate(pair, axis=0) for pair in pairs], axis=1)
    for p in range(HEADS):
        stage1[p, :, 512:896] = weights
    for z in range(2):
        wide[z, 0:256, :] = x[:, :, z * 128:z * 128 + 128].reshape(256, 128).astype(F32)
        wide[z, 256:512, :] = u[:, :, z * 128:z * 128 + 128].reshape(256, 128).astype(F32)
    to_pairs(wide, stage1, 16, 16)
    pl.semaphore_wait(pltpu.get_barrier_semaphore(), 2 * HEADS + ROWS + 8 - 4)
    inputs = over(0, HEADS, head_peer, lambda s: stage1.at[head_at(s)], recv1.at[me])
    inputs.start()
    recv1[me] = stage1[me]
    constants(w)
    node = row * 32 + lax.broadcasted_iota(jnp.int32, (32, 128), 0)
    column = lax.broadcasted_iota(jnp.int32, (32, 128), 1)
    for z in range(2):
        valid = (allowance[:, z * 128:z * 128 + 128] == 1) | (node == column + z * 128)
        w["mask"][z] = jnp.where(valid, 0.0, -1e30)
    bias = jnp.concatenate([w["mask"][z, pl.ds(2 * me + a, 1), :] for z in range(2) for a in range(2)], axis=1)
    bias = jnp.broadcast_to(bias, (8, 512))
    inputs.finish()
    for n in range(3):
        wall[:, 16 * n:16 * n + 16, :] = recv1[:, :, 512 + 128 * n:640 + 128 * n]
    both = recv1[:, :, 0:512].astype(F32)
    w["xp"][...] = both[:, 0:8].reshape(128, 512).astype(BF16)
    w["up"][...] = both[:, 8:16].reshape(128, 512).astype(BF16)

    stage2, recv2, kr = w["stage2"], w["recv2"], w["kr"]
    mapped = over(2, HEADS, slot_peer, lambda s: stage2.at[slot_at(s)], recv2.at[slot])
    for first in range(0, HEADS, 4):
        peers = [slot_at(first + a) for a in range(4)]
        of_x = dot(jnp.concatenate([wall[p, 0:32] for p in peers], axis=0), w["xp"][...]).astype(BF16)
        of_u = dot(jnp.concatenate([wall[p, 32:48] for p in peers], axis=0), w["up"][...])
        for a, p in enumerate(peers):
            stage2[p, 0:32] = of_x[a * 32:a * 32 + 32]
            stage2[p, 32:48] = jnp.concatenate([of_u[a * 16:a * 16 + 8], bias], axis=0).astype(BF16)
            if first + a:
                mapped.copy(first + a).start()
            else:
                recv2[slot] = stage2[slot]

    for n in range(2):
        w["turned"][n] = wall[:, 16 * n:16 * n + 16, :].reshape(256, 128).astype(F32).T.astype(BF16)
    near, wide2 = w["near"], w["wide2"]

    def four(g):
        return lax.rem(slot // 4 + 4 - g, 4) * 4

    def kr_copy(g, s):
        some = pl.ds(four(g), 4)
        to = lax.rem(part + s, 8)
        return pltpu.make_async_remote_copy(
            src_ref=recv2.at[some, pl.ds(0, 16), pl.ds(pl.multiple_of(lax.rem(to, 2) * 256, 128), 256)], dst_ref=kr.at[part, some],
            send_sem=w["ks"].at[0, g, s], recv_sem=w["ks"].at[1, g, s], device_id=part_peer(s), device_id_type=MESH)

    def near_copy(g):
        some = pl.ds(four(g), 4)
        return to_partner(g, recv2.at[some, pl.ds(16, 32)], near.at[some])

    def unpack_near(g):
        near_copy(g).wait_recv()
        from_pairs(near, 0, 32, wide2, 32 - core * 32, I, four(g), 4)

    @pl.loop(0, 4)
    def _(g):
        @pl.loop(0, 4)
        def _(a):
            @pl.when(g * 4 + a > 0)
            def _():
                mapped.copy(g * 4 + a).wait_recv()

        near_copy(g).start()

        @pl.loop(1, 8)
        def _(s):
            kr_copy(g, s).start()

        from_pairs(recv2, 16, 48, wide2, core * 32, I, four(g), 4)

        @pl.when(g > 0)
        def _():
            unpack_near(g - 1)

    unpack_near(3)
    own = pl.multiple_of(core * 32, 32)
    prepare(wide2, w)

    f = jnp.sum(wall[slot, 32:48].astype(F32)[8:16], axis=0, keepdims=True)

    def groups(chip):
        for hi in range(2):
            for y in range(2):
                yield 2 * ((chip // 2) * 4 + hi * 2 + lax.rem(chip, 2)) + y, y * 8 + hi

    @pl.loop(0, 4)
    def _(k):
        chip = lax.rem(block + 4 - k, 4)
        for c in range(2):
            @pl.when(2 * chip + c != part)
            def _():
                @pl.loop(0, 4)
                def _(g):
                    kr_copy(g, lax.rem(part + 8 - 2 * chip - c, 8)).wait_recv()

            @pl.when(2 * chip + c == part)
            def _():
                kr[part] = recv2[:, 0:16, pl.ds(pl.multiple_of(core * 256, 128), 256)]

        for n, first in groups(chip):
            for t in range(16):
                at = (first + (t // 4) * 2)
                tile = kr[2 * chip + (t // 2) % 2, at, :, (t % 2) * 128:(t % 2) * 128 + 128].astype(F32)
                rows = pl.ds(pl.multiple_of(n * 128 + t * 8, 8), 8)
                w["kf"][rows, :] = tile[0:8]
                w["rf"][rows, :] = tile[8:16]
            scores(n, w)

    forward(wide2, core, f, w["mx"], w)
    mine, other = pl.ds(own, 32), pl.ds(pl.multiple_of(32 - core * 32, 32), 32)
    mixed_out = to_partner(4, w["mx"].at[:, other], w["mixin"])
    mixed_out.start()
    ql2, qlin, kro, krin = w["ql2"], w["qlin"], w["kro"], w["krin"]
    stageq, recvq = w["stageq"], w["recvq"]

    def out_copy(y, to):
        s = lax.rem(to + 8 - part, 8)
        rows = pl.ds(y * 16, 16)
        return pltpu.make_async_remote_copy(
            src_ref=kro.at[to, rows], dst_ref=krin.at[part, rows], send_sem=w["os"].at[y, 0, s], recv_sem=w["os"].at[y, 1, s],
            device_id=part_peer(s), device_id_type=MESH)

    mixed = over(3, HEADS, slot_peer, lambda s: w["stagem"].at[slot_at(s)], w["recvm"].at[slot])

    def group_out(n):
        lanes = pl.ds(pl.multiple_of(n * 128, 128), 128)
        return to_partner(5 + n, ql2.at[:, other, lanes], qlin.at[:, :, lanes])

    def half_out(h, n):
        @pl.loop(0, 8)
        def _(g):
            group_out(8 * h + g).wait()

        lanes = pl.ds(pl.multiple_of(h * 1024, 1024), 1024)
        total = (ql2[:, mine, lanes] + qlin[:, :, lanes]).astype(BF16).reshape(64, 1024)
        plain = dot(total, w["pt"][...])
        for c in range(CH):
            wide[n, c * 32:c * 32 + 32, :] = plain[0:32, c * 128:c * 128 + 128]
            wide[n, 256 + c * 32:288 + c * 32, :] = plain[32:64, c * 128:c * 128 + 128]
        for i in range(32):
            stageq[n, i // 2, :, (i % 2) * 128:(i % 2) * 128 + 128] = wide[n, pl.ds(i, 16, stride=32), :].astype(BF16)
        halves[n].start()
        recvq[h, slot] = stageq[n, slot]

    far = 1 - y_lo
    halves = [over(4 + 3 * n, HEADS, slot_peer, lambda s, n=n: stageq.at[n, slot_at(s)], recvq.at[h, slot]) for n, h in enumerate((far, y_lo))]

    @pl.loop(0, 8)
    def _(k):
        first, last_two, odd = 1 - (k + 6) // 8, k // 6, lax.rem(k, 2)
        between = 1 - first - last_two
        cy = lax.rem(y_lo + first + between * (1 - odd), 2)
        cx = lax.rem(x_lo + first + between * odd, 2)
        yh = (first + last_two) * odd + between * (k // 2 - 1)
        chip = cy * 2 + cx

        @pl.loop(0, 2)
        def _(j):
            n = 2 * (cy * 4 + j * 2 + cx) + yh
            backward(n, chip, yh * 16 + j * 2, f, ql2.at[0], ql2.at[1], kro, w)
            group_out(n).start()

        for c in range(2):
            to = 2 * chip + c

            @pl.when(to != part)
            def _():
                out_copy(yh, to).start()

        @pl.when(k == 7)
        def _():
            krin[part] = kro[part]

        @pl.when(k == 5)
        def _():
            half_out(far, 0)

        @pl.when(k == 1)
        def _():
            mixed_out.wait()
            mixf = w["mixf"]
            for c in range(CH):
                mixf[core, c * 32:c * 32 + 32, :] = w["mx"][c, mine, :].astype(F32)
                mixf[1 - core, c * 32:c * 32 + 32, :] = w["mixin"][c].astype(F32)
            to_pairs(mixf, w["stagem"], 8, 16)
            mixed.start()
            w["recvm"][slot] = w["stagem"][slot]

    @pl.loop(1, 8)
    def _(s):
        for y in range(2):
            out_copy(y, lax.rem(part + s, 8)).wait_recv()

    stage3, recv3 = w["stage3"], w["recv3"]
    for j in range(2):
        total = krin[j] + krin[2 + j] + krin[4 + j] + krin[6 + j]
        total = total.astype(BF16).reshape(16, 2, 16, 128)
        for a in range(2):
            stage3[:, :, j * 256 + a * 128:j * 256 + a * 128 + 128] = total[:, a]
    backs = over(8, HEADS, slot_peer, lambda s: stage3.at[slot_at(s)], recv3.at[slot])
    backs.start()
    recv3[slot] = stage3[slot]
    half_out(y_lo, 1)
    mixed.finish()
    gws = w["gws"]
    gws[:, 32:40, :] = dot(w["recvm"][...].reshape(256, 512), w["up"][...], NT).reshape(16, 16, 128)[:, 0:8]

    spans = (pl.ds(0, 16), pl.ds(16, 24))
    sums = [over(5 + 4 * n, HEADS, head_peer, lambda s, c=c: gws.at[head_at(s), c], w["gwin"].at[me, c]) for n, c in enumerate(spans)]
    image = None
    for n in (0, 1):
        if n:
            halves[0].finish()
            halves[1].finish()
            every = jnp.concatenate([recvq[0].reshape(256, 256), recvq[1].reshape(256, 256)], axis=1)
        else:
            backs.finish()
            every = recv3[...].reshape(256, 512)
        gws[:, 16 * n:16 * n + 16, :] = dot(every, w["xp"][...], NT).reshape(16, 16, 128)
        sums[n].start()
        term = dot(w["turned"][n], every)
        image = term if image is None else image + term
    w["gwin"][me] = gws[me]
    image = image.reshape(16, 8, 512)
    w["stage4"][...] = jnp.concatenate([image[:, :, 0:256], image[:, :, 256:512]], axis=1).astype(BF16)
    images = over(6, HEADS, head_peer, lambda s: w["stage4"].at[head_at(s)], w["recv4"].at[me])
    images.start()
    w["recv4"][me] = w["stage4"][me]
    for trade in (inputs, mapped, mixed, *halves, backs):
        trade.drain()

    @pl.loop(0, 4)
    def _(g):
        near_copy(g).wait_send()

        @pl.loop(1, 8)
        def _(s):
            kr_copy(g, s).wait_send()

    @pl.loop(1, 8)
    def _(s):
        for y in range(2):
            out_copy(y, lax.rem(part + s, 8)).wait_send()

    for trade in sums:
        trade.finish()
    total = w["gwin"][0]
    for p in range(1, HEADS):
        total = total + w["gwin"][p]
    w["part"][...] = total
    last = over(1, ROWS, row_peer, lambda s: w["part"], w["gwrow"].at[row])
    last.start()
    w["gwrow"][row] = total
    images.finish()
    for i in range(32):
        two = w["recv4"][i // 2, :, (i % 2) * 128:(i % 2) * 128 + 128].astype(F32)
        for z in range(2):
            wide[z, pl.ds(i, 8, stride=32), :] = two[z * 8:z * 8 + 8]
    for z in range(2):
        grads[:, :, z * 128:z * 128 + 128] = wide[z, 0:256, :].astype(BF16).reshape(8, 32, 128)
    last.finish()
    total = w["gwrow"][0]
    for p in range(1, ROWS):
        total = total + w["gwrow"][p]
    gw[...] = total * (1.0 / 256.0)
    for trade in (*sums, images, last):
        trade.drain()


def results(grads, gw, out, gq, gk, gl, gr, go):
    out[...] = grads[...]
    for n, ref in enumerate((gk, gr, gq, gl, go)):
        ref[...] = gw[8 * n:8 * n + 8, :]


def layer_scratch():
    vmem, dma = pltpu.VMEM, pltpu.SemaphoreType.DMA
    return dict(
        core_scratch(),
        wide=vmem((2, 1024, 128), F32), wide2=vmem((2, 2048, 128), F32), wall=vmem((16, 48, 128), BF16),
        stage1=vmem((16, 16, 896), BF16), recv1=vmem((16, 16, 896), BF16), turned=vmem((2, 128, 256), BF16), xp=vmem((128, 512), BF16), up=vmem((128, 512), BF16),
        stage2=vmem((16, 48, 512), BF16), recv2=vmem((16, 48, 512), BF16), near=vmem((16, 32, 512), BF16), mask=vmem((2, 32, 128), F32),
        kr=vmem((8, 16, 16, 256), BF16),
        ql2=vmem((2, 64, 2048), F32), qlin=vmem((2, 32, 2048), F32), kro=vmem((8, 32, 16, 128), F32), krin=vmem((8, 32, 16, 128), F32),
        mx=vmem((8, 64, 128), BF16), mixin=vmem((8, 32, 128), BF16), mixf=vmem((2, 256, 128), F32),
        stagem=vmem((16, 16, 512), BF16), recvm=vmem((16, 16, 512), BF16),
        stage3=vmem((16, 16, 512), BF16), recv3=vmem((16, 16, 512), BF16), stageq=vmem((2, 16, 16, 256), BF16), recvq=vmem((2, 16, 16, 256), BF16), stage4=vmem((16, 16, 256), BF16), recv4=vmem((16, 16, 256), BF16),
        gws=vmem((16, 40, 128), F32), gwin=vmem((16, 40, 128), F32), part=vmem((40, 128), F32), gwrow=vmem((8, 40, 128), F32),
        os=dma((2, 2, 8)), hs=dma((20, 16)), rs=dma((4, 8)), ps=dma((2, 21)), ks=dma((2, 4, 8)),
    )


def local(x, allowance, asking, lookup, first_content, second_content, final, scaling, upstream):
    vm = pl.BlockSpec(memory_space=pltpu.VMEM)
    names = layer_scratch()
    grads, gw = pl.pallas_call(
        functools.partial(layer, list(names)),
        out_shape=[jax.ShapeDtypeStruct((8, 32, 256), BF16), jax.ShapeDtypeStruct((40, 128), F32)],
        in_specs=[vm] * 8 + [pl.BlockSpec(memory_space=pltpu.SMEM)], out_specs=[vm] * 2,
        scratch_shapes=list(names.values()),
        compiler_params=pltpu.CompilerParams(collective_id=0, has_side_effects=True, vmem_limit_bytes=56 * 2 ** 20),
        name="layer",
    )(x, upstream, asking.T, lookup.T, first_content.T, second_content.T, final, allowance, scaling)
    grads, gq, gk, gl, gr, go = pl.pallas_call(
        results, out_shape=[jax.ShapeDtypeStruct((8, 32, 256), BF16)] + [jax.ShapeDtypeStruct((8, 128), F32)] * 5,
        in_specs=[vm] * 2, out_specs=[vm] * 6, name="results",
    )(grads, gw)
    return grads, gq.T, gk.T, gl.T, gr.T, go


def solution(mesh):
    pairs, columns = P("head", "row", None), P(None, "head")
    placed = (pairs, P("row", None), columns, columns, columns, columns, P("head", None), P("head"), pairs)
    return jax.shard_map(
        local, mesh=mesh, in_specs=placed,
        out_specs=(pairs, columns, columns, columns, columns, P("head", None)), check_vma=False,
    )
```
